128 devices in a mesh: lat: 4 (over z_hi, core), lon: 32 (over x, y, z_lo).
Axes of the slice: x: 4, y: 4, z: 4 (z_hi: 2, z_lo: 2; z = z_hi * 2 + z_lo), core: 2. Of those that a mesh axis runs over, the one named last changes fastest.
Arguments:
- tokens: bfloat16 [2, 48, 768, 512], P(None, 'lat', 'lon'), may hold values from -15 to 15
- land_mask: int32 [48, 768], P('lat', 'lon'), may hold values 0 or 1
- land_embed: float32 [512], replicated, may hold values from -3 to 3
- shifts: int32 [2, 2], replicated, may hold values from 0 to 5
- gain_attn: float32 [512], replicated, may hold values from 0.1 to 1.9
- w_qkv_fine: bfloat16 [512, 1536], replicated, may hold values from -11 to 11
- w_out_fine: bfloat16 [512, 512], replicated, may hold values from -0.75 to 0.75
- gain_mlp: float32 [512], replicated, may hold values from 0.1 to 1.9
- w_up_fine: bfloat16 [512, 2048], replicated, may hold values from -0.25 to 0.25
- w_down_fine: bfloat16 [2048, 512], replicated, may hold values from -0.125 to 0.125
- gain_merge: float32 [2048], replicated, may hold values from 0.1 to 1.9
- w_merge: bfloat16 [2048, 1024], replicated, may hold values from -0.125 to 0.125
- gain_coarse: float32 [1024], replicated, may hold values from 0.1 to 1.9
- w_qkv_coarse: bfloat16 [1024, 3072], replicated, may hold values from -11 to 11
- w_out_coarse: bfloat16 [1024, 1024], replicated, may hold values from -0.75 to 0.75
- w_expand: bfloat16 [1024, 2048], replicated, may hold values from -0.1875 to 0.1875
Outputs:
- blended: bfloat16 [2, 48, 768, 512], P(None, 'lat', 'lon')
The draws below stay inside these ranges and needn't reach their ends.
All inputs are finite; a program needn't handle non-finite values. No bound on the sum of `land_mask` on one device may be relied on, other than what follows from the above.
Results may differ from the reference program's by a relative error of at most 0.02.
Values may be sent and summed in bfloat16 or wider, within the bound.
A program may use at most 128 MiB of HBM per device.

```python
import jax
import jax.numpy as jnp
from jax import lax

D1 = 512
HEAD = 64
LEV = 2
WLAT = 6
WLON = 12
D2 = 1024
FF1 = 2048
NLAT = 48
NLON = 768


def projection_matrix(key, width, strength):
    base_key, pick_key, factor_key = jax.random.split(key, 3)
    head_count = width // HEAD
    weights = jnp.clip(jax.random.normal(base_key, (width, 3 * width), jnp.float32), -4.0, 4.0) * width ** (-0.5)
    chosen = jax.random.bernoulli(pick_key, 0.5, (head_count,)).astype(jnp.float32)
    factors = jnp.exp(jax.random.uniform(factor_key, (head_count,), jnp.float32, 0.0, 1.1)) * strength * chosen
    column_factor = jnp.repeat(factors, HEAD)
    keep_share = 1.0 - jnp.repeat(chosen, HEAD) * min(strength, 1.0)
    key_part = weights[:, width:2 * width] * keep_share + weights[:, :width] * column_factor
    joined = jnp.concatenate([weights[:, :width], key_part, weights[:, 2 * width:]], axis=1)
    return jnp.clip(joined, -11.0, 11.0).astype(jnp.bfloat16)


def draw_tokens(key, part):
    key = jax.random.fold_in(key, 3)
    noise_key, column_key = jax.random.split(key, 2)
    shape = (LEV, NLAT, NLON, D1)
    column_scale = jnp.exp(jax.random.uniform(column_key, (D1,), jnp.float32, 0.0, 2.3)) * 0.25
    noise = jax.random.normal(noise_key, shape, jnp.float32)
    return jnp.clip(noise * column_scale, -15.0, 15.0).astype(jnp.bfloat16)


def draw_w_qkv_fine(key, part):
    key = jax.random.fold_in(key, 5)
    strength = 0.0
    return projection_matrix(key, D1, strength)


def draw_w_qkv_coarse(key, part):
    key = jax.random.fold_in(key, 7)
    strength = 0.0
    return projection_matrix(key, D2, strength)


def with_ends(values, rng, smallest, high):
    longest = values.shape.index(max(values.shape))
    spots = []
    for shift in (0, 1):
        where = [jax.random.randint(jax.random.fold_in(rng, axis), (), 0, length) for axis, length in enumerate(values.shape)]
        where[longest] = (where[longest] + shift) % values.shape[longest]
        spots.append(tuple(where))
    return values.at[spots[0]].set(smallest).at[spots[1]].set(high)


def normal_values(own_key, shape, scale, limit, held_as=jnp.bfloat16):
    return jnp.clip(scale * jax.random.normal(own_key, shape, jnp.float32), -limit, limit).astype(held_as)


def setup_inputs(seed: int = 0) -> dict:
    keys = jax.random.split(jax.random.key(seed), 17)
    tokens = draw_tokens(jax.random.fold_in(keys[16], 71), 0)
    land_mask = with_ends((jax.random.randint(keys[1], (NLAT, NLON), 0, 10) < 3).astype(jnp.int32), jax.random.fold_in(keys[1], 1), 0, 1)
    land_embed = normal_values(keys[2], (D1,), 0.5, 3.0, jnp.float32)
    shifts = with_ends(jax.random.randint(keys[3], (2, 2), 0, WLAT), jax.random.fold_in(keys[3], 1), 0, WLAT - 1).astype(jnp.int32)
    gain_attn = jnp.clip(1.0 + 0.18 * jax.random.normal(keys[4], (D1,), jnp.float32), 0.1, 1.9)
    w_qkv_fine = draw_w_qkv_fine(jax.random.fold_in(keys[16], 71), 0)
    w_out_fine = normal_values(keys[6], (D1, D1), HEAD ** -0.5, 0.75)
    gain_mlp = jnp.clip(1.0 + 0.18 * jax.random.normal(keys[7], (D1,), jnp.float32), 0.1, 1.9)
    w_up_fine = normal_values(keys[8], (D1, FF1), D1 ** -0.5, 0.25)
    w_down_fine = normal_values(keys[9], (FF1, D1), FF1 ** -0.5, 0.125)
    gain_merge = jnp.clip(1.0 + 0.18 * jax.random.normal(keys[10], (4 * D1,), jnp.float32), 0.1, 1.9)
    w_merge = normal_values(keys[11], (4 * D1, D2), (4 * D1) ** -0.5, 0.125)
    gain_coarse = jnp.clip(1.0 + 0.18 * jax.random.normal(keys[12], (D2,), jnp.float32), 0.1, 1.9)
    w_qkv_coarse = draw_w_qkv_coarse(jax.random.fold_in(keys[16], 71), 0)
    w_out_coarse = normal_values(keys[14], (D2, D2), HEAD ** -0.5, 0.75)
    w_expand = normal_values(keys[15], (D2, 4 * D1), D2 ** -0.5, 0.1875)
    return {"tokens": tokens, "land_mask": land_mask, "land_embed": land_embed, "shifts": shifts, "gain_attn": gain_attn, "w_qkv_fine": w_qkv_fine, "w_out_fine": w_out_fine, "gain_mlp": gain_mlp, "w_up_fine": w_up_fine, "w_down_fine": w_down_fine, "gain_merge": gain_merge, "w_merge": w_merge, "gain_coarse": gain_coarse, "w_qkv_coarse": w_qkv_coarse, "w_out_coarse": w_out_coarse, "w_expand": w_expand}


EPSILON = 1e-05
NEGATIVE = -1e+30

def layer_norm(field_in, gain_vector):
    numbers = field_in.astype(jnp.float32)
    center = numbers - lax.optimization_barrier(jnp.mean(numbers, axis=-1, keepdims=True))
    variance = lax.optimization_barrier(jnp.mean(center * center, axis=-1, keepdims=True))
    return (center * lax.rsqrt(variance + EPSILON) * gain_vector).astype(jnp.bfloat16)

def window_attend(queries, keys_in, values, valid_keys, head_count):
    window_count, window_size, channels = queries.shape
    head_width = channels // head_count
    query_heads = queries.reshape(window_count, window_size, head_count, head_width).astype(jnp.float32)
    key_heads = keys_in.reshape(window_count, window_size, head_count, head_width).astype(jnp.float32)
    value_heads = values.reshape(window_count, window_size, head_count, head_width).astype(jnp.float32)
    scores = jnp.einsum('wqhd,wkhd->whqk', query_heads, key_heads) * head_width ** (-0.5)
    scores = jnp.where(valid_keys[:, None, None, :], scores, NEGATIVE)
    row_max = lax.optimization_barrier(jnp.max(scores, axis=-1, keepdims=True))
    weights_raw = jnp.exp(scores - row_max)
    weights = (weights_raw / lax.optimization_barrier(jnp.sum(weights_raw, axis=-1, keepdims=True))).astype(jnp.bfloat16)
    mixed_out = jnp.einsum('whqk,wkhd->wqhd', weights.astype(jnp.float32), value_heads)
    return mixed_out.reshape(window_count, window_size, channels).astype(jnp.bfloat16)

def shifted_attention(field_in, offsets, gain_vector, w_packed, w_project):
    levels, lat_total, lon_total, channels = field_in.shape
    head_count = channels // HEAD
    lat_shift = offsets[0].astype(jnp.int32)
    lon_shift = offsets[1].astype(jnp.int32)
    normed = layer_norm(field_in, gain_vector)
    padded = jnp.pad(normed, ((0, 0), (WLAT, WLAT), (0, 0), (0, 0)))
    framed = lax.dynamic_slice_in_dim(padded, (WLAT - lat_shift).astype(jnp.int32), lat_total + WLAT, 1)
    framed = jnp.roll(framed, lon_shift, axis=2)
    lat_rows = jnp.arange(lat_total + WLAT) - lat_shift
    valid_rows = (lat_rows >= 0) & (lat_rows < lat_total)
    across_lat = (lat_total + WLAT) // WLAT
    window_size = levels * WLAT * WLON
    valid_keys = jnp.broadcast_to(valid_rows.reshape(across_lat, 1, WLAT, 1), (across_lat, levels, WLAT, WLON)).reshape(across_lat, window_size)

    def one_column(column_index):
        start = (column_index * WLON).astype(jnp.int32)
        column_block = lax.dynamic_slice_in_dim(framed, start, WLON, 2)
        column_block = column_block.reshape(levels, across_lat, WLAT, WLON, channels).transpose(1, 0, 2, 3, 4)
        column_block = column_block.reshape(across_lat, window_size, channels)
        packed = jnp.dot(column_block, w_packed, preferred_element_type=jnp.float32).astype(jnp.bfloat16)
        return window_attend(packed[..., :channels], packed[..., channels:2 * channels], packed[..., 2 * channels:], valid_keys, head_count)
    along_lon = lon_total // WLON
    mixed_out = lax.map(one_column, jnp.arange(along_lon).astype(jnp.int32))
    mixed_out = mixed_out.reshape(along_lon, across_lat, levels, WLAT, WLON, channels).transpose(2, 1, 3, 0, 4, 5)
    mixed_out = mixed_out.reshape(levels, lat_total + WLAT, lon_total, channels)
    mixed_out = jnp.roll(mixed_out, -lon_shift, axis=2)
    mixed_out = lax.dynamic_slice_in_dim(mixed_out, lat_shift, lat_total, 1)
    projected = jnp.dot(mixed_out, w_project, preferred_element_type=jnp.float32)
    return (field_in.astype(jnp.float32) + projected).astype(jnp.bfloat16)

def reference(tokens, land_mask, land_embed, shifts, gain_attn, w_qkv_fine, w_out_fine, gain_mlp, w_up_fine, w_down_fine, gain_merge, w_merge, gain_coarse, w_qkv_coarse, w_out_coarse, w_expand):
    inputs = (tokens.astype(jnp.float32) + land_mask.astype(jnp.float32)[None, :, :, None] * land_embed).astype(jnp.bfloat16)
    attended = shifted_attention(inputs, shifts[0], gain_attn, w_qkv_fine, w_out_fine)
    hidden = jax.nn.gelu(jnp.dot(layer_norm(attended, gain_mlp), w_up_fine, preferred_element_type=jnp.float32)).astype(jnp.bfloat16)
    skipped = (attended.astype(jnp.float32) + jnp.dot(hidden, w_down_fine, preferred_element_type=jnp.float32)).astype(jnp.bfloat16)
    levels, lat_total, lon_total, channels = skipped.shape
    merged = skipped.reshape(levels, lat_total // 2, 2, lon_total // 2, 2, channels).transpose(0, 1, 3, 4, 2, 5)
    merged = merged.reshape(levels, lat_total // 2, lon_total // 2, 4 * channels)
    coarse = jnp.dot(layer_norm(merged, gain_merge), w_merge, preferred_element_type=jnp.float32).astype(jnp.bfloat16)
    coarse_out = shifted_attention(coarse, shifts[1], gain_coarse, w_qkv_coarse, w_out_coarse)
    spread = jnp.dot(coarse_out, w_expand, preferred_element_type=jnp.float32)
    spread = spread.reshape(levels, lat_total // 2, lon_total // 2, 2, 2, channels).transpose(0, 1, 4, 2, 3, 5)
    spread = spread.reshape(levels, lat_total, lon_total, channels)
    return (skipped.astype(jnp.float32) + spread).astype(jnp.bfloat16)
```

```python
import jax
import jax.numpy as jnp
from jax import lax
from jax.experimental import pallas as pl
from jax.experimental.pallas import tpu as pltpu
from jax.sharding import PartitionSpec as P

HEAD = 64
WLAT = 6
WLON = 12
WIN = 2 * WLAT * WLON
REACH = 5
MAIN = 128
REST = WIN - MAIN

D1 = 512
D2 = 1024
FF1 = 2048
ROWS, COLS = 12, 24
ROWS2, COLS2 = 6, 12
TOK = 2 * ROWS * COLS
TOK2 = 2 * ROWS2 * COLS2
LINE = 2 * COLS
SPAN = (WLAT + REACH) * LINE

EPSILON = 1e-05
NEGATIVE = -1e30
SCALE = HEAD ** (-0.5) * 1.4426950408889634
BF = jnp.bfloat16
F32 = jnp.float32
I32 = jnp.int32
MESH = pl.DeviceIdType.MESH


def div(x, d):
    return (x * ((1 << 20) // d + 1)) >> 20


def col(n):
    return lax.broadcasted_iota(I32, (n, 1), 0)


def row(n):
    return lax.broadcasted_iota(I32, (1, n), 1)


def onehot(target, lanes):
    return jnp.where(lanes == target, 1.0, 0.0).astype(BF)


def mm(a, b):
    return lax.dot_general(a, b, (((1,), (0,)), ((), ())), preferred_element_type=F32)


def mm_nt(a, b):
    return lax.dot_general(a, b, (((1,), (1,)), ((), ())), preferred_element_type=F32)


def mm_tn(a, b):
    return lax.dot_general(a, b, (((0,), (0,)), ((), ())), preferred_element_type=F32)


def norm(x, gain):
    mean = jnp.mean(x, axis=-1, keepdims=True)
    center = x - mean
    var = jnp.mean(center * center, axis=-1, keepdims=True)
    return (center * lax.rsqrt(var + EPSILON) * gain).astype(BF)


def slot_parts(s):
    r = div(s, 24)
    rest = s - r * 24
    lev = div(rest, 12)
    return r, lev, rest - lev * 12


def soften(s, bias):
    s = s + bias
    top = jnp.max(s, axis=0, keepdims=True)
    p = jnp.exp2(s * SCALE - top * SCALE)
    total = jnp.sum(p, axis=0, keepdims=True)
    return p.astype(BF), 1.0 / total


def window_attend(q_of, k_of, v_of, width, bias, put):
    heads = width // HEAD
    lane = row(2 * HEAD)
    for pair in range(heads // 2):
        part = pl.ds(pair * 2 * HEAD, 2 * HEAD)
        q = q_of(pl.ds(0, MAIN), part)
        zero = jnp.zeros_like(q)
        both = jnp.concatenate(
            [jnp.where(lane < HEAD, q, zero), jnp.where(lane < HEAD, zero, q)], axis=0
        )
        p, inv = soften(mm_nt(k_of(part), both), bias)
        o = mm_tn(v_of(part), p) * inv
        put(pair * 2 * HEAD, HEAD, 0, MAIN, o[:HEAD, :MAIN])
        put(pair * 2 * HEAD + HEAD, HEAD, 0, MAIN, o[HEAD:, MAIN:])
    every = pl.ds(0, width)
    spread = REST * heads
    q = q_of(pl.ds(MAIN, REST), every)
    tiled = jnp.concatenate([q] * heads, axis=0)
    own = (col(spread) >> 4) == (row(width) >> 6)
    tiled = jnp.where(own, tiled, jnp.zeros_like(tiled))
    p, inv = soften(mm_nt(k_of(every), tiled), bias)
    o = mm_tn(v_of(every), p) * inv
    o = jnp.where((col(width) >> 6) == (row(spread) >> 4), o, 0.0)
    put(0, width, MAIN, spread, o)


def kernel(
    tokens, mask, embed, shifts, gain_attn, gain_mlp, gain_merge, gain_coarse,
    w_qkv_h, w_out_h, w_up_h, w_down_h, w_merge_h, w_qkv2_h, w_out2_h, w_expand_h,
    out,
    w_qkv, w_out, w_up, w_down, w_merge, w_qkv2, w_out2, w_expand,
    inputs, ext, side_out, side, sel_own, sel_side, sel_back, qkv, mixed, back_out, back_in,
    resid, skipped, acc,
    norm2, send2, ext2, sel2, qkv2, mixed2, back2_out, back2_in,
    w_sem, send_sem, recv_sem,
):
    lat = lax.axis_index("lat")
    lon = lax.axis_index("lon")
    lat_n = lax.axis_size("lat")
    lon_n = lax.axis_size("lon")
    right = lax.rem(lon + 1, lon_n)
    left = lax.rem(lon + lon_n - 1, lon_n)
    has_up = lat > 0
    has_down = lat < lat_n - 1

    loads = []
    for i, (src, dst) in enumerate(
        [
            (w_qkv_h, w_qkv), (w_out_h, w_out), (w_up_h, w_up), (w_down_h, w_down),
            (w_merge_h, w_merge), (w_qkv2_h, w_qkv2), (w_out2_h, w_out2), (w_expand_h, w_expand),
        ]
    ):
        load = pltpu.make_async_copy(src, dst, w_sem.at[i])
        load.start()
        loads.append(load)

    barrier = pltpu.get_barrier_semaphore()

    def greet(a, b):
        pl.semaphore_signal(barrier, inc=1, device_id=(a, b), device_id_type=MESH)

    greet(lat, left)
    greet(lat, right)

    @pl.when(has_up)
    def _():
        for b in (left, lon, right):
            greet(lat - 1, b)

    @pl.when(has_down)
    def _():
        for b in (left, lon, right):
            greet(lat + 1, b)

    def remote(i, src, dst, a, b):
        return pltpu.make_async_remote_copy(
            src_ref=src, dst_ref=dst, send_sem=send_sem.at[i], recv_sem=recv_sem.at[i],
            device_id=(a, b), device_id_type=MESH,
        )

    eye = col(COLS) == row(COLS)
    add = embed[...]
    gain = gain_attn[...]
    for r in range(ROWS):
        land = jnp.sum(jnp.where(eye, mask[r : r + 1, :].astype(F32), 0.0), axis=1, keepdims=True)
        x = jnp.concatenate(
            [tokens[0, r].astype(F32) + land * add, tokens[1, r].astype(F32) + land * add], axis=0
        ).astype(BF)
        inputs[r] = x
        ext[REACH + r] = norm(x.astype(F32), gain)

    s = col(256)
    part = jnp.where(s < 128, 0, jnp.where(s < 192, 1, 2))
    within = s - jnp.where(part == 0, 0, jnp.where(part == 1, 128, 192))
    r = div(within, 10)
    rest = within - r * 10
    lev = div(rest, 5)
    c = rest - lev * 5
    r = r + jnp.where(part == 1, ROWS - REACH, 0)
    target = jnp.where(r < ROWS, r * LINE + lev * COLS + c + (COLS - REACH), -1)
    own = ext[REACH : REACH + ROWS].reshape(TOK, D1)
    side_out[...] = mm(onehot(target, row(TOK)), own).astype(BF)

    ext[2 * REACH + ROWS] = jnp.zeros((LINE, D1), BF)

    @pl.when(jnp.logical_not(has_up))
    def _():
        ext[0:REACH] = jnp.zeros((REACH, LINE, D1), BF)
        side[128:192] = jnp.zeros((64, D1), BF)

    @pl.when(jnp.logical_not(has_down))
    def _():
        ext[REACH + ROWS : 2 * REACH + ROWS] = jnp.zeros((REACH, LINE, D1), BF)
        side[192:256] = jnp.zeros((64, D1), BF)

    pl.semaphore_wait(
        barrier, 2 + jnp.where(has_up, 3, 0) + jnp.where(has_down, 3, 0)
    )

    go_right = remote(0, side_out.at[0:128], side.at[0:128], lat, right)
    go_down = remote(1, ext.at[ROWS : ROWS + REACH], ext.at[0:REACH], lat + 1, lon)
    go_up = remote(2, ext.at[REACH : 2 * REACH], ext.at[REACH + ROWS : 2 * REACH + ROWS], lat - 1, lon)
    go_down_right = remote(3, side_out.at[128:192], side.at[128:192], lat + 1, right)
    go_up_right = remote(4, side_out.at[192:256], side.at[192:256], lat - 1, right)

    def exchange(r_, d_, u_, dr_, ur_):
        r_.start()

        @pl.when(has_down)
        def _():
            d_.start()
            dr_.start()

        @pl.when(has_up)
        def _():
            u_.start()
            ur_.start()

    def arrived(r_, d_, u_, dr_, ur_):
        r_.wait_recv()

        @pl.when(has_up)
        def _():
            d_.wait_recv()
            dr_.wait_recv()

        @pl.when(has_down)
        def _():
            u_.wait_recv()
            ur_.wait_recv()

    def sent(r_, d_, u_, dr_, ur_):
        r_.wait_send()

        @pl.when(has_down)
        def _():
            d_.wait_send()
            dr_.wait_send()

        @pl.when(has_up)
        def _():
            u_.wait_send()
            ur_.wait_send()

    moves = (go_right, go_down, go_up, go_down_right, go_up_right)
    exchange(*moves)

    a = shifts[0, 0]
    b = shifts[0, 1]

    sr, sl, sc = slot_parts(col(WIN))
    for jc in range(2):
        c = sc + (WLON * jc) - b
        target = jnp.where(c >= 0, (sr + REACH - a) * LINE + sl * COLS + c, -1)
        sel_own[jc] = onehot(target, row(SPAN))
    c = sc - b
    for jr in range(3):
        r = sr + (WLAT * jr) - a
        place = jnp.where(
            r < 0, 128 + (r + REACH) * 10, jnp.where(r < ROWS, r * 10, 192 + (r - ROWS) * 10)
        )
        target = jnp.where(c < 0, place + sl * 5 + c + REACH, -1)
        sel_side[jr] = onehot(target, row(256))

    q = col(TOK)
    k = div(q, TOK2)
    cr, clev, cc = slot_parts(q - k * TOK2)
    fr = cr * 2 + (k & 1)
    fc = cc * 2 + (k >> 1)
    resid[...] = mm(
        onehot(fr * LINE + clev * COLS + fc, row(TOK)), inputs[...].reshape(TOK, D1)
    )
    up = fr + a
    jr = div(up, WLAT)
    over = fc + b
    jc = div(over, WLON)
    slot = ((up - jr * WLAT) * 2 + clev) * WLON + (over - jc * WLON)
    lanes = row(256)
    lanes = jnp.where(lanes < MAIN, lanes, MAIN + (lanes & 15))
    for w in range(6):
        target = jnp.where((jr == w % 3) & (jc == w // 3), slot, -1)
        sel_back[:, w * 256 : (w + 1) * 256] = onehot(target, lanes)
    target = jnp.where(jc == 2, (fr * 2 + clev) * 5 + fc - (COLS - REACH), -1)
    sel_back[:, 6 * 256 : 6 * 256 + 128] = onehot(target, row(128))

    loads[0].wait()

    def key_bias(jr, rows, a, lat_rows):
        r = sr + jr * WLAT - a + lat * rows
        return jnp.where((r >= 0) & (r < lat_rows), 0.0, NEGATIVE).astype(F32)

    def project(n, xs):
        x = jnp.concatenate(xs, axis=0) if len(xs) > 1 else xs[0]
        qkv[0 : n * WIN] = mm(x, w_qkv[...]).astype(BF)

    def gather(jr, jc):
        x = mm(sel_own[jc], ext[WLAT * jr : WLAT * jr + WLAT + REACH].reshape(SPAN, D1))
        if jc == 0:
            x = x + mm(sel_side[jr], side[...])
        return x.astype(BF)

    def attend(at, w, jr):
        base = pl.multiple_of(at * WIN, 16)
        lane0 = pl.multiple_of(w * 256, 256)

        def shifted(d, start):
            return pl.ds(start + d.start, d.size)

        def put(r0, rn, l0, ln, value):
            mixed[r0 : r0 + rn, pl.ds(lane0 + l0, ln)] = value.astype(BF)

        window_attend(
            lambda rows, part: qkv[pl.ds(base + rows.start, rows.size), part],
            lambda part: qkv[pl.ds(base, WIN), shifted(part, D1)],
            lambda part: qkv[pl.ds(base, WIN), shifted(part, 2 * D1)],
            D1,
            key_bias(jr, ROWS, a, ROWS * lat_n),
            put,
        )

    project(1, [gather(1, 1)])
    attend(0, 4, 1)

    arrived(*moves)
    project(3, [gather(jr, 0) for jr in range(3)])

    @pl.loop(0, 3)
    def _(i):
        attend(i, i, i)

    s = col(128)
    r = div(s, 10)
    rest = s - r * 10
    lev = div(rest, 5)
    c = rest - lev * 5 + b - REACH
    up = r + a
    jr = div(up, WLAT)
    slot = ((up - jr * WLAT) * 2 + lev) * WLON + c
    back = jnp.zeros((128, D1), F32)
    for w in range(3):
        target = jnp.where((jr == w) & (c >= 0) & (r < ROWS), slot, -1)
        back += mm_nt(onehot(target, lanes), mixed[:, w * 256 : (w + 1) * 256])
    back_out[...] = back.astype(BF)
    go_back = remote(5, back_out, back_in, lat, left)
    go_back.start()

    project(2, [gather(0, 1), gather(2, 1)])

    @pl.loop(0, 2)
    def _(i):
        attend(i, 3 + 2 * i, 2 * i)

    own = mm_nt(sel_back[:, 0 : 6 * 256], mixed[...])
    loads[1].wait()
    go_back.wait_recv()
    own = (own + mm(sel_back[:, 6 * 256 :], back_in[...])).astype(BF)
    attended = (resid[...] + mm(own, w_out[...])).astype(BF)
    resid[...] = attended.astype(F32)
    x = norm(attended.astype(F32), gain_mlp[...])

    loads[2].wait()
    loads[3].wait()
    chunk = 512
    acc[...] = resid[...]
    for i in range(FF1 // chunk):
        h = mm(x, w_up[:, i * chunk : (i + 1) * chunk])
        h = jax.nn.gelu(h).astype(BF)
        acc[...] += mm(h, w_down[i * chunk : (i + 1) * chunk, :])
    skipped[...] = acc[...].astype(BF)

    loads[4].wait()
    merged = jnp.concatenate(
        [skipped[i * TOK2 : (i + 1) * TOK2, :].astype(F32) for i in range(4)], axis=1
    )
    coarse = mm(norm(merged, gain_merge[...]), w_merge[...]).astype(BF)
    acc2 = coarse.astype(F32)
    normed = norm(acc2, gain_coarse[...])
    norm2[...] = normed

    a2 = shifts[1, 0]
    b2 = shifts[1, 1]

    s = col(448)
    is_row = s < 256
    downward = (s < 128) | ((s >= 320) & (s < 384))
    u = jnp.where(s < 128, s, s - 128)
    r_row = div(u, 24)
    lev_row = div(u - r_row * 24, 12)
    c_row = u - r_row * 24 - lev_row * 12
    v = jnp.where(s < 320, s - 256, jnp.where(s < 384, s - 320, s - 384))
    v = jnp.maximum(v, 0)
    r_col = div(v, 10)
    lev_col = div(v - r_col * 10, 5)
    c_col = v - r_col * 10 - lev_col * 5 + COLS2 - REACH
    r = jnp.where(is_row, r_row, r_col) + jnp.where(downward, ROWS2 - REACH, 0)
    lev = jnp.where(is_row, lev_row, lev_col)
    c = jnp.where(is_row, c_row, c_col)
    target = jnp.where(r < ROWS2, (r * 2 + lev) * COLS2 + c, -1)
    send2[...] = mm(onehot(target, row(TOK2)), normed).astype(BF)

    @pl.when(jnp.logical_not(has_up))
    def _():
        ext2[0:128] = jnp.zeros((128, D2), BF)
        ext2[320:384] = jnp.zeros((64, D2), BF)

    @pl.when(jnp.logical_not(has_down))
    def _():
        ext2[128:256] = jnp.zeros((128, D2), BF)
        ext2[384:448] = jnp.zeros((64, D2), BF)

    moves2 = (
        remote(6, send2.at[256:320], ext2.at[256:320], lat, right),
        remote(7, send2.at[0:128], ext2.at[0:128], lat + 1, lon),
        remote(8, send2.at[128:256], ext2.at[128:256], lat - 1, lon),
        remote(9, send2.at[320:384], ext2.at[320:384], lat + 1, right),
        remote(10, send2.at[384:448], ext2.at[384:448], lat - 1, right),
    )
    exchange(*moves2)

    c = sc - b2
    lane = row(TOK2)
    from_own = []
    for jr in range(2):
        r = sr + WLAT * jr - a2
        inside = (r >= 0) & (r < ROWS2)
        target = jnp.where(inside & (c >= 0), (r * 2 + sl) * COLS2 + c, -1)
        from_own.append(onehot(target, lane))
        base_row = jnp.where(
            r < 0, (r + REACH) * 24, jnp.where(r < ROWS2, -1, 128 + (r - ROWS2) * 24)
        ) + sl * 12 + c
        base_col = jnp.where(
            r < 0, 320 + (r + REACH) * 10, jnp.where(r < ROWS2, 256 + r * 10, 384 + (r - ROWS2) * 10)
        ) + sl * 5 + c + REACH
        target = jnp.where(c < 0, base_col, jnp.where(inside, -1, base_row))
        sel2[jr * WIN : (jr + 1) * WIN, :] = onehot(target, row(448))
    x2 = mm(jnp.concatenate(from_own, axis=0), normed)
    loads[5].wait()
    arrived(*moves2)
    x2 = (x2 + mm(sel2[...], ext2[...])).astype(BF)
    for i in range(3):
        qkv2[:, i * D2 : (i + 1) * D2] = mm(x2, w_qkv2[:, i * D2 : (i + 1) * D2]).astype(BF)

    held = MAIN + REST * (D2 // HEAD)

    @pl.loop(0, 2)
    def _(i):
        base = pl.multiple_of(i * WIN, 16)
        lane0 = pl.multiple_of(i * held, 128)

        def put(r0, rn, l0, ln, value):
            mixed2[r0 : r0 + rn, pl.ds(lane0 + l0, ln)] = value.astype(BF)

        window_attend(
            lambda rows, part: qkv2[pl.ds(base + rows.start, rows.size), part],
            lambda part: qkv2[pl.ds(base, WIN), pl.ds(D2 + part.start, part.size)],
            lambda part: qkv2[pl.ds(base, WIN), pl.ds(2 * D2 + part.start, part.size)],
            D2,
            key_bias(i, ROWS2, a2, ROWS2 * lat_n),
            put,
        )

    lanes = row(held)
    lanes = jnp.where(lanes < MAIN, lanes, MAIN + (lanes & 15))
    s = col(64)
    r = div(s, 10)
    rest = s - r * 10
    lev = div(rest, 5)
    c = rest - lev * 5 + b2 - REACH
    up = r + a2
    jr = div(up, WLAT)
    slot = ((up - jr * WLAT) * 2 + lev) * WLON + c
    pick = [
        onehot(jnp.where((jr == w) & (c >= 0) & (r < ROWS2), slot, -1), lanes) for w in range(2)
    ]
    back2_out[...] = mm_nt(jnp.concatenate(pick, axis=1), mixed2[...]).astype(BF)
    go_back2 = remote(11, back2_out, back2_in, lat, left)
    go_back2.start()

    up = sr + a2
    jr = div(up, WLAT)
    over = sc + b2
    slot = ((up - jr * WLAT) * 2 + sl) * WLON + over
    inside = over < COLS2
    pick = [onehot(jnp.where((jr == w) & inside, slot, -1), lanes) for w in range(2)]
    own2 = mm_nt(jnp.concatenate(pick, axis=1), mixed2[...])
    target = jnp.where(inside, -1, (sr * 2 + sl) * 5 + sc - (COLS2 - REACH))
    pick = onehot(target, row(64))
    loads[6].wait()
    loads[7].wait()
    go_back2.wait_recv()
    own2 = (own2 + mm(pick, back2_in[...])).astype(BF)
    coarse_out = (acc2 + mm(own2, w_out2[...])).astype(BF)
    for i in range(4):
        part = slice(i * TOK2, (i + 1) * TOK2)
        spread = mm(coarse_out, w_expand[:, i * D1 : (i + 1) * D1])
        skipped[part, :] = (skipped[part, :].astype(F32) + spread).astype(BF)

    t = col(TOK)
    lev = div(t, ROWS * COLS)
    rest = t - lev * (ROWS * COLS)
    r = div(rest, COLS)
    c = rest - r * COLS
    target = ((c & 1) * 2 + (r & 1)) * TOK2 + ((r >> 1) * 2 + lev) * COLS2 + (c >> 1)
    final = mm(onehot(target, row(TOK)), skipped[...])
    out[...] = final.reshape(2, ROWS, COLS, D1).astype(BF)

    sent(*moves)
    sent(*moves2)
    go_back.wait_send()
    go_back2.wait_send()


def local(
    tokens, land_mask, land_embed, shifts, gain_attn, w_qkv_fine, w_out_fine, gain_mlp, w_up_fine,
    w_down_fine, gain_merge, w_merge, gain_coarse, w_qkv_coarse, w_out_coarse, w_expand,
):
    vmem = pl.BlockSpec(memory_space=pltpu.VMEM)
    hbm = pl.BlockSpec(memory_space=pl.ANY)
    smem = pl.BlockSpec(memory_space=pltpu.SMEM)
    weights = [
        w_qkv_fine, w_out_fine, w_up_fine, w_down_fine, w_merge, w_qkv_coarse, w_out_coarse, w_expand,
    ]
    V = pltpu.VMEM
    held = MAIN + REST * (D2 // HEAD)
    return pl.pallas_call(
        kernel,
        out_shape=jax.ShapeDtypeStruct(tokens.shape, BF),
        in_specs=[vmem, vmem, vmem, smem, vmem, vmem, vmem, vmem] + [hbm] * 8,
        out_specs=vmem,
        scratch_shapes=[V(w.shape, BF) for w in weights]
        + [
            V((ROWS, LINE, D1), BF),
            V((ROWS + 2 * REACH + 1, LINE, D1), BF),
            V((256, D1), BF),
            V((256, D1), BF),
            V((2, WIN, SPAN), BF),
            V((3, WIN, 256), BF),
            V((TOK, 6 * 256 + 128), BF),
            V((3 * WIN, 3 * D1), BF),
            V((D1, 6 * 256), BF),
            V((128, D1), BF),
            V((128, D1), BF),
            V((TOK, D1), F32),
            V((TOK, D1), BF),
            V((TOK, D1), F32),
            V((TOK2, D2), BF),
            V((448, D2), BF),
            V((448, D2), BF),
            V((2 * WIN, 448), BF),
            V((2 * WIN, 3 * D2), BF),
            V((D2, 2 * held), BF),
            V((64, D2), BF),
            V((64, D2), BF),
            pltpu.SemaphoreType.DMA((8,)),
            pltpu.SemaphoreType.DMA((12,)),
            pltpu.SemaphoreType.DMA((12,)),
        ],
        compiler_params=pltpu.CompilerParams(
            collective_id=0, has_side_effects=True, vmem_limit_bytes=56 * 1024 * 1024
        ),
    )(
        tokens, land_mask, land_embed.reshape(1, D1), shifts, gain_attn.reshape(1, D1),
        gain_mlp.reshape(1, D1), gain_merge.reshape(1, 4 * D1), gain_coarse.reshape(1, D2), *weights,
    )


def solution(mesh):
    spec = P(None, "lat", "lon", None)
    return jax.shard_map(
        local,
        mesh=mesh,
        in_specs=(spec, P("lat", "lon")) + (P(),) * 14,
        out_specs=spec,
        check_vma=False,
    )
```

```python
import jax
import jax.numpy as jnp
from jax import lax
from jax.experimental import pallas as pl
from jax.experimental.pallas import tpu as pltpu
from jax.sharding import PartitionSpec as P

HEAD = 64
WLAT = 6
WLON = 12
WIN = 2 * WLAT * WLON
REACH = 5
MAIN = 128
REST = WIN - MAIN

D1 = 512
D2 = 1024
FF1 = 2048
held = MAIN + REST * (D2 // HEAD)
ROWS, COLS = 12, 24
ROWS2, COLS2 = 6, 12
TOK = 2 * ROWS * COLS
TOK2 = 2 * ROWS2 * COLS2
LINE = 2 * COLS
SPAN = (WLAT + REACH) * LINE

EPSILON = 1e-05
NEGATIVE = -1e30
SCALE = HEAD ** (-0.5) * 1.4426950408889634
BF = jnp.bfloat16
F32 = jnp.float32
I32 = jnp.int32
MESH = pl.DeviceIdType.MESH


def div(x, d):
    return (x * ((1 << 20) // d + 1)) >> 20


def col(n):
    return lax.broadcasted_iota(I32, (n, 1), 0)


def row(n):
    return lax.broadcasted_iota(I32, (1, n), 1)


def onehot(target, lanes):
    return jnp.where(lanes == target, 1.0, 0.0).astype(BF)


def mm(a, b):
    return lax.dot_general(a, b, (((1,), (0,)), ((), ())), preferred_element_type=F32)


def mm_nt(a, b):
    return lax.dot_general(a, b, (((1,), (1,)), ((), ())), preferred_element_type=F32)


def mm_tn(a, b):
    return lax.dot_general(a, b, (((0,), (0,)), ((), ())), preferred_element_type=F32)


def norm(x, gain):
    mean = jnp.mean(x, axis=-1, keepdims=True)
    center = x - mean
    var = jnp.mean(center * center, axis=-1, keepdims=True)
    return (center * lax.rsqrt(var + EPSILON) * gain).astype(BF)


def slot_parts(s):
    r = div(s, 24)
    rest = s - r * 24
    lev = div(rest, 12)
    return r, lev, rest - lev * 12


def soften(s, bias):
    s = s + bias
    top = jnp.max(s, axis=0, keepdims=True)
    p = jnp.exp2(s * SCALE - top * SCALE)
    total = jnp.sum(p, axis=0, keepdims=True)
    return p.astype(BF), 1.0 / total


def window_attend(q_of, k_of, v_of, width, bias, put):
    heads = width // HEAD
    pairs = heads // 2
    lane = row(2 * HEAD)
    every = pl.ds(0, width)
    parts = [pl.ds(i * 2 * HEAD, 2 * HEAD) for i in range(pairs)]
    spread = REST * heads
    tiled = jnp.concatenate([q_of(pl.ds(MAIN, REST), every)] * heads, axis=0)
    own = (col(spread) >> 4) == (row(width) >> 6)
    tiled = jnp.where(own, tiled, jnp.zeros_like(tiled))
    scores = [mm_nt(k_of(every), tiled)]
    for part in parts:
        q = q_of(pl.ds(0, MAIN), part)
        zero = jnp.zeros_like(q)
        both = jnp.concatenate(
            [jnp.where(lane < HEAD, q, zero), jnp.where(lane < HEAD, zero, q)], axis=0
        )
        scores.append(mm_nt(k_of(part), both))
    weights = [soften(x, bias) for x in scores]
    results = [mm_tn(v_of(part), p) for part, (p, _) in zip([every] + parts, weights)]
    o = results[0] * weights[0][1]
    o = jnp.where((col(width) >> 6) == (row(spread) >> 4), o, 0.0)
    put(0, width, MAIN, spread, o)
    for i in range(pairs):
        o = results[i + 1] * weights[i + 1][1]
        put(i * 2 * HEAD, HEAD, 0, MAIN, o[:HEAD, :MAIN])
        put(i * 2 * HEAD + HEAD, HEAD, 0, MAIN, o[HEAD:, MAIN:])


def kernel(
    tokens, mask, embed, shifts, gain_attn, gain_mlp, gain_merge, gain_coarse,
    w_qkv_h, w_out_h, w_up_h, w_down_h, w_merge_h, w_qkv2_h, w_out2_h, w_expand_h,
    out,
    w_qkv, w_out, w_up, w_down, w_merge, w_qkv2, w_out2, w_expand,
    inputs, ext, side_out, side, sel_own, sel_side, sel_back, qkv, mixed, back_out, back_in,
    resid, skipped, acc,
    norm2, send2, ext2, sel2, sel2_own, x2, qkv2, mixed2, back2_out, last_out, back2_in,
    w_sem, send_sem, recv_sem,
):
    lat = lax.axis_index("lat")
    lon = lax.axis_index("lon")
    lat_n = lax.axis_size("lat")
    lon_n = lax.axis_size("lon")
    right = lax.rem(lon + 1, lon_n)
    left = lax.rem(lon + lon_n - 1, lon_n)
    has_up = lat > 0
    has_down = lat < lat_n - 1

    loads = []
    for i, (src, dst) in enumerate(
        [
            (w_qkv_h, w_qkv), (w_out_h, w_out), (w_up_h, w_up), (w_down_h, w_down),
            (w_merge_h, w_merge), (w_qkv2_h, w_qkv2), (w_out2_h, w_out2), (w_expand_h, w_expand),
        ]
    ):
        load = pltpu.make_async_copy(src, dst, w_sem.at[i])
        load.start()
        loads.append(load)

    barrier = pltpu.get_barrier_semaphore()

    def greet(a, b):
        pl.semaphore_signal(barrier, inc=1, device_id=(a, b), device_id_type=MESH)

    greet(lat, left)
    greet(lat, right)

    @pl.when(has_up)
    def _():
        for b in (left, lon, right):
            greet(lat - 1, b)

    @pl.when(has_down)
    def _():
        for b in (left, lon, right):
            greet(lat + 1, b)

    def remote(i, src, dst, a, b):
        return pltpu.make_async_remote_copy(
            src_ref=src, dst_ref=dst, send_sem=send_sem.at[i], recv_sem=recv_sem.at[i],
            device_id=(a, b), device_id_type=MESH,
        )

    eye = col(COLS) == row(COLS)
    add = embed[...]
    gain = gain_attn[...]
    for r in range(ROWS):
        land = jnp.sum(jnp.where(eye, mask[r : r + 1, :].astype(F32), 0.0), axis=1, keepdims=True)
        x = jnp.concatenate(
            [tokens[0, r].astype(F32) + land * add, tokens[1, r].astype(F32) + land * add], axis=0
        ).astype(BF)
        inputs[r] = x
        ext[REACH + r] = norm(x.astype(F32), gain)

    s = col(256)
    part = jnp.where(s < 128, 0, jnp.where(s < 192, 1, 2))
    within = s - jnp.where(part == 0, 0, jnp.where(part == 1, 128, 192))
    r = div(within, 10)
    rest = within - r * 10
    lev = div(rest, 5)
    c = rest - lev * 5
    r = r + jnp.where(part == 1, ROWS - REACH, 0)
    target = jnp.where(r < ROWS, r * LINE + lev * COLS + c + (COLS - REACH), -1)
    own = ext[REACH : REACH + ROWS].reshape(TOK, D1)
    side_out[...] = mm(onehot(target, row(TOK)), own).astype(BF)

    @pl.when(jnp.logical_not(has_up))
    def _():
        ext2[0:128] = jnp.zeros((128, D2), BF)
        ext2[192:256] = jnp.zeros((64, D2), BF)

    ext[2 * REACH + ROWS] = jnp.zeros((LINE, D1), BF)

    @pl.when(jnp.logical_not(has_up))
    def _():
        ext[0:REACH] = jnp.zeros((REACH, LINE, D1), BF)
        side[128:192] = jnp.zeros((64, D1), BF)

    @pl.when(jnp.logical_not(has_down))
    def _():
        ext[REACH + ROWS : 2 * REACH + ROWS] = jnp.zeros((REACH, LINE, D1), BF)
        side[192:256] = jnp.zeros((64, D1), BF)

    pl.semaphore_wait(
        barrier, 2 + jnp.where(has_up, 3, 0) + jnp.where(has_down, 3, 0)
    )

    go_right = remote(0, side_out.at[0:128], side.at[0:128], lat, right)
    go_down = remote(1, ext.at[ROWS : ROWS + REACH], ext.at[0:REACH], lat + 1, lon)
    go_up = remote(2, ext.at[REACH : 2 * REACH], ext.at[REACH + ROWS : 2 * REACH + ROWS], lat - 1, lon)
    go_down_right = remote(3, side_out.at[128:192], side.at[128:192], lat + 1, right)
    go_up_right = remote(4, side_out.at[192:256], side.at[192:256], lat - 1, right)

    def exchange(r_, d_, u_, dr_, ur_):
        r_.start()

        @pl.when(has_down)
        def _():
            d_.start()
            dr_.start()

        @pl.when(has_up)
        def _():
            u_.start()
            ur_.start()

    def arrived(d_, u_, dr_, ur_):
        @pl.when(has_up)
        def _():
            d_.wait_recv()
            dr_.wait_recv()

        @pl.when(has_down)
        def _():
            u_.wait_recv()
            ur_.wait_recv()

    def sent(r_, d_, u_, dr_, ur_):
        r_.wait_send()

        @pl.when(has_down)
        def _():
            d_.wait_send()
            dr_.wait_send()

        @pl.when(has_up)
        def _():
            u_.wait_send()
            ur_.wait_send()

    moves = (go_right, go_down, go_up, go_down_right, go_up_right)
    exchange(*moves)

    a = shifts[0, 0]
    b = shifts[0, 1]

    sr, sl, sc = slot_parts(col(WIN))
    for jc in range(2):
        c = sc + (WLON * jc) - b
        target = jnp.where(c >= 0, (sr + REACH - a) * LINE + sl * COLS + c, -1)
        sel_own[jc] = onehot(target, row(SPAN))
    c = sc - b
    for jr in range(3):
        r = sr + (WLAT * jr) - a
        place = jnp.where(
            r < 0, 128 + (r + REACH) * 10, jnp.where(r < ROWS, r * 10, 192 + (r - ROWS) * 10)
        )
        target = jnp.where(c < 0, place + sl * 5 + c + REACH, -1)
        sel_side[jr] = onehot(target, row(256))

    q = col(TOK)
    k = div(q, TOK2)
    cr, clev, cc = slot_parts(q - k * TOK2)
    fr = cr * 2 + (k & 1)
    fc = cc * 2 + (k >> 1)
    resid[...] = mm(
        onehot(fr * LINE + clev * COLS + fc, row(TOK)), inputs[...].reshape(TOK, D1)
    )
    up = fr + a
    jr = div(up, WLAT)
    over = fc + b
    jc = div(over, WLON)
    slot = ((up - jr * WLAT) * 2 + clev) * WLON + (over - jc * WLON)
    lanes = row(256)
    lanes = jnp.where(lanes < MAIN, lanes, MAIN + (lanes & 15))
    for w in range(6):
        target = jnp.where((jr == w % 3) & (jc == w // 3), slot, -1)
        sel_back[:, w * 256 : (w + 1) * 256] = onehot(target, lanes)
    target = jnp.where(
        jc == 2, jr * 64 + ((up - jr * WLAT) * 2 + clev) * REACH + over - COLS, -1
    )
    sel_back[:, 6 * 256 :] = onehot(target, row(192))

    loads[0].wait()

    def key_bias(jr, rows, a, lat_rows):
        r = sr + jr * WLAT - a + lat * rows
        return jnp.where((r >= 0) & (r < lat_rows), 0.0, NEGATIVE).astype(F32)

    def project(at, x):
        qkv[at * WIN : (at + 1) * WIN] = mm(x, w_qkv[...]).astype(BF)

    def gather(jr, jc):
        x = mm(sel_own[jc], ext[WLAT * jr : WLAT * jr + WLAT + REACH].reshape(SPAN, D1))
        if jc == 0:
            n = 128 if jr == 1 else 256
            x = x + mm(sel_side[jr, :, 0:n], side[0:n])
        return x.astype(BF)

    def attend(at, jr, jc):
        base = at * WIN
        lane0 = (jc * 3 + jr) * 256

        def put(r0, rn, l0, ln, value):
            mixed[r0 : r0 + rn, lane0 + l0 : lane0 + l0 + ln] = value.astype(BF)

        window_attend(
            lambda rows, part: qkv[pl.ds(base + rows.start, rows.size), part],
            lambda part: qkv[pl.ds(base, WIN), pl.ds(D1 + part.start, part.size)],
            lambda part: qkv[pl.ds(base, WIN), pl.ds(2 * D1 + part.start, part.size)],
            D1,
            key_bias(jr, ROWS, a, ROWS * lat_n),
            put,
        )

    s = col(64)
    r = div(s, 10)
    rest = s - r * 10
    lev = div(rest, 5)
    first = jnp.where(r < WLAT, (r * 2 + lev) * WLON + rest - lev * 5, -1)
    pick_first = onehot(first, lanes)
    returns = []

    def give_back(jr):
        part = pl.ds(jr * 64, 64)
        back_out[part, :] = mm_nt(pick_first, mixed[:, jr * 256 : (jr + 1) * 256]).astype(BF)
        copy = remote(11 + jr, back_out.at[part], back_in.at[part], lat, left)
        copy.start()
        returns.append(copy)

    project(0, gather(1, 1))
    attend(0, 1, 1)
    moves[0].wait_recv()
    project(1, gather(1, 0))
    attend(1, 1, 0)
    give_back(1)

    arrived(*moves[1:])
    for at, jr in ((2, 0), (3, 2)):
        project(at, gather(jr, 0))
        attend(at, jr, 0)
        give_back(jr)

    project(4, gather(0, 1))
    project(5, gather(2, 1))
    attend(4, 0, 1)
    attend(5, 2, 1)

    own = mm_nt(sel_back[:, 0 : 6 * 256], mixed[...])
    loads[1].wait()
    for copy in returns:
        copy.wait_recv()
    own = (own + mm(sel_back[:, 6 * 256 :], back_in[...])).astype(BF)
    attended = (resid[...] + mm(own, w_out[...])).astype(BF)
    resid[...] = attended.astype(F32)
    x = norm(attended.astype(F32), gain_mlp[...])

    loads[2].wait()
    loads[3].wait()
    chunk = 512
    acc[...] = resid[...]
    for i in range(FF1 // chunk):
        h = mm(x, w_up[:, i * chunk : (i + 1) * chunk])
        h = jax.nn.gelu(h).astype(BF)
        acc[...] += mm(h, w_down[i * chunk : (i + 1) * chunk, :])
    skipped[...] = acc[...].astype(BF)

    loads[4].wait()
    merged = jnp.concatenate(
        [skipped[i * TOK2 : (i + 1) * TOK2, :].astype(F32) for i in range(4)], axis=1
    )
    coarse = mm(norm(merged, gain_merge[...]), w_merge[...]).astype(BF)
    acc2 = coarse.astype(F32)
    normed = norm(acc2, gain_coarse[...])
    norm2[...] = normed

    a2 = shifts[1, 0]
    b2 = shifts[1, 1]

    s = col(256)
    is_row = s < 128
    r_row = div(s, 24)
    lev_row = div(s - r_row * 24, 12)
    c_row = s - r_row * 24 - lev_row * 12
    v = jnp.where(s < 192, jnp.maximum(s - 128, 0), s - 192)
    r_col = div(v, 10)
    lev_col = div(v - r_col * 10, 5)
    c_col = v - r_col * 10 - lev_col * 5 + COLS2 - REACH
    r = jnp.where(is_row, r_row, r_col) + jnp.where(is_row | (s >= 192), ROWS2 - REACH, 0)
    lev = jnp.where(is_row, lev_row, lev_col)
    c = jnp.where(is_row, c_row, c_col)
    target = jnp.where(r < ROWS2, (r * 2 + lev) * COLS2 + c, -1)
    send2[...] = mm(onehot(target, row(TOK2)), normed).astype(BF)

    right2 = remote(5, send2.at[128:192], ext2.at[128:192], lat, right)
    down2 = remote(6, send2.at[0:128], ext2.at[0:128], lat + 1, lon)
    corner2 = remote(7, send2.at[192:256], ext2.at[192:256], lat + 1, right)
    right2.start()

    @pl.when(has_down)
    def _():
        down2.start()
        corner2.start()

    c = sc - b2
    for w in range(2):
        r = sr + WLAT * w - a2
        inside = (r >= 0) & (r < ROWS2)
        target = jnp.where(inside & (c >= 0), (r * 2 + sl) * COLS2 + c, -1)
        sel2_own[w * WIN : (w + 1) * WIN, :] = onehot(target, row(TOK2))
        base_row = jnp.where(r < 0, (r + REACH) * 24 + sl * 12 + c, -1)
        base_col = jnp.where(
            r < 0, 192 + (r + REACH) * 10, jnp.where(r < ROWS2, 128 + r * 10, -1000)
        ) + sl * 5 + c + REACH
        target = jnp.where(c < 0, base_col, base_row)
        sel2[w * WIN : (w + 1) * WIN, :] = onehot(target, row(256))

    def collect(w):
        part = pl.ds(w * WIN, WIN)
        return (mm(sel2_own[part, :], norm2[...]) + mm(sel2[part, :], ext2[...])).astype(BF)

    lanes = row(held)
    lanes = jnp.where(lanes < MAIN, lanes, MAIN + (lanes & 15))
    up = sr + a2
    over = sc + b2
    here = (up < WLAT) & (over < COLS2)
    pick_here = onehot(jnp.where(here, (up * 2 + sl) * WLON + over, -1), lanes)
    below = up >= WLAT
    up = jnp.where(below, up - WLAT, up)
    target = jnp.where(
        over < COLS2,
        jnp.where(below, (up * 2 + sl) * WLON + over, -1),
        jnp.where(below, 192, 128) + (up * 2 + sl) * REACH + over - COLS2,
    )
    pick_there = onehot(target, row(256))
    s = col(192)
    target = jnp.where(s < 128, s, jnp.concatenate([jnp.zeros((128, 1), I32), first], axis=0))
    pick_out = onehot(target, lanes)

    loads[5].wait()
    right2.wait_recv()

    @pl.when(has_up)
    def _():
        down2.wait_recv()
        corner2.wait_recv()

    x2[0:WIN] = collect(0)

    @pl.when(has_down)
    def _():
        for i in range(3):
            part = slice(i * D2, (i + 1) * D2)
            qkv2[0:WIN, part] = mm(x2[0:WIN], w_qkv2[:, part]).astype(BF)

    @pl.when(jnp.logical_not(has_down))
    def _():
        x2[WIN:] = collect(1)
        for i in range(3):
            part = slice(i * D2, (i + 1) * D2)
            qkv2[:, part] = mm(x2[...], w_qkv2[:, part]).astype(BF)

    def attend2(w):
        base = w * WIN

        def put(r0, rn, l0, ln, value):
            mixed2[r0 : r0 + rn, l0 : l0 + ln] = value.astype(BF)

        window_attend(
            lambda rows, part: qkv2[pl.ds(base + rows.start, rows.size), part],
            lambda part: qkv2[pl.ds(base, WIN), pl.ds(D2 + part.start, part.size)],
            lambda part: qkv2[pl.ds(base, WIN), pl.ds(2 * D2 + part.start, part.size)],
            D2,
            key_bias(w, ROWS2, a2, ROWS2 * lat_n),
            put,
        )

    attend2(0)
    back2_out[...] = mm_nt(pick_out, mixed2[...]).astype(BF)
    left2 = remote(8, back2_out.at[128:192], back2_in.at[128:192], lat, left)
    up2 = remote(9, back2_out.at[0:128], back2_in.at[0:128], lat - 1, lon)
    up_left2 = remote(10, back2_out.at[128:192], back2_in.at[192:256], lat - 1, left)
    last_left2 = remote(14, last_out, back2_in.at[192:256], lat, left)
    left2.start()

    @pl.when(has_up)
    def _():
        up2.start()
        up_left2.start()

    own2 = mm_nt(pick_here, mixed2[...])

    @pl.when(jnp.logical_not(has_down))
    def _():
        attend2(1)
        leaving = mm_nt(pick_out, mixed2[...]).astype(BF)
        back2_in[0:128] = leaving[0:128]
        last_out[...] = leaving[128:192]
        last_left2.start()
        last_left2.wait_recv()

    loads[6].wait()
    loads[7].wait()
    left2.wait_recv()

    @pl.when(has_down)
    def _():
        up2.wait_recv()
        up_left2.wait_recv()

    own2 = (own2 + mm(pick_there, back2_in[...])).astype(BF)
    coarse_out = (acc2 + mm(own2, w_out2[...])).astype(BF)
    for i in range(4):
        part = slice(i * TOK2, (i + 1) * TOK2)
        spread = mm(coarse_out, w_expand[:, i * D1 : (i + 1) * D1])
        skipped[part, :] = (skipped[part, :].astype(F32) + spread).astype(BF)

    t = col(TOK)
    lev = div(t, ROWS * COLS)
    rest = t - lev * (ROWS * COLS)
    r = div(rest, COLS)
    c = rest - r * COLS
    target = ((c & 1) * 2 + (r & 1)) * TOK2 + ((r >> 1) * 2 + lev) * COLS2 + (c >> 1)
    final = mm(onehot(target, row(TOK)), skipped[...])
    out[...] = final.reshape(2, ROWS, COLS, D1).astype(BF)

    sent(*moves)
    right2.wait_send()
    left2.wait_send()

    @pl.when(has_down)
    def _():
        down2.wait_send()
        corner2.wait_send()

    @pl.when(has_up)
    def _():
        up2.wait_send()
        up_left2.wait_send()

    @pl.when(jnp.logical_not(has_down))
    def _():
        last_left2.wait_send()

    for copy in returns:
        copy.wait_send()


def local(
    tokens, land_mask, land_embed, shifts, gain_attn, w_qkv_fine, w_out_fine, gain_mlp, w_up_fine,
    w_down_fine, gain_merge, w_merge, gain_coarse, w_qkv_coarse, w_out_coarse, w_expand,
):
    vmem = pl.BlockSpec(memory_space=pltpu.VMEM)
    hbm = pl.BlockSpec(memory_space=pl.ANY)
    smem = pl.BlockSpec(memory_space=pltpu.SMEM)
    weights = [
        w_qkv_fine, w_out_fine, w_up_fine, w_down_fine, w_merge, w_qkv_coarse, w_out_coarse, w_expand,
    ]
    V = pltpu.VMEM
    return pl.pallas_call(
        kernel,
        out_shape=jax.ShapeDtypeStruct(tokens.shape, BF),
        in_specs=[vmem, vmem, vmem, smem, vmem, vmem, vmem, vmem] + [hbm] * 8,
        out_specs=vmem,
        scratch_shapes=[V(w.shape, BF) for w in weights]
        + [
            V((ROWS, LINE, D1), BF),
            V((ROWS + 2 * REACH + 1, LINE, D1), BF),
            V((256, D1), BF),
            V((256, D1), BF),
            V((2, WIN, SPAN), BF),
            V((3, WIN, 256), BF),
            V((TOK, 6 * 256 + 192), BF),
            V((6 * WIN, 3 * D1), BF),
            V((D1, 6 * 256), BF),
            V((192, D1), BF),
            V((192, D1), BF),
            V((TOK, D1), F32),
            V((TOK, D1), BF),
            V((TOK, D1), F32),
            V((TOK2, D2), BF),
            V((256, D2), BF),
            V((256, D2), BF),
            V((2 * WIN, 256), BF),
            V((2 * WIN, TOK2), BF),
            V((2 * WIN, D2), BF),
            V((2 * WIN, 3 * D2), BF),
            V((D2, held), BF),
            V((192, D2), BF),
            V((64, D2), BF),
            V((256, D2), BF),
            pltpu.SemaphoreType.DMA((8,)),
            pltpu.SemaphoreType.DMA((15,)),
            pltpu.SemaphoreType.DMA((15,)),
        ],
        compiler_params=pltpu.CompilerParams(
            collective_id=0, has_side_effects=True, vmem_limit_bytes=56 * 1024 * 1024
        ),
    )(
        tokens, land_mask, land_embed.reshape(1, D1), shifts, gain_attn.reshape(1, D1),
        gain_mlp.reshape(1, D1), gain_merge.reshape(1, 4 * D1), gain_coarse.reshape(1, D2), *weights,
    )


def solution(mesh):
    spec = P(None, "lat", "lon", None)
    return jax.shard_map(
        local,
        mesh=mesh,
        in_specs=(spec, P("lat", "lon")) + (P(),) * 14,
        out_specs=spec,
        check_vma=False,
    )
```

```python
import jax
import jax.numpy as jnp
from jax import lax
from jax.experimental import pallas as pl
from jax.experimental.pallas import tpu as pltpu
from jax.sharding import PartitionSpec as P

HEAD = 64
WLAT = 6
WLON = 12
WIN = 2 * WLAT * WLON
REACH = 5
MAIN = 128
REST = WIN - MAIN

D1 = 512
D2 = 1024
FF1 = 2048
held = MAIN + REST * (D2 // HEAD)
ROWS, COLS = 12, 24
ROWS2, COLS2 = 6, 12
TOK = 2 * ROWS * COLS
TOK2 = 2 * ROWS2 * COLS2
HALF, HALF2 = TOK // 2, TOK2 // 2
LINE = 2 * COLS
SPAN = (WLAT + REACH) * LINE

EPSILON = 1e-05
NEGATIVE = -1e30
SCALE = HEAD ** (-0.5) * 1.4426950408889634
BF = jnp.bfloat16
F32 = jnp.float32
I32 = jnp.int32
MESH = pl.DeviceIdType.MESH


def div(x, d):
    return (x * ((1 << 20) // d + 1)) >> 20


def col(n):
    return lax.broadcasted_iota(I32, (n, 1), 0)


def row(n):
    return lax.broadcasted_iota(I32, (1, n), 1)


def onehot(target, lanes):
    return jnp.where(lanes == target, 1.0, 0.0).astype(BF)


def mm(a, b):
    return lax.dot_general(a, b, (((1,), (0,)), ((), ())), preferred_element_type=F32)


def mm_nt(a, b):
    return lax.dot_general(a, b, (((1,), (1,)), ((), ())), preferred_element_type=F32)


def mm_tn(a, b):
    return lax.dot_general(a, b, (((0,), (0,)), ((), ())), preferred_element_type=F32)


def norm(x, gain):
    mean = jnp.mean(x, axis=-1, keepdims=True)
    center = x - mean
    var = jnp.mean(center * center, axis=-1, keepdims=True)
    return (center * lax.rsqrt(var + EPSILON) * gain).astype(BF)


def slot_parts(s):
    r = div(s, 24)
    rest = s - r * 24
    lev = div(rest, 12)
    return r, lev, rest - lev * 12


def own_parts(t):
    half = div(t, HALF2)
    rest = t - half * HALF2
    rl = div(rest, COLS2 // 2)
    return rl >> 1, rl & 1, half * (COLS2 // 2) + rest - rl * (COLS2 // 2)


def soften(s, bias):
    s = s + bias
    top = jnp.max(s, axis=0, keepdims=True)
    p = jnp.exp2(s * SCALE - top * SCALE)
    total = jnp.sum(p, axis=0, keepdims=True)
    return p.astype(BF), 1.0 / total


def window_attend(q_of, k_of, v_of, width, bias, put):
    heads = width // HEAD
    pairs = heads // 2
    lane = row(2 * HEAD)
    every = pl.ds(0, width)
    parts = [pl.ds(i * 2 * HEAD, 2 * HEAD) for i in range(pairs)]
    spread = REST * heads
    tiled = jnp.concatenate([q_of(pl.ds(MAIN, REST), every)] * heads, axis=0)
    own = (col(spread) >> 4) == (row(width) >> 6)
    tiled = jnp.where(own, tiled, jnp.zeros_like(tiled))
    scores = [mm_nt(k_of(every), tiled)]
    for part in parts:
        q = q_of(pl.ds(0, MAIN), part)
        zero = jnp.zeros_like(q)
        both = jnp.concatenate(
            [jnp.where(lane < HEAD, q, zero), jnp.where(lane < HEAD, zero, q)], axis=0
        )
        scores.append(mm_nt(k_of(part), both))
    weights = [soften(x, bias) for x in scores]
    results = [mm_tn(v_of(part), p) for part, (p, _) in zip([every] + parts, weights)]
    o = results[0] * weights[0][1]
    o = jnp.where((col(width) >> 6) == (row(spread) >> 4), o, 0.0)
    put(0, width, MAIN, spread, o)
    for i in range(pairs):
        o = results[i + 1] * weights[i + 1][1]
        put(i * 2 * HEAD, HEAD, 0, MAIN, o[:HEAD, :MAIN])
        put(i * 2 * HEAD + HEAD, HEAD, 0, MAIN, o[HEAD:, MAIN:])


def kernel(
    tokens, mask, embed, shifts, gain_attn, gain_mlp, gain_merge, gain_coarse,
    w_qkv_h, w_out_h, w_up_h, w_down_h, w_merge_h, w_qkv2_h, w_out2_h, w_expand_h,
    out,
    w_qkv, w_out, w_up, w_down, w_merge, w_qkv2, w_out2, w_expand,
    inputs, ext, side_out, side, sel_own, sel_side, sel_back, qkv, mixed, back_out, back_in,
    resid, acc,
    norm2, send2, ext2, sel2, sel2_own, x2, qkv2, mixed2, back2_out, last_out, back2_in,
    w_sem, send_sem, recv_sem,
):
    lat = lax.axis_index("lat")
    lon = lax.axis_index("lon")
    lat_n = lax.axis_size("lat")
    lon_n = lax.axis_size("lon")
    right = lax.rem(lon + 1, lon_n)
    left = lax.rem(lon + lon_n - 1, lon_n)
    has_up = lat > 0
    has_down = lat < lat_n - 1
    odd = lax.rem(lat, 2) == 1
    even = jnp.logical_not(odd)

    loads = []
    for i, (src, dst) in enumerate(
        [
            (w_qkv_h, w_qkv), (w_out_h, w_out), (w_up_h, w_up), (w_down_h, w_down),
            (w_merge_h, w_merge), (w_qkv2_h, w_qkv2), (w_out2_h, w_out2), (w_expand_h, w_expand),
        ]
    ):
        load = pltpu.make_async_copy(src, dst, w_sem.at[i])
        load.start()
        loads.append(load)

    barrier = pltpu.get_barrier_semaphore()

    def greet(a, b):
        pl.semaphore_signal(barrier, inc=1, device_id=(a, b), device_id_type=MESH)

    greet(lat, left)
    greet(lat, right)

    @pl.when(has_up)
    def _():
        for b in (left, lon, right):
            greet(lat - 1, b)

    @pl.when(has_down)
    def _():
        for b in (left, lon, right):
            greet(lat + 1, b)

    def remote(i, src, dst, a, b):
        return pltpu.make_async_remote_copy(
            src_ref=src, dst_ref=dst, send_sem=send_sem.at[i], recv_sem=recv_sem.at[i],
            device_id=(a, b), device_id_type=MESH,
        )

    eye = col(COLS) == row(COLS)
    add = embed[...]
    gain = gain_attn[...]
    for r in range(ROWS):
        land = jnp.sum(jnp.where(eye, mask[r : r + 1, :].astype(F32), 0.0), axis=1, keepdims=True)
        x = jnp.concatenate(
            [tokens[0, r].astype(F32) + land * add, tokens[1, r].astype(F32) + land * add], axis=0
        ).astype(BF)
        inputs[r] = x
        ext[REACH + r] = norm(x.astype(F32), gain)

    s = col(256)
    part = jnp.where(s < 128, 0, jnp.where(s < 192, 1, 2))
    within = s - jnp.where(part == 0, 0, jnp.where(part == 1, 128, 192))
    r = div(within, 10)
    rest = within - r * 10
    lev = div(rest, 5)
    c = rest - lev * 5
    r = r + jnp.where(part == 1, ROWS - REACH, 0)
    target = jnp.where(r < ROWS, r * LINE + lev * COLS + c + (COLS - REACH), -1)
    own = ext[REACH : REACH + ROWS].reshape(TOK, D1)
    side_out[...] = mm(onehot(target, row(TOK)), own).astype(BF)

    @pl.when(jnp.logical_not(has_up))
    def _():
        for at in (0, 128, 320):
            ext2[at : at + 64] = jnp.zeros((64, D2), BF)

    @pl.when(even | jnp.logical_not(has_down))
    def _():
        for at in (64, 192, 384):
            ext2[at : at + 64] = jnp.zeros((64, D2), BF)

    ext[2 * REACH + ROWS] = jnp.zeros((LINE, D1), BF)

    @pl.when(jnp.logical_not(has_up))
    def _():
        ext[0:REACH] = jnp.zeros((REACH, LINE, D1), BF)
        side[128:192] = jnp.zeros((64, D1), BF)

    @pl.when(jnp.logical_not(has_down))
    def _():
        ext[REACH + ROWS : 2 * REACH + ROWS] = jnp.zeros((REACH, LINE, D1), BF)
        side[192:256] = jnp.zeros((64, D1), BF)

    pl.semaphore_wait(
        barrier, 2 + jnp.where(has_up, 3, 0) + jnp.where(has_down, 3, 0)
    )

    go_right = remote(0, side_out.at[0:128], side.at[0:128], lat, right)
    go_down = remote(1, ext.at[ROWS : ROWS + REACH], ext.at[0:REACH], lat + 1, lon)
    go_up = remote(2, ext.at[REACH : 2 * REACH], ext.at[REACH + ROWS : 2 * REACH + ROWS], lat - 1, lon)
    go_down_right = remote(3, side_out.at[128:192], side.at[128:192], lat + 1, right)
    go_up_right = remote(4, side_out.at[192:256], side.at[192:256], lat - 1, right)

    def exchange(r_, d_, u_, dr_, ur_):
        r_.start()

        @pl.when(has_down)
        def _():
            d_.start()
            dr_.start()

        @pl.when(has_up)
        def _():
            u_.start()
            ur_.start()

    def arrived(d_, u_, dr_, ur_):
        @pl.when(has_up)
        def _():
            d_.wait_recv()
            dr_.wait_recv()

        @pl.when(has_down)
        def _():
            u_.wait_recv()
            ur_.wait_recv()

    def sent(r_, d_, u_, dr_, ur_):
        r_.wait_send()

        @pl.when(has_down)
        def _():
            d_.wait_send()
            dr_.wait_send()

        @pl.when(has_up)
        def _():
            u_.wait_send()
            ur_.wait_send()

    moves = (go_right, go_down, go_up, go_down_right, go_up_right)
    exchange(*moves)

    a = shifts[0, 0]
    b = shifts[0, 1]

    sr, sl, sc = slot_parts(col(WIN))
    for jc in range(2):
        c = sc + (WLON * jc) - b
        target = jnp.where(c >= 0, (sr + REACH - a) * LINE + sl * COLS + c, -1)
        sel_own[jc] = onehot(target, row(SPAN))
    c = sc - b
    for jr in range(3):
        r = sr + (WLAT * jr) - a
        place = jnp.where(
            r < 0, 128 + (r + REACH) * 10, jnp.where(r < ROWS, r * 10, 192 + (r - ROWS) * 10)
        )
        target = jnp.where(c < 0, place + sl * 5 + c + REACH, -1)
        sel_side[jr] = onehot(target, row(256))

    q = col(TOK)
    half = div(q, HALF)
    k = div(q - half * HALF, HALF2)
    cr, clev, cc = own_parts(q - half * HALF - k * HALF2)
    fr = cr * 2 + (k & 1)
    fc = (cc + half * (COLS2 // 2)) * 2 + (k >> 1)
    resid[...] = mm(
        onehot(fr * LINE + clev * COLS + fc, row(TOK)), inputs[...].reshape(TOK, D1)
    )
    up = fr + a
    jr = div(up, WLAT)
    over = fc + b
    jc = div(over, WLON)
    slot = ((up - jr * WLAT) * 2 + clev) * WLON + (over - jc * WLON)
    lanes = row(256)
    lanes = jnp.where(lanes < MAIN, lanes, MAIN + (lanes & 15))
    for w in range(6):
        target = jnp.where((jr == w % 3) & (jc == w // 3), slot, -1)
        sel_back[:, w * 256 : (w + 1) * 256] = onehot(target, lanes)
    target = jnp.where(
        jc == 2, jr * 64 + ((up - jr * WLAT) * 2 + clev) * REACH + over - COLS, -1
    )
    sel_back[:, 6 * 256 :] = onehot(target, row(192))

    loads[0].wait()

    def key_bias(jr, rows, a, lat_rows):
        r = sr + jr * WLAT - a + lat * rows
        return jnp.where((r >= 0) & (r < lat_rows), 0.0, NEGATIVE).astype(F32)

    def project(at, x):
        qkv[at * WIN : (at + 1) * WIN] = mm(x, w_qkv[...]).astype(BF)

    def gather(jr, jc):
        x = mm(sel_own[jc], ext[WLAT * jr : WLAT * jr + WLAT + REACH].reshape(SPAN, D1))
        if jc == 0:
            n = 128 if jr == 1 else 256
            x = x + mm(sel_side[jr, :, 0:n], side[0:n])
        return x.astype(BF)

    def attend(at, jr, jc):
        base = at * WIN
        lane0 = (jc * 3 + jr) * 256

        def put(r0, rn, l0, ln, value):
            mixed[r0 : r0 + rn, lane0 + l0 : lane0 + l0 + ln] = value.astype(BF)

        window_attend(
            lambda rows, part: qkv[pl.ds(base + rows.start, rows.size), part],
            lambda part: qkv[pl.ds(base, WIN), pl.ds(D1 + part.start, part.size)],
            lambda part: qkv[pl.ds(base, WIN), pl.ds(2 * D1 + part.start, part.size)],
            D1,
            key_bias(jr, ROWS, a, ROWS * lat_n),
            put,
        )

    s = col(64)
    r = div(s, 10)
    rest = s - r * 10
    lev = div(rest, 5)
    first = jnp.where(r < WLAT, (r * 2 + lev) * WLON + rest - lev * 5, -1)
    pick_first = onehot(first, lanes)
    returns = []

    def give_back(jr):
        part = pl.ds(jr * 64, 64)
        back_out[part, :] = mm_nt(pick_first, mixed[:, jr * 256 : (jr + 1) * 256]).astype(BF)
        copy = remote(11 + jr, back_out.at[part], back_in.at[part], lat, left)
        copy.start()
        returns.append(copy)

    project(0, gather(1, 1))
    attend(0, 1, 1)
    moves[0].wait_recv()
    project(1, gather(1, 0))
    attend(1, 1, 0)
    give_back(1)

    arrived(*moves[1:])
    for at, jr in ((2, 0), (3, 2)):
        project(at, gather(jr, 0))
        attend(at, jr, 0)
        give_back(jr)

    project(4, gather(0, 1))
    project(5, gather(2, 1))
    attend(4, 0, 1)
    attend(5, 2, 1)

    loads[1].wait()
    loads[2].wait()
    loads[3].wait()
    loads[4].wait()
    a2 = shifts[1, 0]
    b2 = shifts[1, 1]

    def message(i, there, d_lat, d_lon):
        part = pl.ds(i * 64, 64)
        return remote(i + 14, send2.at[part], ext2.at[part], there + d_lat, d_lon)

    downs = [message(i, lat, 1, lon) for i in (0, 2)] + [message(5, lat, 1, right)]
    ups = [message(i, lat, -1, lon) for i in (1, 3)] + [message(6, lat, -1, right)]
    right2 = message(4, lat, 0, right)
    goes_up = even & has_up
    from_below = odd & has_down

    s = col(64)
    rl6 = div(s, 6)
    lines = rl6 * 6 + (s - rl6 * 6)
    rl5 = div(s, 5)
    columns = rl5 * 6 + (s - rl5 * 5) + 1
    top = jnp.where(s < 60, lines, -1)
    bottom = jnp.where(s < 60, lines + 12, -1)
    aside = jnp.where(s < 60, columns, -1)
    aside_bottom = jnp.where(s < 50, columns + 12, -1)
    aside_top = jnp.where(s < 50, columns, -1)

    coarse = []
    for h in range(2):
        if h == 1:
            for copy in returns:
                copy.wait_recv()
        part = slice(h * HALF, (h + 1) * HALF)
        own = mm_nt(sel_back[part, 0 : 6 * 256], mixed[...])
        if h == 1:
            own = own + mm(sel_back[part, 6 * 256 :], back_in[...])
        attended = (resid[part] + mm(own.astype(BF), w_out[...])).astype(BF)
        total = attended.astype(F32)
        x = norm(total, gain_mlp[...])
        acc[part] = total
        chunk = 512
        for i in range(FF1 // chunk):
            y = mm(x, w_up[:, i * chunk : (i + 1) * chunk])
            y = jax.nn.gelu(y).astype(BF)
            acc[part] += mm(y, w_down[i * chunk : (i + 1) * chunk, :])
        total = acc[part].astype(BF).astype(F32)
        acc[part] = total
        merged = jnp.concatenate(
            [total[k * HALF2 : (k + 1) * HALF2] for k in range(4)], axis=1
        )
        merged = mm(norm(merged, gain_merge[...]), w_merge[...]).astype(BF).astype(F32)
        coarse.append(merged)
        normed = norm(merged, gain_coarse[...])
        norm2[h] = normed.astype(F32)
        if h == 0:
            pick = jnp.concatenate([bottom, top], axis=0)
            send2[0:128] = mm(onehot(pick, row(HALF2)), normed).astype(BF)
        else:
            pick = jnp.concatenate([bottom, top, aside, aside_bottom, aside_top], axis=0)
            send2[128:448] = mm(onehot(pick, row(HALF2)), normed).astype(BF)
            right2.start()

        @pl.when(has_down)
        def _():
            for copy in downs[h : 2 * h + 1]:
                copy.start()

        @pl.when(goes_up)
        def _():
            for copy in ups[h : 2 * h + 1]:
                copy.start()


    c = sc - b2
    for w in range(2):
        r = sr + WLAT * w - a2
        inside = (r >= 0) & (r < ROWS2)
        right_half = jnp.where(c >= 6, 1, 0)
        place = (r * 2 + sl) * 6 + c - right_half * 6
        for h in range(2):
            target = jnp.where(inside & (c >= 0) & (right_half == h), place, -1)
            sel2_own[w, h] = onehot(target, row(HALF2))
        beyond = jnp.where(r < 0, r + REACH, r - ROWS2)
        beyond = jnp.where(beyond < REACH, beyond, -1000)
        line = jnp.where(r < 0, 0, 64) + right_half * 128 + (beyond * 2 + sl) * 6 + c - right_half * 6
        corner = jnp.where(r < 0, 320, 384) + (beyond * 2 + sl) * 5 + c + REACH
        aside = 256 + (r * 2 + sl) * 5 + c + REACH
        target = jnp.where(
            inside, jnp.where(c < 0, aside, -1), jnp.where(c < 0, corner, line)
        )
        sel2[w * WIN : (w + 1) * WIN, :] = onehot(target, row(448))

    def collect(w):
        x = mm(sel2[w * WIN : (w + 1) * WIN, :], ext2[...])
        for h in range(2):
            x = x + mm(sel2_own[w, h], norm2[h].astype(BF))
        return x.astype(BF)

    lanes = row(held)
    lanes = jnp.where(lanes < MAIN, lanes, MAIN + (lanes & 15))
    pick_here, pick_there = [], []
    for h in range(2):
        rr, ll, cc = own_parts(col(HALF2) + h * HALF2)
        up = rr + a2
        over = cc + b2
        here = (up < WLAT) & (over < COLS2)
        pick_here.append(onehot(jnp.where(here, (up * 2 + ll) * WLON + over, -1), lanes))
        below = up >= WLAT
        up = jnp.where(below, up - WLAT, up)
        target = jnp.where(
            over < COLS2,
            jnp.where(below, (up * 2 + ll) * WLON + over, -1),
            jnp.where(below, 192, 128) + (up * 2 + ll) * REACH + over - COLS2,
        )
        pick_there.append(onehot(target, row(256)))
    s = col(192)
    target = jnp.where(s < 128, s, jnp.concatenate([jnp.zeros((128, 1), I32), first], axis=0))
    pick_out = onehot(target, lanes)

    loads[5].wait()
    right2.wait_recv()

    @pl.when(has_up)
    def _():
        for copy in downs:
            copy.wait_recv()

    @pl.when(from_below)
    def _():
        for copy in ups:
            copy.wait_recv()

    x2[0:WIN] = collect(0)

    @pl.when(even)
    def _():
        for i in range(3):
            part = slice(i * D2, (i + 1) * D2)
            qkv2[0:WIN, part] = mm(x2[0:WIN], w_qkv2[:, part]).astype(BF)

    @pl.when(odd)
    def _():
        x2[WIN:] = collect(1)
        for i in range(3):
            part = slice(i * D2, (i + 1) * D2)
            qkv2[:, part] = mm(x2[...], w_qkv2[:, part]).astype(BF)

    def attend2(w):
        base = w * WIN

        def put(r0, rn, l0, ln, value):
            mixed2[r0 : r0 + rn, l0 : l0 + ln] = value.astype(BF)

        window_attend(
            lambda rows, part: qkv2[pl.ds(base + rows.start, rows.size), part],
            lambda part: qkv2[pl.ds(base, WIN), pl.ds(D2 + part.start, part.size)],
            lambda part: qkv2[pl.ds(base, WIN), pl.ds(2 * D2 + part.start, part.size)],
            D2,
            key_bias(w, ROWS2, a2, ROWS2 * lat_n),
            put,
        )

    attend2(0)
    back2_out[...] = mm_nt(pick_out, mixed2[...]).astype(BF)
    left2 = remote(5, back2_out.at[128:192], back2_in.at[128:192], lat, left)
    up2 = remote(6, back2_out.at[0:128], back2_in.at[0:128], lat - 1, lon)
    up_left2 = remote(7, back2_out.at[128:192], back2_in.at[192:256], lat - 1, left)
    last_left2 = remote(8, last_out, back2_in.at[192:256], lat, left)

    @pl.when(odd)
    def _():
        up2.start()
        up_left2.start()

    left2.start()
    own2 = [mm_nt(pick, mixed2[...]) for pick in pick_here]

    @pl.when(odd)
    def _():
        attend2(1)
        leaving = mm_nt(pick_out, mixed2[...]).astype(BF)
        back2_in[0:128] = leaving[0:128]
        last_out[...] = leaving[128:192]
        last_left2.start()

    loads[6].wait()
    loads[7].wait()

    @pl.when(even)
    def _():
        up2.wait_recv()

    for h in range(2):
        if h == 0:
            other = mm(pick_there[0][:, 0:128], back2_in[0:128])
        else:
            left2.wait_recv()

            @pl.when(even)
            def _():
                up_left2.wait_recv()

            @pl.when(odd)
            def _():
                last_left2.wait_recv()

            other = mm(pick_there[1], back2_in[...])
        coarse_out = (coarse[h] + mm((own2[h] + other).astype(BF), w_out2[...])).astype(BF)
        for k in range(4):
            at = h * HALF + k * HALF2
            spread = mm(coarse_out, w_expand[:, k * D1 : (k + 1) * D1])
            acc[at : at + HALF2] = acc[at : at + HALF2] + spread

    t = col(TOK)
    lev = div(t, ROWS * COLS)
    rest = t - lev * (ROWS * COLS)
    r = div(rest, COLS)
    c = rest - r * COLS
    half = jnp.where(c >= COLS // 2, 1, 0)
    quadrant = (c & 1) * 2 + (r & 1)
    target = half * HALF + quadrant * HALF2 + ((r >> 1) * 2 + lev) * 6 + (c >> 1) - half * 6
    final = mm(onehot(target, row(TOK)), acc[...].astype(BF))
    out[...] = final.reshape(2, ROWS, COLS, D1).astype(BF)

    sent(*moves)
    right2.wait_send()
    left2.wait_send()

    @pl.when(has_down)
    def _():
        for copy in downs:
            copy.wait_send()

    @pl.when(goes_up)
    def _():
        for copy in ups:
            copy.wait_send()

    @pl.when(odd)
    def _():
        up2.wait_send()
        up_left2.wait_send()
        last_left2.wait_send()

    for copy in returns:
        copy.wait_send()


def local(
    tokens, land_mask, land_embed, shifts, gain_attn, w_qkv_fine, w_out_fine, gain_mlp, w_up_fine,
    w_down_fine, gain_merge, w_merge, gain_coarse, w_qkv_coarse, w_out_coarse, w_expand,
):
    vmem = pl.BlockSpec(memory_space=pltpu.VMEM)
    hbm = pl.BlockSpec(memory_space=pl.ANY)
    smem = pl.BlockSpec(memory_space=pltpu.SMEM)
    weights = [
        w_qkv_fine, w_out_fine, w_up_fine, w_down_fine, w_merge, w_qkv_coarse, w_out_coarse, w_expand,
    ]
    V = pltpu.VMEM
    return pl.pallas_call(
        kernel,
        out_shape=jax.ShapeDtypeStruct(tokens.shape, BF),
        in_specs=[vmem, vmem, vmem, smem, vmem, vmem, vmem, vmem] + [hbm] * 8,
        out_specs=vmem,
        scratch_shapes=[V(w.shape, BF) for w in weights]
        + [
            V((ROWS, LINE, D1), BF),
            V((ROWS + 2 * REACH + 1, LINE, D1), BF),
            V((256, D1), BF),
            V((256, D1), BF),
            V((2, WIN, SPAN), BF),
            V((3, WIN, 256), BF),
            V((TOK, 6 * 256 + 192), BF),
            V((6 * WIN, 3 * D1), BF),
            V((D1, 6 * 256), BF),
            V((192, D1), BF),
            V((192, D1), BF),
            V((TOK, D1), F32),
            V((TOK, D1), F32),
            V((2, HALF2, D2), F32),
            V((448, D2), BF),
            V((448, D2), BF),
            V((2 * WIN, 448), BF),
            V((2, 2, WIN, HALF2), BF),
            V((2 * WIN, D2), BF),
            V((2 * WIN, 3 * D2), BF),
            V((D2, held), BF),
            V((192, D2), BF),
            V((64, D2), BF),
            V((256, D2), BF),
            pltpu.SemaphoreType.DMA((8,)),
            pltpu.SemaphoreType.DMA((21,)),
            pltpu.SemaphoreType.DMA((21,)),
        ],
        compiler_params=pltpu.CompilerParams(
            collective_id=0, has_side_effects=True, vmem_limit_bytes=56 * 1024 * 1024
        ),
    )(
        tokens, land_mask, land_embed.reshape(1, D1), shifts, gain_attn.reshape(1, D1),
        gain_mlp.reshape(1, D1), gain_merge.reshape(1, 4 * D1), gain_coarse.reshape(1, D2), *weights,
    )


def solution(mesh):
    spec = P(None, "lat", "lon", None)
    return jax.shard_map(
        local,
        mesh=mesh,
        in_specs=(spec, P("lat", "lon")) + (P(),) * 14,
        out_specs=spec,
        check_vma=False,
    )
```

```python
import jax
import jax.numpy as jnp
from jax import lax
from jax.experimental import pallas as pl
from jax.experimental.pallas import tpu as pltpu
from jax.sharding import PartitionSpec as P

HEAD = 64
WLAT = 6
WLON = 12
WIN = 2 * WLAT * WLON
REACH = 5
MAIN = 128
REST = WIN - MAIN

D1 = 512
D2 = 1024
FF1 = 2048
held = MAIN + REST * (D2 // HEAD)
ROWS, COLS = 12, 24
ROWS2, COLS2 = 6, 12
TOK = 2 * ROWS * COLS
TOK2 = 2 * ROWS2 * COLS2
HALF, HALF2 = TOK // 2, TOK2 // 2
LINE = 2 * COLS
SPAN = (WLAT + REACH) * LINE

EPSILON = 1e-05
NEGATIVE = -1e30
SCALE = HEAD ** (-0.5) * 1.4426950408889634
BF = jnp.bfloat16
F32 = jnp.float32
I32 = jnp.int32
MESH = pl.DeviceIdType.MESH


def div(x, d):
    return (x * ((1 << 20) // d + 1)) >> 20


def col(n):
    return lax.broadcasted_iota(I32, (n, 1), 0)


def row(n):
    return lax.broadcasted_iota(I32, (1, n), 1)


def onehot(target, lanes):
    return jnp.where(lanes == target, 1.0, 0.0).astype(BF)


def mm(a, b):
    return lax.dot_general(a, b, (((1,), (0,)), ((), ())), preferred_element_type=F32)


def mm_nt(a, b):
    return lax.dot_general(a, b, (((1,), (1,)), ((), ())), preferred_element_type=F32)


def mm_tn(a, b):
    return lax.dot_general(a, b, (((0,), (0,)), ((), ())), preferred_element_type=F32)


def norm(x, gain):
    mean = jnp.mean(x, axis=-1, keepdims=True)
    center = x - mean
    var = jnp.mean(center * center, axis=-1, keepdims=True)
    return (center * lax.rsqrt(var + EPSILON) * gain).astype(BF)


def slot_parts(s):
    r = div(s, 24)
    rest = s - r * 24
    lev = div(rest, 12)
    return r, lev, rest - lev * 12


def own_parts(t):
    half = div(t, HALF2)
    rest = t - half * HALF2
    rl = div(rest, COLS2 // 2)
    return rl >> 1, rl & 1, half * (COLS2 // 2) + rest - rl * (COLS2 // 2)


def soften(s, bias):
    s = s + bias
    top = jnp.max(s, axis=0, keepdims=True)
    p = jnp.exp2(s * SCALE - top * SCALE)
    total = jnp.sum(p, axis=0, keepdims=True)
    return p.astype(BF), 1.0 / total


def window_attend(q_of, k_of, v_of, width, bias, put):
    heads = width // HEAD
    pairs = heads // 2
    lane = row(2 * HEAD)
    every = pl.ds(0, width)
    parts = [pl.ds(i * 2 * HEAD, 2 * HEAD) for i in range(pairs)]
    spread = REST * heads
    tiled = jnp.concatenate([q_of(pl.ds(MAIN, REST), every)] * heads, axis=0)
    own = (col(spread) >> 4) == (row(width) >> 6)
    tiled = jnp.where(own, tiled, jnp.zeros_like(tiled))
    scores = [mm_nt(k_of(every), tiled)]
    for part in parts:
        q = q_of(pl.ds(0, MAIN), part)
        zero = jnp.zeros_like(q)
        both = jnp.concatenate(
            [jnp.where(lane < HEAD, q, zero), jnp.where(lane < HEAD, zero, q)], axis=0
        )
        scores.append(mm_nt(k_of(part), both))
    weights = [soften(x, bias) for x in scores]
    results = [mm_tn(v_of(part), p) for part, (p, _) in zip([every] + parts, weights)]
    o = results[0] * weights[0][1]
    o = jnp.where((col(width) >> 6) == (row(spread) >> 4), o, 0.0)
    put(0, width, MAIN, spread, o)
    for i in range(pairs):
        o = results[i + 1] * weights[i + 1][1]
        put(i * 2 * HEAD, HEAD, 0, MAIN, o[:HEAD, :MAIN])
        put(i * 2 * HEAD + HEAD, HEAD, 0, MAIN, o[HEAD:, MAIN:])


def kernel(
    tokens_h, mask_h, embed_h, shifts, gain_attn_h, gain_mlp_h, gain_merge_h, gain_coarse_h,
    w_qkv_h, w_out_h, w_up_h, w_down_h, w_merge_h, w_qkv2_h, w_out2_h, w_expand_h,
    out,
    tokens, mask, embed, gain_attn, gain_mlp, gain_merge, gain_coarse,
    w_qkv, w_out, w_up, w_down, w_merge, w_qkv2, w_out2, w_expand,
    inputs, ext, side_out, side, sel_own, sel_side, sel_back, qkv, mixed, back_out, back_in,
    resid, acc,
    norm2, send2, ext2, sel2, sel2_own, x2, qkv2, mixed2, back2_out, last_out, back2_in,
    w_sem, send_sem, recv_sem,
):
    lat = lax.axis_index("lat")
    lon = lax.axis_index("lon")
    lat_n = lax.axis_size("lat")
    lon_n = lax.axis_size("lon")
    right = lax.rem(lon + 1, lon_n)
    left = lax.rem(lon + lon_n - 1, lon_n)
    has_up = lat > 0
    has_down = lat < lat_n - 1
    odd = lax.rem(lat, 2) == 1
    even = jnp.logical_not(odd)

    barrier = pltpu.get_barrier_semaphore()

    def greet(a, b):
        pl.semaphore_signal(barrier, inc=1, device_id=(a, b), device_id_type=MESH)

    greet(lat, left)
    greet(lat, right)

    @pl.when(has_up)
    def _():
        for b in (left, lon, right):
            greet(lat - 1, b)

    @pl.when(has_down)
    def _():
        for b in (left, lon, right):
            greet(lat + 1, b)

    loads = []
    for i, (src, dst) in enumerate(
        [
            (tokens_h, tokens), (mask_h, mask), (embed_h, embed), (gain_attn_h, gain_attn),
            (w_qkv_h, w_qkv), (gain_mlp_h, gain_mlp), (gain_merge_h, gain_merge),
            (gain_coarse_h, gain_coarse), (w_out_h, w_out), (w_up_h, w_up), (w_down_h, w_down),
            (w_merge_h, w_merge), (w_qkv2_h, w_qkv2), (w_out2_h, w_out2), (w_expand_h, w_expand),
        ]
    ):
        load = pltpu.make_async_copy(src, dst, w_sem.at[i])
        load.start()
        loads.append(load)

    def remote(i, src, dst, a, b):
        return pltpu.make_async_remote_copy(
            src_ref=src, dst_ref=dst, send_sem=send_sem.at[i], recv_sem=recv_sem.at[i],
            device_id=(a, b), device_id_type=MESH,
        )

    for load in loads[:4]:
        load.wait()
    eye = col(COLS) == row(COLS)
    add = embed[...]
    gain = gain_attn[...]
    for r in range(ROWS):
        land = jnp.sum(jnp.where(eye, mask[r : r + 1, :].astype(F32), 0.0), axis=1, keepdims=True)
        x = jnp.concatenate(
            [tokens[0, r].astype(F32) + land * add, tokens[1, r].astype(F32) + land * add], axis=0
        ).astype(BF)
        inputs[r] = x
        ext[REACH + r] = norm(x.astype(F32), gain)

    s = col(256)
    part = jnp.where(s < 128, 0, jnp.where(s < 192, 1, 2))
    within = s - jnp.where(part == 0, 0, jnp.where(part == 1, 128, 192))
    r = div(within, 10)
    rest = within - r * 10
    lev = div(rest, 5)
    c = rest - lev * 5
    r = r + jnp.where(part == 1, ROWS - REACH, 0)
    target = jnp.where(r < ROWS, r * LINE + lev * COLS + c + (COLS - REACH), -1)
    own = ext[REACH : REACH + ROWS].reshape(TOK, D1)
    side_out[...] = mm(onehot(target, row(TOK)), own).astype(BF)

    @pl.when(jnp.logical_not(has_up))
    def _():
        for at in (0, 128, 320):
            ext2[at : at + 64] = jnp.zeros((64, D2), BF)

    @pl.when(even | jnp.logical_not(has_down))
    def _():
        for at in (64, 192, 384):
            ext2[at : at + 64] = jnp.zeros((64, D2), BF)

    ext[2 * REACH + ROWS] = jnp.zeros((LINE, D1), BF)

    @pl.when(jnp.logical_not(has_up))
    def _():
        ext[0:REACH] = jnp.zeros((REACH, LINE, D1), BF)
        side[128:192] = jnp.zeros((64, D1), BF)

    @pl.when(jnp.logical_not(has_down))
    def _():
        ext[REACH + ROWS : 2 * REACH + ROWS] = jnp.zeros((REACH, LINE, D1), BF)
        side[192:256] = jnp.zeros((64, D1), BF)

    pl.semaphore_wait(
        barrier, 2 + jnp.where(has_up, 3, 0) + jnp.where(has_down, 3, 0)
    )

    go_right = remote(0, side_out.at[0:128], side.at[0:128], lat, right)
    go_down = remote(1, ext.at[ROWS : ROWS + REACH], ext.at[0:REACH], lat + 1, lon)
    go_up = remote(2, ext.at[REACH : 2 * REACH], ext.at[REACH + ROWS : 2 * REACH + ROWS], lat - 1, lon)
    go_down_right = remote(3, side_out.at[128:192], side.at[128:192], lat + 1, right)
    go_up_right = remote(4, side_out.at[192:256], side.at[192:256], lat - 1, right)

    def exchange(r_, d_, u_, dr_, ur_):
        r_.start()

        @pl.when(has_down)
        def _():
            d_.start()
            dr_.start()

        @pl.when(has_up)
        def _():
            u_.start()
            ur_.start()

    def arrived(d_, u_, dr_, ur_):
        @pl.when(has_up)
        def _():
            d_.wait_recv()
            dr_.wait_recv()

        @pl.when(has_down)
        def _():
            u_.wait_recv()
            ur_.wait_recv()

    def sent(r_, d_, u_, dr_, ur_):
        r_.wait_send()

        @pl.when(has_down)
        def _():
            d_.wait_send()
            dr_.wait_send()

        @pl.when(has_up)
        def _():
            u_.wait_send()
            ur_.wait_send()

    moves = (go_right, go_down, go_up, go_down_right, go_up_right)
    exchange(*moves)

    a = shifts[0, 0]
    b = shifts[0, 1]

    sr, sl, sc = slot_parts(col(WIN))
    for jc in range(2):
        c = sc + (WLON * jc) - b
        target = jnp.where(c >= 0, (sr + REACH - a) * LINE + sl * COLS + c, -1)
        sel_own[jc] = onehot(target, row(SPAN))
    c = sc - b
    for jr in range(3):
        r = sr + (WLAT * jr) - a
        place = jnp.where(
            r < 0, 128 + (r + REACH) * 10, jnp.where(r < ROWS, r * 10, 192 + (r - ROWS) * 10)
        )
        target = jnp.where(c < 0, place + sl * 5 + c + REACH, -1)
        sel_side[jr] = onehot(target, row(256))

    q = col(TOK)
    half = div(q, HALF)
    k = div(q - half * HALF, HALF2)
    cr, clev, cc = own_parts(q - half * HALF - k * HALF2)
    fr = cr * 2 + (k & 1)
    fc = (cc + half * (COLS2 // 2)) * 2 + (k >> 1)
    resid[...] = mm(
        onehot(fr * LINE + clev * COLS + fc, row(TOK)), inputs[...].reshape(TOK, D1)
    )
    up = fr + a
    jr = div(up, WLAT)
    over = fc + b
    jc = div(over, WLON)
    slot = ((up - jr * WLAT) * 2 + clev) * WLON + (over - jc * WLON)
    lanes = row(256)
    lanes = jnp.where(lanes < MAIN, lanes, MAIN + (lanes & 15))
    for w in range(6):
        target = jnp.where((jr == w % 3) & (jc == w // 3), slot, -1)
        sel_back[:, w * 256 : (w + 1) * 256] = onehot(target, lanes)
    target = jnp.where(
        jc == 2, jr * 64 + ((up - jr * WLAT) * 2 + clev) * REACH + over - COLS, -1
    )
    sel_back[:, 6 * 256 :] = onehot(target, row(192))

    loads[4].wait()

    def key_bias(jr, rows, a, lat_rows):
        r = sr + jr * WLAT - a + lat * rows
        return jnp.where((r >= 0) & (r < lat_rows), 0.0, NEGATIVE).astype(F32)

    def project(at, x):
        qkv[at * WIN : (at + 1) * WIN] = mm(x, w_qkv[...]).astype(BF)

    def gather(jr, jc):
        x = mm(sel_own[jc], ext[WLAT * jr : WLAT * jr + WLAT + REACH].reshape(SPAN, D1))
        if jc == 0:
            n = 128 if jr == 1 else 256
            x = x + mm(sel_side[jr, :, 0:n], side[0:n])
        return x.astype(BF)

    def attend(at, jr, jc):
        base = at * WIN
        lane0 = (jc * 3 + jr) * 256

        def put(r0, rn, l0, ln, value):
            mixed[r0 : r0 + rn, lane0 + l0 : lane0 + l0 + ln] = value.astype(BF)

        window_attend(
            lambda rows, part: qkv[pl.ds(base + rows.start, rows.size), part],
            lambda part: qkv[pl.ds(base, WIN), pl.ds(D1 + part.start, part.size)],
            lambda part: qkv[pl.ds(base, WIN), pl.ds(2 * D1 + part.start, part.size)],
            D1,
            key_bias(jr, ROWS, a, ROWS * lat_n),
            put,
        )

    s = col(64)
    r = div(s, 10)
    rest = s - r * 10
    lev = div(rest, 5)
    first = jnp.where(r < WLAT, (r * 2 + lev) * WLON + rest - lev * 5, -1)
    pick_first = onehot(first, lanes)
    returns = []

    def give_back(jr):
        part = pl.ds(jr * 64, 64)
        back_out[part, :] = mm_nt(pick_first, mixed[:, jr * 256 : (jr + 1) * 256]).astype(BF)
        copy = remote(11 + jr, back_out.at[part], back_in.at[part], lat, left)
        copy.start()
        returns.append(copy)

    project(0, gather(1, 1))
    attend(0, 1, 1)
    moves[0].wait_recv()
    project(1, gather(1, 0))
    attend(1, 1, 0)
    give_back(1)

    arrived(*moves[1:])
    for at, jr in ((2, 0), (3, 2)):
        project(at, gather(jr, 0))
        attend(at, jr, 0)
        give_back(jr)

    project(4, gather(0, 1))
    project(5, gather(2, 1))
    attend(4, 0, 1)
    attend(5, 2, 1)

    for load in loads[5:12]:
        load.wait()
    a2 = shifts[1, 0]
    b2 = shifts[1, 1]

    def message(i, there, d_lat, d_lon):
        part = pl.ds(i * 64, 64)
        return remote(i + 14, send2.at[part], ext2.at[part], there + d_lat, d_lon)

    downs = [message(i, lat, 1, lon) for i in (0, 2)] + [message(5, lat, 1, right)]
    ups = [message(i, lat, -1, lon) for i in (1, 3)] + [message(6, lat, -1, right)]
    right2 = message(4, lat, 0, right)
    goes_up = even & has_up
    from_below = odd & has_down

    s = col(64)
    rl6 = div(s, 6)
    lines = rl6 * 6 + (s - rl6 * 6)
    rl5 = div(s, 5)
    columns = rl5 * 6 + (s - rl5 * 5) + 1
    top = jnp.where(s < 60, lines, -1)
    bottom = jnp.where(s < 60, lines + 12, -1)
    aside = jnp.where(s < 60, columns, -1)
    aside_bottom = jnp.where(s < 50, columns + 12, -1)
    aside_top = jnp.where(s < 50, columns, -1)

    coarse = []
    for h in range(2):
        if h == 1:
            for copy in returns:
                copy.wait_recv()
        part = slice(h * HALF, (h + 1) * HALF)
        own = mm_nt(sel_back[part, 0 : 6 * 256], mixed[...])
        if h == 1:
            own = own + mm(sel_back[part, 6 * 256 :], back_in[...])
        attended = (resid[part] + mm(own.astype(BF), w_out[...])).astype(BF)
        total = attended.astype(F32)
        x = norm(total, gain_mlp[...])
        y = jax.nn.gelu(mm(x, w_up[...])).astype(BF)
        total = (total + mm(y, w_down[...])).astype(BF).astype(F32)
        acc[part] = total
        merged = jnp.concatenate(
            [total[k * HALF2 : (k + 1) * HALF2] for k in range(4)], axis=1
        )
        merged = mm(norm(merged, gain_merge[...]), w_merge[...]).astype(BF).astype(F32)
        coarse.append(merged)
        normed = norm(merged, gain_coarse[...])
        norm2[h] = normed.astype(F32)
        if h == 0:
            pick = jnp.concatenate([bottom, top], axis=0)
            send2[0:128] = mm(onehot(pick, row(HALF2)), normed).astype(BF)
        else:
            pick = jnp.concatenate([bottom, top, aside, aside_bottom, aside_top], axis=0)
            send2[128:448] = mm(onehot(pick, row(HALF2)), normed).astype(BF)
            right2.start()

        @pl.when(has_down)
        def _():
            for copy in downs[h : 2 * h + 1]:
                copy.start()

        @pl.when(goes_up)
        def _():
            for copy in ups[h : 2 * h + 1]:
                copy.start()


    c = sc - b2
    for w in range(2):
        r = sr + WLAT * w - a2
        inside = (r >= 0) & (r < ROWS2)
        right_half = jnp.where(c >= 6, 1, 0)
        place = (r * 2 + sl) * 6 + c - right_half * 6
        for h in range(2):
            target = jnp.where(inside & (c >= 0) & (right_half == h), place, -1)
            sel2_own[w, h] = onehot(target, row(HALF2))
        beyond = jnp.where(r < 0, r + REACH, r - ROWS2)
        beyond = jnp.where(beyond < REACH, beyond, -1000)
        line = jnp.where(r < 0, 0, 64) + right_half * 128 + (beyond * 2 + sl) * 6 + c - right_half * 6
        corner = jnp.where(r < 0, 320, 384) + (beyond * 2 + sl) * 5 + c + REACH
        aside = 256 + (r * 2 + sl) * 5 + c + REACH
        target = jnp.where(
            inside, jnp.where(c < 0, aside, -1), jnp.where(c < 0, corner, line)
        )
        sel2[w * WIN : (w + 1) * WIN, :] = onehot(target, row(448))

    def collect(w):
        x = mm(sel2[w * WIN : (w + 1) * WIN, :], ext2[...])
        for h in range(2):
            x = x + mm(sel2_own[w, h], norm2[h].astype(BF))
        return x.astype(BF)

    lanes = row(held)
    lanes = jnp.where(lanes < MAIN, lanes, MAIN + (lanes & 15))
    pick_here, pick_there = [], []
    for h in range(2):
        rr, ll, cc = own_parts(col(HALF2) + h * HALF2)
        up = rr + a2
        over = cc + b2
        here = (up < WLAT) & (over < COLS2)
        pick_here.append(onehot(jnp.where(here, (up * 2 + ll) * WLON + over, -1), lanes))
        below = up >= WLAT
        up = jnp.where(below, up - WLAT, up)
        target = jnp.where(
            over < COLS2,
            jnp.where(below, (up * 2 + ll) * WLON + over, -1),
            jnp.where(below, 192, 128) + (up * 2 + ll) * REACH + over - COLS2,
        )
        pick_there.append(onehot(target, row(256)))
    s = col(192)
    target = jnp.where(s < 128, s, jnp.concatenate([jnp.zeros((128, 1), I32), first], axis=0))
    pick_out = onehot(target, lanes)

    loads[12].wait()
    right2.wait_recv()

    @pl.when(has_up)
    def _():
        for copy in downs:
            copy.wait_recv()

    @pl.when(from_below)
    def _():
        for copy in ups:
            copy.wait_recv()

    x2[0:WIN] = collect(0)

    @pl.when(even)
    def _():
        for i in range(3):
            part = slice(i * D2, (i + 1) * D2)
            qkv2[0:WIN, part] = mm(x2[0:WIN], w_qkv2[:, part]).astype(BF)

    @pl.when(odd)
    def _():
        x2[WIN:] = collect(1)
        for i in range(3):
            part = slice(i * D2, (i + 1) * D2)
            qkv2[:, part] = mm(x2[...], w_qkv2[:, part]).astype(BF)

    def attend2(w):
        base = w * WIN

        def put(r0, rn, l0, ln, value):
            mixed2[r0 : r0 + rn, l0 : l0 + ln] = value.astype(BF)

        window_attend(
            lambda rows, part: qkv2[pl.ds(base + rows.start, rows.size), part],
            lambda part: qkv2[pl.ds(base, WIN), pl.ds(D2 + part.start, part.size)],
            lambda part: qkv2[pl.ds(base, WIN), pl.ds(2 * D2 + part.start, part.size)],
            D2,
            key_bias(w, ROWS2, a2, ROWS2 * lat_n),
            put,
        )

    attend2(0)
    back2_out[...] = mm_nt(pick_out, mixed2[...]).astype(BF)
    left2 = remote(5, back2_out.at[128:192], back2_in.at[128:192], lat, left)
    up2 = remote(6, back2_out.at[0:128], back2_in.at[0:128], lat - 1, lon)
    up_left2 = remote(7, back2_out.at[128:192], back2_in.at[192:256], lat - 1, left)
    last_left2 = remote(8, last_out, back2_in.at[192:256], lat, left)

    @pl.when(odd)
    def _():
        up2.start()
        up_left2.start()

    left2.start()
    own2 = [mm_nt(pick, mixed2[...]) for pick in pick_here]

    @pl.when(odd)
    def _():
        attend2(1)
        leaving = mm_nt(pick_out, mixed2[...]).astype(BF)
        back2_in[0:128] = leaving[0:128]
        last_out[...] = leaving[128:192]
        last_left2.start()

    loads[13].wait()
    loads[14].wait()

    @pl.when(even)
    def _():
        up2.wait_recv()

    for h in range(2):
        if h == 0:
            other = mm(pick_there[0][:, 0:128], back2_in[0:128])
        else:
            left2.wait_recv()

            @pl.when(even)
            def _():
                up_left2.wait_recv()

            @pl.when(odd)
            def _():
                last_left2.wait_recv()

            other = mm(pick_there[1], back2_in[...])
        coarse_out = (coarse[h] + mm((own2[h] + other).astype(BF), w_out2[...])).astype(BF)
        for k in range(4):
            at = h * HALF + k * HALF2
            spread = mm(coarse_out, w_expand[:, k * D1 : (k + 1) * D1])
            acc[at : at + HALF2] = acc[at : at + HALF2] + spread

    t = col(TOK)
    lev = div(t, ROWS * COLS)
    rest = t - lev * (ROWS * COLS)
    r = div(rest, COLS)
    c = rest - r * COLS
    half = jnp.where(c >= COLS // 2, 1, 0)
    quadrant = (c & 1) * 2 + (r & 1)
    target = half * HALF + quadrant * HALF2 + ((r >> 1) * 2 + lev) * 6 + (c >> 1) - half * 6
    final = mm(onehot(target, row(TOK)), acc[...].astype(BF))
    out[...] = final.reshape(2, ROWS, COLS, D1).astype(BF)

    sent(*moves)
    right2.wait_send()
    left2.wait_send()

    @pl.when(has_down)
    def _():
        for copy in downs:
            copy.wait_send()

    @pl.when(goes_up)
    def _():
        for copy in ups:
            copy.wait_send()

    @pl.when(odd)
    def _():
        up2.wait_send()
        up_left2.wait_send()
        last_left2.wait_send()

    for copy in returns:
        copy.wait_send()


def local(
    tokens, land_mask, land_embed, shifts, gain_attn, w_qkv_fine, w_out_fine, gain_mlp, w_up_fine,
    w_down_fine, gain_merge, w_merge, gain_coarse, w_qkv_coarse, w_out_coarse, w_expand,
):
    vmem = pl.BlockSpec(memory_space=pltpu.VMEM)
    hbm = pl.BlockSpec(memory_space=pl.ANY)
    smem = pl.BlockSpec(memory_space=pltpu.SMEM)
    weights = [
        w_qkv_fine, w_out_fine, w_up_fine, w_down_fine, w_merge, w_qkv_coarse, w_out_coarse, w_expand,
    ]
    V = pltpu.VMEM
    return pl.pallas_call(
        kernel,
        out_shape=pltpu.VMEM(tokens.shape, BF),
        in_specs=[hbm, hbm, hbm, smem] + [hbm] * 12,
        out_specs=vmem,
        scratch_shapes=[
            V(tokens.shape, BF), V(land_mask.shape, I32), V((1, D1), F32), V((1, D1), F32),
            V((1, D1), F32), V((1, 4 * D1), F32), V((1, D2), F32),
        ]
        + [V(w.shape, BF) for w in weights]
        + [
            V((ROWS, LINE, D1), BF),
            V((ROWS + 2 * REACH + 1, LINE, D1), BF),
            V((256, D1), BF),
            V((256, D1), BF),
            V((2, WIN, SPAN), BF),
            V((3, WIN, 256), BF),
            V((TOK, 6 * 256 + 192), BF),
            V((6 * WIN, 3 * D1), BF),
            V((D1, 6 * 256), BF),
            V((192, D1), BF),
            V((192, D1), BF),
            V((TOK, D1), F32),
            V((TOK, D1), F32),
            V((2, HALF2, D2), F32),
            V((448, D2), BF),
            V((448, D2), BF),
            V((2 * WIN, 448), BF),
            V((2, 2, WIN, HALF2), BF),
            V((2 * WIN, D2), BF),
            V((2 * WIN, 3 * D2), BF),
            V((D2, held), BF),
            V((192, D2), BF),
            V((64, D2), BF),
            V((256, D2), BF),
            pltpu.SemaphoreType.DMA((15,)),
            pltpu.SemaphoreType.DMA((21,)),
            pltpu.SemaphoreType.DMA((21,)),
        ],
        compiler_params=pltpu.CompilerParams(
            collective_id=0, has_side_effects=True, vmem_limit_bytes=56 * 1024 * 1024
        ),
    )(
        tokens, land_mask, land_embed.reshape(1, D1), shifts, gain_attn.reshape(1, D1),
        gain_mlp.reshape(1, D1), gain_merge.reshape(1, 4 * D1), gain_coarse.reshape(1, D2), *weights,
    )


def solution(mesh):
    spec = P(None, "lat", "lon", None)
    return jax.shard_map(
        local,
        mesh=mesh,
        in_specs=(spec, P("lat", "lon")) + (P(),) * 14,
        out_specs=spec,
        check_vma=False,
    )
```

```python
import jax
import jax.numpy as jnp
from jax import lax
from jax.experimental import pallas as pl
from jax.experimental.pallas import tpu as pltpu
from jax.sharding import PartitionSpec as P

HEAD = 64
WLAT = 6
WLON = 12
WIN = 2 * WLAT * WLON
REACH = 5
MAIN = 128
REST = WIN - MAIN

D1 = 512
D2 = 1024
FF1 = 2048
held = MAIN + REST * (D1 // HEAD)
ROWS, COLS = 12, 24
ROWS2, COLS2 = 6, 12
TOK = 2 * ROWS * COLS
TOK2 = 2 * ROWS2 * COLS2
HALF, HALF2 = TOK // 2, TOK2 // 2
LINE = 2 * COLS
SPAN = (WLAT + REACH) * LINE

EPSILON = 1e-05
NEGATIVE = -1e30
SCALE = HEAD ** (-0.5) * 1.4426950408889634
BF = jnp.bfloat16
F32 = jnp.float32
I32 = jnp.int32
MESH = pl.DeviceIdType.MESH


def div(x, d):
    return (x * ((1 << 20) // d + 1)) >> 20


def col(n):
    return lax.broadcasted_iota(I32, (n, 1), 0)


def row(n):
    return lax.broadcasted_iota(I32, (1, n), 1)


def onehot(target, lanes):
    return jnp.where(lanes == target, 1.0, 0.0).astype(BF)


def mm(a, b):
    return lax.dot_general(a, b, (((1,), (0,)), ((), ())), preferred_element_type=F32)


def mm_nt(a, b):
    return lax.dot_general(a, b, (((1,), (1,)), ((), ())), preferred_element_type=F32)


def mm_tn(a, b):
    return lax.dot_general(a, b, (((0,), (0,)), ((), ())), preferred_element_type=F32)


def norm(x, gain):
    mean = jnp.mean(x, axis=-1, keepdims=True)
    center = x - mean
    var = jnp.mean(center * center, axis=-1, keepdims=True)
    return (center * lax.rsqrt(var + EPSILON) * gain).astype(BF)


def slot_parts(s):
    r = div(s, 24)
    rest = s - r * 24
    lev = div(rest, 12)
    return r, lev, rest - lev * 12


def own_parts(t):
    half = div(t, HALF2)
    rest = t - half * HALF2
    rl = div(rest, COLS2 // 2)
    return rl >> 1, rl & 1, half * (COLS2 // 2) + rest - rl * (COLS2 // 2)


def soften(s, bias):
    s = s + bias
    top = jnp.max(s, axis=0, keepdims=True)
    p = jnp.exp2(s * SCALE - top * SCALE)
    total = jnp.sum(p, axis=0, keepdims=True)
    return p.astype(BF), 1.0 / total


def window_attend(q_of, k_of, v_of, width, bias, put):
    heads = width // HEAD
    pairs = heads // 2
    lane = row(2 * HEAD)
    every = pl.ds(0, width)
    parts = [pl.ds(i * 2 * HEAD, 2 * HEAD) for i in range(pairs)]
    spread = REST * heads
    tiled = jnp.concatenate([q_of(pl.ds(MAIN, REST), every)] * heads, axis=0)
    own = (col(spread) >> 4) == (row(width) >> 6)
    tiled = jnp.where(own, tiled, jnp.zeros_like(tiled))
    scores = [mm_nt(k_of(every), tiled)]
    for part in parts:
        q = q_of(pl.ds(0, MAIN), part)
        zero = jnp.zeros_like(q)
        both = jnp.concatenate(
            [jnp.where(lane < HEAD, q, zero), jnp.where(lane < HEAD, zero, q)], axis=0
        )
        scores.append(mm_nt(k_of(part), both))
    weights = [soften(x, bias) for x in scores]
    results = [mm_tn(v_of(part), p) for part, (p, _) in zip([every] + parts, weights)]
    o = results[0] * weights[0][1]
    o = jnp.where((col(width) >> 6) == (row(spread) >> 4), o, 0.0)
    put(0, width, MAIN, spread, o)
    for i in range(pairs):
        o = results[i + 1] * weights[i + 1][1]
        put(i * 2 * HEAD, HEAD, 0, MAIN, o[:HEAD, :MAIN])
        put(i * 2 * HEAD + HEAD, HEAD, 0, MAIN, o[HEAD:, MAIN:])


def kernel(
    tokens_h, mask_h, embed_h, shifts, gain_attn_h, gain_mlp_h, gain_merge_h, gain_coarse_h,
    w_qkv_h, w_out_h, w_up_h, w_down_h, w_merge_h, w_qkv2_h, w_out2_h, w_expand_h,
    out,
    tokens, mask, embed, gain_attn, gain_mlp, gain_merge, gain_coarse,
    w_qkv, w_out, w_up, w_down, w_merge, w_qkv2, w_out2, w_expand,
    inputs, ext, side_out, side, sel_own, sel_side, sel_back, qkv, mixed, back_out, back_in,
    resid, acc,
    norm2, send2, ext2, sel2, sel2_own, x2, qkv2, mixed2, back2_out, last_out, back2_in, sel_out,
    w_sem, send_sem, recv_sem,
):
    lat = lax.axis_index("lat")
    lon = lax.axis_index("lon")
    lat_n = lax.axis_size("lat")
    lon_n = lax.axis_size("lon")
    right = lax.rem(lon + 1, lon_n)
    left = lax.rem(lon + lon_n - 1, lon_n)
    has_up = lat > 0
    has_down = lat < lat_n - 1
    odd = lax.rem(lat, 2) == 1
    even = jnp.logical_not(odd)

    barrier = pltpu.get_barrier_semaphore()

    def greet(a, b):
        pl.semaphore_signal(barrier, inc=1, device_id=(a, b), device_id_type=MESH)

    greet(lat, left)
    greet(lat, right)

    @pl.when(has_up)
    def _():
        for b in (left, lon, right):
            greet(lat - 1, b)

    @pl.when(has_down)
    def _():
        for b in (left, lon, right):
            greet(lat + 1, b)

    loads = []
    for i, (src, dst) in enumerate(
        [
            (tokens_h, tokens), (mask_h, mask), (embed_h, embed), (gain_attn_h, gain_attn),
            (w_qkv_h, w_qkv), (gain_mlp_h, gain_mlp), (gain_merge_h, gain_merge),
            (gain_coarse_h, gain_coarse), (w_out_h, w_out), (w_up_h, w_up), (w_down_h, w_down),
            (w_merge_h, w_merge), (w_qkv2_h, w_qkv2), (w_out2_h, w_out2), (w_expand_h, w_expand),
        ]
    ):
        load = pltpu.make_async_copy(src, dst, w_sem.at[i])
        load.start()
        loads.append(load)

    def remote(i, src, dst, a, b):
        return pltpu.make_async_remote_copy(
            src_ref=src, dst_ref=dst, send_sem=send_sem.at[i], recv_sem=recv_sem.at[i],
            device_id=(a, b), device_id_type=MESH,
        )

    for load in loads[:4]:
        load.wait()
    eye = col(COLS) == row(COLS)
    add = embed[...]
    gain = gain_attn[...]
    lands = [
        jnp.sum(jnp.where(eye, mask[r : r + 1, :].astype(F32), 0.0), axis=1, keepdims=True)
        for r in range(ROWS)
    ]
    for group in range(0, ROWS, 4):
        lines = []
        for r in range(group, group + 4):
            shift = lands[r] * add
            lines += [tokens[0, r].astype(F32) + shift, tokens[1, r].astype(F32) + shift]
        x = jnp.concatenate(lines, axis=0).astype(BF)
        inputs[group : group + 4] = x.reshape(4, LINE, D1)
        x = norm(x.astype(F32), gain)
        ext[REACH + group : REACH + group + 4] = x.reshape(4, LINE, D1)

    s = col(256)
    part = jnp.where(s < 128, 0, jnp.where(s < 192, 1, 2))
    within = s - jnp.where(part == 0, 0, jnp.where(part == 1, 128, 192))
    r = div(within, 10)
    rest = within - r * 10
    lev = div(rest, 5)
    c = rest - lev * 5
    r = r + jnp.where(part == 1, ROWS - REACH, 0)
    target = jnp.where(r < ROWS, r * LINE + lev * COLS + c + (COLS - REACH), -1)
    own = ext[REACH : REACH + ROWS].reshape(TOK, D1)
    side_out[...] = mm(onehot(target, row(TOK)), own).astype(BF)

    @pl.when(jnp.logical_not(has_up))
    def _():
        for at in (0, 128, 320):
            ext2[at : at + 64] = jnp.zeros((64, D2), BF)

    @pl.when(even | jnp.logical_not(has_down))
    def _():
        for at in (64, 192, 384):
            ext2[at : at + 64] = jnp.zeros((64, D2), BF)

    ext[2 * REACH + ROWS] = jnp.zeros((LINE, D1), BF)

    @pl.when(jnp.logical_not(has_up))
    def _():
        ext[0:REACH] = jnp.zeros((REACH, LINE, D1), BF)
        side[128:192] = jnp.zeros((64, D1), BF)

    @pl.when(jnp.logical_not(has_down))
    def _():
        ext[REACH + ROWS : 2 * REACH + ROWS] = jnp.zeros((REACH, LINE, D1), BF)
        side[192:256] = jnp.zeros((64, D1), BF)

    pl.semaphore_wait(
        barrier, 2 + jnp.where(has_up, 3, 0) + jnp.where(has_down, 3, 0)
    )

    go_right = remote(0, side_out.at[0:128], side.at[0:128], lat, right)
    go_down = remote(1, ext.at[ROWS : ROWS + REACH], ext.at[0:REACH], lat + 1, lon)
    go_up = remote(2, ext.at[REACH : 2 * REACH], ext.at[REACH + ROWS : 2 * REACH + ROWS], lat - 1, lon)
    go_down_right = remote(3, side_out.at[128:192], side.at[128:192], lat + 1, right)
    go_up_right = remote(4, side_out.at[192:256], side.at[192:256], lat - 1, right)

    def exchange(r_, d_, u_, dr_, ur_):
        r_.start()

        @pl.when(has_down)
        def _():
            d_.start()
            dr_.start()

        @pl.when(has_up)
        def _():
            u_.start()
            ur_.start()

    def arrived(d_, u_, dr_, ur_):
        @pl.when(has_up)
        def _():
            d_.wait_recv()
            dr_.wait_recv()

        @pl.when(has_down)
        def _():
            u_.wait_recv()
            ur_.wait_recv()

    def sent(r_, d_, u_, dr_, ur_):
        r_.wait_send()

        @pl.when(has_down)
        def _():
            d_.wait_send()
            dr_.wait_send()

        @pl.when(has_up)
        def _():
            u_.wait_send()
            ur_.wait_send()

    moves = (go_right, go_down, go_up, go_down_right, go_up_right)
    exchange(*moves)

    a = shifts[0, 0]
    b = shifts[0, 1]

    sr, sl, sc = slot_parts(col(WIN))
    for jc in range(2):
        c = sc + (WLON * jc) - b
        target = jnp.where(c >= 0, (sr + REACH - a) * LINE + sl * COLS + c, -1)
        sel_own[jc] = onehot(target, row(SPAN))
    c = sc - b
    for jr in range(3):
        r = sr + (WLAT * jr) - a
        place = jnp.where(
            r < 0, 128 + (r + REACH) * 10, jnp.where(r < ROWS, r * 10, 192 + (r - ROWS) * 10)
        )
        target = jnp.where(c < 0, place + sl * 5 + c + REACH, -1)
        sel_side[jr] = onehot(target, row(256))

    q = col(TOK)
    half = div(q, HALF)
    k = div(q - half * HALF, HALF2)
    cr, clev, cc = own_parts(q - half * HALF - k * HALF2)
    fr = cr * 2 + (k & 1)
    fc = (cc + half * (COLS2 // 2)) * 2 + (k >> 1)
    resid[...] = mm(
        onehot(fr * LINE + clev * COLS + fc, row(TOK)), inputs[...].reshape(TOK, D1)
    )
    up = fr + a
    jr = div(up, WLAT)
    over = fc + b
    jc = div(over, WLON)
    slot = ((up - jr * WLAT) * 2 + clev) * WLON + (over - jc * WLON)
    lanes = row(256)
    lanes = jnp.where(lanes < MAIN, lanes, MAIN + (lanes & 15))
    for w in range(6):
        target = jnp.where((jr == w % 3) & (jc == w // 3), slot, -1)
        sel_back[:, w * 256 : (w + 1) * 256] = onehot(target, lanes)
    target = jnp.where(
        jc == 2, jr * 64 + ((up - jr * WLAT) * 2 + clev) * REACH + over - COLS, -1
    )
    sel_back[:, 6 * 256 :] = onehot(target, row(192))

    loads[4].wait()

    def key_bias(jr, rows, a, lat_rows):
        r = sr + jr * WLAT - a + lat * rows
        return jnp.where((r >= 0) & (r < lat_rows), 0.0, NEGATIVE).astype(F32)

    def project(at, *xs):
        x = jnp.concatenate(xs, axis=0)
        qkv[at * WIN : (at + len(xs)) * WIN] = mm(x, w_qkv[...]).astype(BF)

    def gather(jr, jc):
        x = mm(sel_own[jc], ext[WLAT * jr : WLAT * jr + WLAT + REACH].reshape(SPAN, D1))
        if jc == 0:
            n = 128 if jr == 1 else 256
            x = x + mm(sel_side[jr, :, 0:n], side[0:n])
        return x.astype(BF)

    def attend(at, jr, jc):
        base = at * WIN
        lane0 = (jc * 3 + jr) * 256

        def put(r0, rn, l0, ln, value):
            mixed[r0 : r0 + rn, lane0 + l0 : lane0 + l0 + ln] = value.astype(BF)

        window_attend(
            lambda rows, part: qkv[pl.ds(base + rows.start, rows.size), part],
            lambda part: qkv[pl.ds(base, WIN), pl.ds(D1 + part.start, part.size)],
            lambda part: qkv[pl.ds(base, WIN), pl.ds(2 * D1 + part.start, part.size)],
            D1,
            key_bias(jr, ROWS, a, ROWS * lat_n),
            put,
        )

    s = col(64)
    r = div(s, 10)
    rest = s - r * 10
    lev = div(rest, 5)
    first = jnp.where(r < WLAT, (r * 2 + lev) * WLON + rest - lev * 5, -1)
    pick_first = onehot(first, lanes)
    returns = []

    def give_back(jr):
        part = pl.ds(jr * 64, 64)
        back_out[part, :] = mm_nt(pick_first, mixed[:, jr * 256 : (jr + 1) * 256]).astype(BF)
        copy = remote(11 + jr, back_out.at[part], back_in.at[part], lat, left)
        copy.start()
        returns.append(copy)

    project(0, gather(1, 1))
    attend(0, 1, 1)
    moves[0].wait_recv()
    project(1, gather(1, 0))
    attend(1, 1, 0)
    give_back(1)

    arrived(*moves[1:])
    project(2, gather(0, 0), gather(2, 0))
    for at, jr in ((2, 0), (3, 2)):
        attend(at, jr, 0)
        give_back(jr)

    project(4, gather(0, 1), gather(2, 1))
    attend(4, 0, 1)
    attend(5, 2, 1)

    for load in loads[5:12]:
        load.wait()
    a2 = shifts[1, 0]
    b2 = shifts[1, 1]

    def message(i, there, d_lat, d_lon):
        part = pl.ds(i * 64, 64)
        return remote(i + 14, send2.at[part], ext2.at[part], there + d_lat, d_lon)

    downs = [message(i, lat, 1, lon) for i in (0, 2)] + [message(5, lat, 1, right)]
    ups = [message(i, lat, -1, lon) for i in (1, 3)] + [message(6, lat, -1, right)]
    right2 = message(4, lat, 0, right)
    goes_up = even & has_up
    from_below = odd & has_down

    s = col(64)
    rl6 = div(s, 6)
    lines = rl6 * 6 + (s - rl6 * 6)
    rl5 = div(s, 5)
    columns = rl5 * 6 + (s - rl5 * 5) + 1
    top = jnp.where(s < 60, lines, -1)
    bottom = jnp.where(s < 60, lines + 12, -1)
    aside = jnp.where(s < 60, columns, -1)
    aside_bottom = jnp.where(s < 50, columns + 12, -1)
    aside_top = jnp.where(s < 50, columns, -1)

    coarse = []
    for h in range(2):
        if h == 1:
            for copy in returns:
                copy.wait_recv()
        part = slice(h * HALF, (h + 1) * HALF)
        own = mm_nt(sel_back[part, 0 : 6 * 256], mixed[...])
        if h == 1:
            own = own + mm(sel_back[part, 6 * 256 :], back_in[...])
        attended = (resid[part] + mm(own.astype(BF), w_out[...])).astype(BF)
        total = attended.astype(F32)
        x = norm(total, gain_mlp[...])
        y = jax.nn.gelu(mm(x, w_up[...])).astype(BF)
        total = (total + mm(y, w_down[...])).astype(BF).astype(F32)
        acc[part] = total
        merged = jnp.concatenate(
            [total[k * HALF2 : (k + 1) * HALF2] for k in range(4)], axis=1
        )
        merged = mm(norm(merged, gain_merge[...]), w_merge[...]).astype(BF).astype(F32)
        coarse.append(merged)
        normed = norm(merged, gain_coarse[...])
        norm2[h] = normed.astype(F32)
        if h == 0:
            pick = jnp.concatenate([bottom, top], axis=0)
            send2[0:128] = mm(onehot(pick, row(HALF2)), normed).astype(BF)
        else:
            pick = jnp.concatenate([bottom, top, aside, aside_bottom, aside_top], axis=0)
            send2[128:448] = mm(onehot(pick, row(HALF2)), normed).astype(BF)
            right2.start()

        @pl.when(has_down)
        def _():
            for copy in downs[h : 2 * h + 1]:
                copy.start()

        @pl.when(goes_up)
        def _():
            for copy in ups[h : 2 * h + 1]:
                copy.start()


    c = sc - b2
    for w in range(2):
        r = sr + WLAT * w - a2
        inside = (r >= 0) & (r < ROWS2)
        right_half = jnp.where(c >= 6, 1, 0)
        place = (r * 2 + sl) * 6 + c - right_half * 6
        for h in range(2):
            target = jnp.where(inside & (c >= 0) & (right_half == h), place, -1)
            sel2_own[w, h] = onehot(target, row(HALF2))
        beyond = jnp.where(r < 0, r + REACH, r - ROWS2)
        beyond = jnp.where(beyond < REACH, beyond, -1000)
        line = jnp.where(r < 0, 0, 64) + right_half * 128 + (beyond * 2 + sl) * 6 + c - right_half * 6
        corner = jnp.where(r < 0, 320, 384) + (beyond * 2 + sl) * 5 + c + REACH
        aside = 256 + (r * 2 + sl) * 5 + c + REACH
        target = jnp.where(
            inside, jnp.where(c < 0, aside, -1), jnp.where(c < 0, corner, line)
        )
        sel2[w * WIN : (w + 1) * WIN, :] = onehot(target, row(448))

    def collect(w):
        x = mm(sel2[w * WIN : (w + 1) * WIN, :], ext2[...])
        for h in range(2):
            x = x + mm(sel2_own[w, h], norm2[h].astype(BF))
        return x.astype(BF)

    lanes = row(held)
    lanes = jnp.where(lanes < MAIN, lanes, MAIN + (lanes & 15))
    pick_here, pick_there = [], []
    for h in range(2):
        rr, ll, cc = own_parts(col(HALF2) + h * HALF2)
        up = rr + a2
        over = cc + b2
        here = (up < WLAT) & (over < COLS2)
        pick_here.append(onehot(jnp.where(here, (up * 2 + ll) * WLON + over, -1), lanes))
        below = up >= WLAT
        up = jnp.where(below, up - WLAT, up)
        target = jnp.where(
            over < COLS2,
            jnp.where(below, (up * 2 + ll) * WLON + over, -1),
            jnp.where(below, 192, 128) + (up * 2 + ll) * REACH + over - COLS2,
        )
        pick_there.append(onehot(target, row(256)))
    s = col(192)
    target = jnp.where(s < 128, s, jnp.concatenate([jnp.zeros((128, 1), I32), first], axis=0))
    pick_out = onehot(target, lanes)

    loads[12].wait()
    right2.wait_recv()

    @pl.when(has_up)
    def _():
        for copy in downs:
            copy.wait_recv()

    @pl.when(from_below)
    def _():
        for copy in ups:
            copy.wait_recv()

    x2[0:WIN] = collect(0)

    @pl.when(even)
    def _():
        for i in range(3):
            part = slice(i * D2, (i + 1) * D2)
            qkv2[0:WIN, part] = mm(x2[0:WIN], w_qkv2[:, part]).astype(BF)

    @pl.when(odd)
    def _():
        x2[WIN:] = collect(1)
        for i in range(3):
            part = slice(i * D2, (i + 1) * D2)
            qkv2[:, part] = mm(x2[...], w_qkv2[:, part]).astype(BF)

    def attend2(w, g):
        base = w * WIN

        def put(r0, rn, l0, ln, value):
            mixed2[g * D1 + r0 : g * D1 + r0 + rn, l0 : l0 + ln] = value.astype(BF)

        def at(block, part):
            return pl.ds(block * D2 + g * D1 + part.start, part.size)

        window_attend(
            lambda rows, part: qkv2[pl.ds(base + rows.start, rows.size), at(0, part)],
            lambda part: qkv2[pl.ds(base, WIN), at(1, part)],
            lambda part: qkv2[pl.ds(base, WIN), at(2, part)],
            D1,
            key_bias(w, ROWS2, a2, ROWS2 * lat_n),
            put,
        )
        return mm_nt(pick_out, mixed2[g * D1 : (g + 1) * D1, :]).astype(BF)

    left2, up2, up_left2, last_left2 = [], [], [], []
    for g in range(2):
        back2_out[g] = attend2(0, g)
        column = back2_out.at[g, 128:192]
        left2.append(remote(5 + g, column, back2_in.at[g, 128:192], lat, left))
        up2.append(remote(7 + g, back2_out.at[g, 0:128], back2_in.at[g, 0:128], lat - 1, lon))
        up_left2.append(remote(9 + g, column, back2_in.at[g, 192:256], lat - 1, left))
        last_left2.append(remote(21 + g, last_out.at[g], back2_in.at[g, 192:256], lat, left))

        @pl.when(odd)
        def _():
            up2[g].start()
            up_left2[g].start()

        left2[g].start()

    own2 = [mm_nt(pick, mixed2[...]) for pick in pick_here]

    @pl.when(odd)
    def _():
        for g in range(2):
            leaving = attend2(1, g)
            back2_in[g, 0:128] = leaving[0:128]
            last_out[g] = leaving[128:192]
            last_left2[g].start()

    t = col(TOK)
    lev = div(t, ROWS * COLS)
    rest = t - lev * (ROWS * COLS)
    r = div(rest, COLS)
    c = rest - r * COLS
    side_of = jnp.where(c >= COLS // 2, 1, 0)
    quadrant = (c & 1) * 2 + (r & 1)
    target = quadrant * HALF2 + ((r >> 1) * 2 + lev) * 6 + (c >> 1) - side_of * 6
    for h in range(2):
        sel_out[h] = onehot(jnp.where(side_of == h, target, -1), row(HALF))

    loads[13].wait()
    loads[14].wait()

    @pl.when(even)
    def _():
        for copy in up2:
            copy.wait_recv()

    def returned(h, rows):
        pick = pick_there[h][:, 0:rows]
        return jnp.concatenate([mm(pick, back2_in[g, 0:rows]) for g in range(2)], axis=1)

    final = None
    for h in range(2):
        if h == 0:
            other = returned(0, 128)
        else:
            for g in range(2):
                left2[g].wait_recv()

            @pl.when(even)
            def _():
                for copy in up_left2:
                    copy.wait_recv()

            @pl.when(odd)
            def _():
                for copy in last_left2:
                    copy.wait_recv()

            other = returned(1, 256)
        coarse_out = (coarse[h] + mm((own2[h] + other).astype(BF), w_out2[...])).astype(BF)
        spread = mm(coarse_out, w_expand[...])
        blended = jnp.concatenate(
            [
                acc[h * HALF + k * HALF2 : h * HALF + (k + 1) * HALF2]
                + spread[:, k * D1 : (k + 1) * D1]
                for k in range(4)
            ],
            axis=0,
        )
        placed = mm(sel_out[h], blended.astype(BF))
        final = placed if h == 0 else final + placed
    out[...] = final.reshape(2, ROWS, COLS, D1).astype(BF)

    sent(*moves)
    right2.wait_send()
    for copy in left2:
        copy.wait_send()

    @pl.when(has_down)
    def _():
        for copy in downs:
            copy.wait_send()

    @pl.when(goes_up)
    def _():
        for copy in ups:
            copy.wait_send()

    @pl.when(odd)
    def _():
        for copy in up2 + up_left2 + last_left2:
            copy.wait_send()

    for copy in returns:
        copy.wait_send()


def local(
    tokens, land_mask, land_embed, shifts, gain_attn, w_qkv_fine, w_out_fine, gain_mlp, w_up_fine,
    w_down_fine, gain_merge, w_merge, gain_coarse, w_qkv_coarse, w_out_coarse, w_expand,
):
    vmem = pl.BlockSpec(memory_space=pltpu.VMEM)
    hbm = pl.BlockSpec(memory_space=pl.ANY)
    smem = pl.BlockSpec(memory_space=pltpu.SMEM)
    weights = [
        w_qkv_fine, w_out_fine, w_up_fine, w_down_fine, w_merge, w_qkv_coarse, w_out_coarse, w_expand,
    ]
    V = pltpu.VMEM
    return pl.pallas_call(
        kernel,
        out_shape=pltpu.VMEM(tokens.shape, BF),
        in_specs=[hbm, hbm, hbm, smem] + [hbm] * 12,
        out_specs=vmem,
        scratch_shapes=[
            V(tokens.shape, BF), V(land_mask.shape, I32), V((1, D1), F32), V((1, D1), F32),
            V((1, D1), F32), V((1, 4 * D1), F32), V((1, D2), F32),
        ]
        + [V(w.shape, BF) for w in weights]
        + [
            V((ROWS, LINE, D1), BF),
            V((ROWS + 2 * REACH + 1, LINE, D1), BF),
            V((256, D1), BF),
            V((256, D1), BF),
            V((2, WIN, SPAN), BF),
            V((3, WIN, 256), BF),
            V((TOK, 6 * 256 + 192), BF),
            V((6 * WIN, 3 * D1), BF),
            V((D1, 6 * 256), BF),
            V((192, D1), BF),
            V((192, D1), BF),
            V((TOK, D1), F32),
            V((TOK, D1), F32),
            V((2, HALF2, D2), F32),
            V((448, D2), BF),
            V((448, D2), BF),
            V((2 * WIN, 448), BF),
            V((2, 2, WIN, HALF2), BF),
            V((2 * WIN, D2), BF),
            V((2 * WIN, 3 * D2), BF),
            V((D2, held), BF),
            V((2, 192, D1), BF),
            V((2, 64, D1), BF),
            V((2, 256, D1), BF),
            V((2, TOK, HALF), BF),
            pltpu.SemaphoreType.DMA((15,)),
            pltpu.SemaphoreType.DMA((23,)),
            pltpu.SemaphoreType.DMA((23,)),
        ],
        compiler_params=pltpu.CompilerParams(
            collective_id=0, has_side_effects=True, vmem_limit_bytes=56 * 1024 * 1024
        ),
    )(
        tokens, land_mask, land_embed.reshape(1, D1), shifts, gain_attn.reshape(1, D1),
        gain_mlp.reshape(1, D1), gain_merge.reshape(1, 4 * D1), gain_coarse.reshape(1, D2), *weights,
    )


def solution(mesh):
    spec = P(None, "lat", "lon", None)
    return jax.shard_map(
        local,
        mesh=mesh,
        in_specs=(spec, P("lat", "lon")) + (P(),) * 14,
        out_specs=spec,
        check_vma=False,
    )
```

```python
import jax
import jax.numpy as jnp
from jax import lax
from jax.experimental import pallas as pl
from jax.experimental.pallas import tpu as pltpu
from jax.sharding import PartitionSpec as P

HEAD = 64
WLAT = 6
WLON = 12
WIN = 2 * WLAT * WLON
REACH = 5
MAIN = 128
REST = WIN - MAIN

D1 = 512
D2 = 1024
FF1 = 2048
held = MAIN + REST * (D1 // HEAD)
ROWS, COLS = 12, 24
ROWS2, COLS2 = 6, 12
TOK = 2 * ROWS * COLS
TOK2 = 2 * ROWS2 * COLS2
HALF, HALF2 = TOK // 2, TOK2 // 2
LINE = 2 * COLS
SPAN = (WLAT + REACH) * LINE

EPSILON = 1e-05
NEGATIVE = -1e30
SCALE = HEAD ** (-0.5) * 1.4426950408889634
BF = jnp.bfloat16
F32 = jnp.float32
I32 = jnp.int32
MESH = pl.DeviceIdType.MESH


def div(x, d):
    return (x * ((1 << 20) // d + 1)) >> 20


def col(n):
    return lax.broadcasted_iota(I32, (n, 1), 0)


def row(n):
    return lax.broadcasted_iota(I32, (1, n), 1)


def onehot(target, lanes):
    return jnp.where(lanes == target, 1.0, 0.0).astype(BF)


def mm(a, b):
    return lax.dot_general(a, b, (((1,), (0,)), ((), ())), preferred_element_type=F32)


def mm_nt(a, b):
    return lax.dot_general(a, b, (((1,), (1,)), ((), ())), preferred_element_type=F32)


def mm_tn(a, b):
    return lax.dot_general(a, b, (((0,), (0,)), ((), ())), preferred_element_type=F32)


def norm(x, gain):
    mean = jnp.mean(x, axis=-1, keepdims=True)
    center = x - mean
    var = jnp.mean(center * center, axis=-1, keepdims=True)
    return (center * lax.rsqrt(var + EPSILON) * gain).astype(BF)


def slot_parts(s):
    r = div(s, 24)
    rest = s - r * 24
    lev = div(rest, 12)
    return r, lev, rest - lev * 12


def own_parts(t):
    half = div(t, HALF2)
    rest = t - half * HALF2
    rl = div(rest, COLS2 // 2)
    return rl >> 1, rl & 1, half * (COLS2 // 2) + rest - rl * (COLS2 // 2)


def soften(s, bias):
    s = s + bias
    top = jnp.max(s, axis=0, keepdims=True)
    p = jnp.exp2(s * SCALE - top * SCALE)
    total = jnp.sum(p, axis=0, keepdims=True)
    return p.astype(BF), 1.0 / total


def window_attend(q_of, k_of, v_of, width, bias, put):
    heads = width // HEAD
    pairs = heads // 2
    lane = row(2 * HEAD)
    every = pl.ds(0, width)
    parts = [pl.ds(i * 2 * HEAD, 2 * HEAD) for i in range(pairs)]
    spread = REST * heads
    tiled = jnp.concatenate([q_of(pl.ds(MAIN, REST), every)] * heads, axis=0)
    own = (col(spread) >> 4) == (row(width) >> 6)
    tiled = jnp.where(own, tiled, jnp.zeros_like(tiled))
    scores = [mm_nt(k_of(every), tiled)]
    for part in parts:
        q = q_of(pl.ds(0, MAIN), part)
        zero = jnp.zeros_like(q)
        both = jnp.concatenate(
            [jnp.where(lane < HEAD, q, zero), jnp.where(lane < HEAD, zero, q)], axis=0
        )
        scores.append(mm_nt(k_of(part), both))
    weights = [soften(x, bias) for x in scores]
    results = [mm_tn(v_of(part), p) for part, (p, _) in zip([every] + parts, weights)]
    o = results[0] * weights[0][1]
    o = jnp.where((col(width) >> 6) == (row(spread) >> 4), o, 0.0)
    put(0, width, MAIN, spread, o)
    for i in range(pairs):
        o = results[i + 1] * weights[i + 1][1]
        put(i * 2 * HEAD, HEAD, 0, MAIN, o[:HEAD, :MAIN])
        put(i * 2 * HEAD + HEAD, HEAD, 0, MAIN, o[HEAD:, MAIN:])


def kernel(
    tokens_h, mask_h, embed_h, shifts, gain_attn_h, gain_mlp_h, gain_merge_h, gain_coarse_h,
    w_qkv_h, w_out_h, w_up_h, w_down_h, w_merge_h, w_qkv2_h, w_out2_h, w_expand_h,
    out,
    tokens, mask, embed, gain_attn, gain_mlp, gain_merge, gain_coarse,
    w_qkv, w_out, w_up, w_down, w_merge, w_qkv2, w_out2, w_expand,
    inputs, ext, side_out, side, sel_own, sel_side, sel_back, qkv, mixed, back_out, back_in,
    resid, acc,
    norm2, send2, ext2, sel2, sel2_own, x2, qkv2, mixed2, back2_out, last_out, back2_in, sel_out,
    w_sem, send_sem, recv_sem,
):
    lat = lax.axis_index("lat")
    lon = lax.axis_index("lon")
    lat_n = lax.axis_size("lat")
    lon_n = lax.axis_size("lon")
    right = lax.rem(lon + 1, lon_n)
    left = lax.rem(lon + lon_n - 1, lon_n)
    has_up = lat > 0
    has_down = lat < lat_n - 1
    odd = lax.rem(lat, 2) == 1
    even = jnp.logical_not(odd)

    barrier = pltpu.get_barrier_semaphore()

    def greet(a, b):
        pl.semaphore_signal(barrier, inc=1, device_id=(a, b), device_id_type=MESH)

    greet(lat, left)
    greet(lat, right)

    @pl.when(has_up)
    def _():
        for b in (left, lon, right):
            greet(lat - 1, b)

    @pl.when(has_down)
    def _():
        for b in (left, lon, right):
            greet(lat + 1, b)

    loads = []
    for i, (src, dst) in enumerate(
        [
            (tokens_h, tokens), (mask_h, mask), (embed_h, embed), (gain_attn_h, gain_attn),
            (w_qkv_h, w_qkv), (gain_mlp_h, gain_mlp), (gain_merge_h, gain_merge),
            (gain_coarse_h, gain_coarse), (w_out_h, w_out), (w_up_h, w_up), (w_down_h, w_down),
            (w_merge_h, w_merge), (w_qkv2_h, w_qkv2), (w_out2_h, w_out2), (w_expand_h, w_expand),
        ]
    ):
        load = pltpu.make_async_copy(src, dst, w_sem.at[i])
        load.start()
        loads.append(load)

    def remote(i, src, dst, a, b):
        return pltpu.make_async_remote_copy(
            src_ref=src, dst_ref=dst, send_sem=send_sem.at[i], recv_sem=recv_sem.at[i],
            device_id=(a, b), device_id_type=MESH,
        )

    for load in loads[:4]:
        load.wait()
    eye = col(COLS) == row(COLS)
    add = embed[...]
    gain = gain_attn[...]
    lands = [
        jnp.sum(jnp.where(eye, mask[r : r + 1, :].astype(F32), 0.0), axis=1, keepdims=True)
        for r in range(ROWS)
    ]
    for group in range(0, ROWS, 4):
        lines = []
        for r in range(group, group + 4):
            shift = lands[r] * add
            lines += [tokens[0, r].astype(F32) + shift, tokens[1, r].astype(F32) + shift]
        x = jnp.concatenate(lines, axis=0).astype(BF)
        inputs[group : group + 4] = x.reshape(4, LINE, D1)
        x = norm(x.astype(F32), gain)
        ext[REACH + group : REACH + group + 4] = x.reshape(4, LINE, D1)

    s = col(256)
    part = jnp.where(s < 128, 0, jnp.where(s < 192, 1, 2))
    within = s - jnp.where(part == 0, 0, jnp.where(part == 1, 128, 192))
    r = div(within, 10)
    rest = within - r * 10
    lev = div(rest, 5)
    c = rest - lev * 5
    r = r + jnp.where(part == 1, ROWS - REACH, 0)
    target = jnp.where(r < ROWS, r * LINE + lev * COLS + c + (COLS - REACH), -1)
    own = ext[REACH : REACH + ROWS].reshape(TOK, D1)
    side_out[...] = mm(onehot(target, row(TOK)), own).astype(BF)

    @pl.when(jnp.logical_not(has_up))
    def _():
        for at in (0, 128, 320):
            ext2[at : at + 64] = jnp.zeros((64, D2), BF)

    @pl.when(even | jnp.logical_not(has_down))
    def _():
        for at in (64, 192, 384):
            ext2[at : at + 64] = jnp.zeros((64, D2), BF)

    ext[2 * REACH + ROWS] = jnp.zeros((LINE, D1), BF)

    @pl.when(jnp.logical_not(has_up))
    def _():
        ext[0:REACH] = jnp.zeros((REACH, LINE, D1), BF)
        side[128:192] = jnp.zeros((64, D1), BF)

    @pl.when(jnp.logical_not(has_down))
    def _():
        ext[REACH + ROWS : 2 * REACH + ROWS] = jnp.zeros((REACH, LINE, D1), BF)
        side[192:256] = jnp.zeros((64, D1), BF)

    pl.semaphore_wait(
        barrier, 2 + jnp.where(has_up, 3, 0) + jnp.where(has_down, 3, 0)
    )

    go_right = remote(0, side_out.at[0:128], side.at[0:128], lat, right)
    go_down = remote(1, ext.at[ROWS : ROWS + REACH], ext.at[0:REACH], lat + 1, lon)
    go_up = remote(2, ext.at[REACH : 2 * REACH], ext.at[REACH + ROWS : 2 * REACH + ROWS], lat - 1, lon)
    go_down_right = remote(3, side_out.at[128:192], side.at[128:192], lat + 1, right)
    go_up_right = remote(4, side_out.at[192:256], side.at[192:256], lat - 1, right)

    def exchange(r_, d_, u_, dr_, ur_):
        @pl.when(has_up)
        def _():
            u_.start()

        @pl.when(has_down)
        def _():
            d_.start()

        r_.start()

        @pl.when(has_up)
        def _():
            ur_.start()

        @pl.when(has_down)
        def _():
            dr_.start()

    def arrived(d_, u_, dr_, ur_):
        @pl.when(has_up)
        def _():
            d_.wait_recv()
            dr_.wait_recv()

        @pl.when(has_down)
        def _():
            u_.wait_recv()
            ur_.wait_recv()

    def sent(r_, d_, u_, dr_, ur_):
        r_.wait_send()

        @pl.when(has_down)
        def _():
            d_.wait_send()
            dr_.wait_send()

        @pl.when(has_up)
        def _():
            u_.wait_send()
            ur_.wait_send()

    moves = (go_right, go_down, go_up, go_down_right, go_up_right)
    exchange(*moves)

    a = shifts[0, 0]
    b = shifts[0, 1]

    sr, sl, sc = slot_parts(col(WIN))
    for jc in range(2):
        c = sc + (WLON * jc) - b
        target = jnp.where(c >= 0, (sr + REACH - a) * LINE + sl * COLS + c, -1)
        sel_own[jc] = onehot(target, row(SPAN))
    c = sc - b
    for jr in range(3):
        r = sr + (WLAT * jr) - a
        place = jnp.where(
            r < 0, 128 + (r + REACH) * 10, jnp.where(r < ROWS, r * 10, 192 + (r - ROWS) * 10)
        )
        target = jnp.where(c < 0, place + sl * 5 + c + REACH, -1)
        sel_side[jr] = onehot(target, row(256))

    q = col(TOK)
    half = div(q, HALF)
    k = div(q - half * HALF, HALF2)
    cr, clev, cc = own_parts(q - half * HALF - k * HALF2)
    fr = cr * 2 + (k & 1)
    fc = (cc + half * (COLS2 // 2)) * 2 + (k >> 1)
    resid[...] = mm(
        onehot(fr * LINE + clev * COLS + fc, row(TOK)), inputs[...].reshape(TOK, D1)
    )
    up = fr + a
    jr = div(up, WLAT)
    over = fc + b
    jc = div(over, WLON)
    slot = ((up - jr * WLAT) * 2 + clev) * WLON + (over - jc * WLON)
    lanes = row(256)
    lanes = jnp.where(lanes < MAIN, lanes, MAIN + (lanes & 15))
    for w in range(6):
        target = jnp.where((jr == w % 3) & (jc == w // 3), slot, -1)
        sel_back[:, w * 256 : (w + 1) * 256] = onehot(target, lanes)
    target = jnp.where(
        jc == 2, jr * 64 + ((up - jr * WLAT) * 2 + clev) * REACH + over - COLS, -1
    )
    sel_back[:, 6 * 256 :] = onehot(target, row(192))

    loads[4].wait()

    def key_bias(jr, rows, a, lat_rows):
        r = sr + jr * WLAT - a + lat * rows
        return jnp.where((r >= 0) & (r < lat_rows), 0.0, NEGATIVE).astype(F32)

    def project(at, *xs):
        x = jnp.concatenate(xs, axis=0)
        qkv[at * WIN : (at + len(xs)) * WIN] = mm(x, w_qkv[...]).astype(BF)

    def gather(jr, jc):
        x = mm(sel_own[jc], ext[WLAT * jr : WLAT * jr + WLAT + REACH].reshape(SPAN, D1))
        if jc == 0:
            n = 128 if jr == 1 else 256
            x = x + mm(sel_side[jr, :, 0:n], side[0:n])
        return x.astype(BF)

    def attend(at, jr, jc):
        base = at * WIN
        lane0 = (jc * 3 + jr) * 256

        def put(r0, rn, l0, ln, value):
            mixed[r0 : r0 + rn, lane0 + l0 : lane0 + l0 + ln] = value.astype(BF)

        window_attend(
            lambda rows, part: qkv[pl.ds(base + rows.start, rows.size), part],
            lambda part: qkv[pl.ds(base, WIN), pl.ds(D1 + part.start, part.size)],
            lambda part: qkv[pl.ds(base, WIN), pl.ds(2 * D1 + part.start, part.size)],
            D1,
            key_bias(jr, ROWS, a, ROWS * lat_n),
            put,
        )

    s = col(64)
    r = div(s, 10)
    rest = s - r * 10
    lev = div(rest, 5)
    first = jnp.where(r < WLAT, (r * 2 + lev) * WLON + rest - lev * 5, -1)
    pick_first = onehot(first, lanes)
    returns = []

    def give_back(jr):
        part = pl.ds(jr * 64, 64)
        back_out[part, :] = mm_nt(pick_first, mixed[:, jr * 256 : (jr + 1) * 256]).astype(BF)
        copy = remote(11 + jr, back_out.at[part], back_in.at[part], lat, left)
        copy.start()
        returns.append(copy)

    project(0, gather(1, 1))
    attend(0, 1, 1)
    moves[0].wait_recv()
    project(1, gather(1, 0))
    attend(1, 1, 0)
    give_back(1)

    arrived(*moves[1:])
    project(2, gather(0, 0), gather(2, 0))
    for at, jr in ((2, 0), (3, 2)):
        attend(at, jr, 0)
        give_back(jr)

    project(4, gather(0, 1), gather(2, 1))
    attend(4, 0, 1)
    attend(5, 2, 1)

    for load in loads[5:12]:
        load.wait()
    a2 = shifts[1, 0]
    b2 = shifts[1, 1]

    def message(i, there, d_lat, d_lon):
        part = pl.ds(i * 64, 64)
        return remote(i + 14, send2.at[part], ext2.at[part], there + d_lat, d_lon)

    downs = [message(i, lat, 1, lon) for i in (0, 2)] + [message(5, lat, 1, right)]
    ups = [message(i, lat, -1, lon) for i in (1, 3)] + [message(6, lat, -1, right)]
    right2 = message(4, lat, 0, right)
    goes_up = even & has_up
    from_below = odd & has_down

    s = col(64)
    rl6 = div(s, 6)
    lines = rl6 * 6 + (s - rl6 * 6)
    rl5 = div(s, 5)
    columns = rl5 * 6 + (s - rl5 * 5) + 1
    top = jnp.where(s < 60, lines, -1)
    bottom = jnp.where(s < 60, lines + 12, -1)
    aside = jnp.where(s < 60, columns, -1)
    aside_bottom = jnp.where(s < 50, columns + 12, -1)
    aside_top = jnp.where(s < 50, columns, -1)

    coarse = []
    for h in range(2):
        if h == 1:
            for copy in returns:
                copy.wait_recv()
        part = slice(h * HALF, (h + 1) * HALF)
        own = mm_nt(sel_back[part, 0 : 6 * 256], mixed[...])
        if h == 1:
            own = own + mm(sel_back[part, 6 * 256 :], back_in[...])
        attended = (resid[part] + mm(own.astype(BF), w_out[...])).astype(BF)
        total = attended.astype(F32)
        x = norm(total, gain_mlp[...])
        y = jax.nn.gelu(mm(x, w_up[...])).astype(BF)
        total = (total + mm(y, w_down[...])).astype(BF).astype(F32)
        acc[part] = total
        merged = jnp.concatenate(
            [total[k * HALF2 : (k + 1) * HALF2] for k in range(4)], axis=1
        )
        merged = mm(norm(merged, gain_merge[...]), w_merge[...]).astype(BF).astype(F32)
        coarse.append(merged)
        normed = norm(merged, gain_coarse[...])
        norm2[h] = normed.astype(F32)
        if h == 0:
            pick = jnp.concatenate([bottom, top], axis=0)
            send2[0:128] = mm(onehot(pick, row(HALF2)), normed).astype(BF)
        else:
            pick = jnp.concatenate([bottom, top, aside, aside_bottom, aside_top], axis=0)
            send2[128:448] = mm(onehot(pick, row(HALF2)), normed).astype(BF)

        @pl.when(goes_up)
        def _():
            ups[h].start()

        @pl.when(has_down)
        def _():
            downs[h].start()

        if h == 1:
            right2.start()

            @pl.when(goes_up)
            def _():
                ups[2].start()

            @pl.when(has_down)
            def _():
                downs[2].start()


    c = sc - b2
    for w in range(2):
        r = sr + WLAT * w - a2
        inside = (r >= 0) & (r < ROWS2)
        right_half = jnp.where(c >= 6, 1, 0)
        place = (r * 2 + sl) * 6 + c - right_half * 6
        for h in range(2):
            target = jnp.where(inside & (c >= 0) & (right_half == h), place, -1)
            sel2_own[w, h] = onehot(target, row(HALF2))
        beyond = jnp.where(r < 0, r + REACH, r - ROWS2)
        beyond = jnp.where(beyond < REACH, beyond, -1000)
        line = jnp.where(r < 0, 0, 64) + right_half * 128 + (beyond * 2 + sl) * 6 + c - right_half * 6
        corner = jnp.where(r < 0, 320, 384) + (beyond * 2 + sl) * 5 + c + REACH
        aside = 256 + (r * 2 + sl) * 5 + c + REACH
        target = jnp.where(
            inside, jnp.where(c < 0, aside, -1), jnp.where(c < 0, corner, line)
        )
        sel2[w * WIN : (w + 1) * WIN, :] = onehot(target, row(448))

    def collect(w):
        x = mm(sel2[w * WIN : (w + 1) * WIN, :], ext2[...])
        for h in range(2):
            x = x + mm(sel2_own[w, h], norm2[h].astype(BF))
        return x.astype(BF)

    lanes = row(held)
    lanes = jnp.where(lanes < MAIN, lanes, MAIN + (lanes & 15))
    pick_here, pick_there = [], []
    for h in range(2):
        rr, ll, cc = own_parts(col(HALF2) + h * HALF2)
        up = rr + a2
        over = cc + b2
        here = (up < WLAT) & (over < COLS2)
        pick_here.append(onehot(jnp.where(here, (up * 2 + ll) * WLON + over, -1), lanes))
        below = up >= WLAT
        up = jnp.where(below, up - WLAT, up)
        target = jnp.where(
            over < COLS2,
            jnp.where(below, (up * 2 + ll) * WLON + over, -1),
            jnp.where(below, 192, 128) + (up * 2 + ll) * REACH + over - COLS2,
        )
        pick_there.append(onehot(target, row(256)))
    s = col(192)
    target = jnp.where(s < 128, s, jnp.concatenate([jnp.zeros((128, 1), I32), first], axis=0))
    pick_out = onehot(target, lanes)

    loads[12].wait()
    right2.wait_recv()

    @pl.when(has_up)
    def _():
        for copy in downs:
            copy.wait_recv()

    @pl.when(from_below)
    def _():
        for copy in ups:
            copy.wait_recv()

    x2[0:WIN] = collect(0)

    @pl.when(even)
    def _():
        for i in range(3):
            part = slice(i * D2, (i + 1) * D2)
            qkv2[0:WIN, part] = mm(x2[0:WIN], w_qkv2[:, part]).astype(BF)

    @pl.when(odd)
    def _():
        x2[WIN:] = collect(1)
        for i in range(3):
            part = slice(i * D2, (i + 1) * D2)
            qkv2[:, part] = mm(x2[...], w_qkv2[:, part]).astype(BF)

    def attend2(w, g):
        base = w * WIN

        def put(r0, rn, l0, ln, value):
            mixed2[g * D1 + r0 : g * D1 + r0 + rn, l0 : l0 + ln] = value.astype(BF)

        def at(block, part):
            return pl.ds(block * D2 + g * D1 + part.start, part.size)

        window_attend(
            lambda rows, part: qkv2[pl.ds(base + rows.start, rows.size), at(0, part)],
            lambda part: qkv2[pl.ds(base, WIN), at(1, part)],
            lambda part: qkv2[pl.ds(base, WIN), at(2, part)],
            D1,
            key_bias(w, ROWS2, a2, ROWS2 * lat_n),
            put,
        )
        return mm_nt(pick_out, mixed2[g * D1 : (g + 1) * D1, :]).astype(BF)

    left2, up2, up_left2, last_left2 = [], [], [], []
    for g in range(2):
        back2_out[g] = attend2(0, g)
        column = back2_out.at[g, 128:192]
        left2.append(remote(5 + g, column, back2_in.at[g, 128:192], lat, left))
        up2.append(remote(7 + g, back2_out.at[g, 0:128], back2_in.at[g, 0:128], lat - 1, lon))
        up_left2.append(remote(9 + g, column, back2_in.at[g, 192:256], lat - 1, left))
        last_left2.append(remote(21 + g, last_out.at[g], back2_in.at[g, 192:256], lat, left))

        @pl.when(odd)
        def _():
            up2[g].start()

        left2[g].start()

        @pl.when(odd)
        def _():
            up_left2[g].start()

    own2 = [mm_nt(pick, mixed2[...]) for pick in pick_here]

    @pl.when(odd)
    def _():
        for g in range(2):
            leaving = attend2(1, g)
            back2_in[g, 0:128] = leaving[0:128]
            last_out[g] = leaving[128:192]
            last_left2[g].start()

    t = col(TOK)
    lev = div(t, ROWS * COLS)
    rest = t - lev * (ROWS * COLS)
    r = div(rest, COLS)
    c = rest - r * COLS
    side_of = jnp.where(c >= COLS // 2, 1, 0)
    quadrant = (c & 1) * 2 + (r & 1)
    target = quadrant * HALF2 + ((r >> 1) * 2 + lev) * 6 + (c >> 1) - side_of * 6
    for h in range(2):
        sel_out[h] = onehot(jnp.where(side_of == h, target, -1), row(HALF))

    loads[13].wait()
    loads[14].wait()

    @pl.when(even)
    def _():
        for copy in up2:
            copy.wait_recv()

    def returned(h, rows):
        pick = pick_there[h][:, 0:rows]
        return jnp.concatenate([mm(pick, back2_in[g, 0:rows]) for g in range(2)], axis=1)

    final = None
    for h in range(2):
        if h == 0:
            other = returned(0, 128)
        else:
            for g in range(2):
                left2[g].wait_recv()

            @pl.when(even)
            def _():
                for copy in up_left2:
                    copy.wait_recv()

            @pl.when(odd)
            def _():
                for copy in last_left2:
                    copy.wait_recv()

            other = returned(1, 256)
        coarse_out = (coarse[h] + mm((own2[h] + other).astype(BF), w_out2[...])).astype(BF)
        spread = mm(coarse_out, w_expand[...])
        blended = jnp.concatenate(
            [
                acc[h * HALF + k * HALF2 : h * HALF + (k + 1) * HALF2]
                + spread[:, k * D1 : (k + 1) * D1]
                for k in range(4)
            ],
            axis=0,
        )
        placed = mm(sel_out[h], blended.astype(BF))
        final = placed if h == 0 else final + placed
    out[...] = final.reshape(2, ROWS, COLS, D1).astype(BF)

    sent(*moves)
    right2.wait_send()
    for copy in left2:
        copy.wait_send()

    @pl.when(has_down)
    def _():
        for copy in downs:
            copy.wait_send()

    @pl.when(goes_up)
    def _():
        for copy in ups:
            copy.wait_send()

    @pl.when(odd)
    def _():
        for copy in up2 + up_left2 + last_left2:
            copy.wait_send()

    for copy in returns:
        copy.wait_send()


def local(
    tokens, land_mask, land_embed, shifts, gain_attn, w_qkv_fine, w_out_fine, gain_mlp, w_up_fine,
    w_down_fine, gain_merge, w_merge, gain_coarse, w_qkv_coarse, w_out_coarse, w_expand,
):
    vmem = pl.BlockSpec(memory_space=pltpu.VMEM)
    hbm = pl.BlockSpec(memory_space=pl.ANY)
    smem = pl.BlockSpec(memory_space=pltpu.SMEM)
    weights = [
        w_qkv_fine, w_out_fine, w_up_fine, w_down_fine, w_merge, w_qkv_coarse, w_out_coarse, w_expand,
    ]
    V = pltpu.VMEM
    return pl.pallas_call(
        kernel,
        out_shape=pltpu.VMEM(tokens.shape, BF),
        in_specs=[hbm, hbm, hbm, smem] + [hbm] * 12,
        out_specs=vmem,
        scratch_shapes=[
            V(tokens.shape, BF), V(land_mask.shape, I32), V((1, D1), F32), V((1, D1), F32),
            V((1, D1), F32), V((1, 4 * D1), F32), V((1, D2), F32),
        ]
        + [V(w.shape, BF) for w in weights]
        + [
            V((ROWS, LINE, D1), BF),
            V((ROWS + 2 * REACH + 1, LINE, D1), BF),
            V((256, D1), BF),
            V((256, D1), BF),
            V((2, WIN, SPAN), BF),
            V((3, WIN, 256), BF),
            V((TOK, 6 * 256 + 192), BF),
            V((6 * WIN, 3 * D1), BF),
            V((D1, 6 * 256), BF),
            V((192, D1), BF),
            V((192, D1), BF),
            V((TOK, D1), F32),
            V((TOK, D1), F32),
            V((2, HALF2, D2), F32),
            V((448, D2), BF),
            V((448, D2), BF),
            V((2 * WIN, 448), BF),
            V((2, 2, WIN, HALF2), BF),
            V((2 * WIN, D2), BF),
            V((2 * WIN, 3 * D2), BF),
            V((D2, held), BF),
            V((2, 192, D1), BF),
            V((2, 64, D1), BF),
            V((2, 256, D1), BF),
            V((2, TOK, HALF), BF),
            pltpu.SemaphoreType.DMA((15,)),
            pltpu.SemaphoreType.DMA((23,)),
            pltpu.SemaphoreType.DMA((23,)),
        ],
        compiler_params=pltpu.CompilerParams(
            collective_id=0, has_side_effects=True, vmem_limit_bytes=56 * 1024 * 1024
        ),
    )(
        tokens, land_mask, land_embed.reshape(1, D1), shifts, gain_attn.reshape(1, D1),
        gain_mlp.reshape(1, D1), gain_merge.reshape(1, 4 * D1), gain_coarse.reshape(1, D2), *weights,
    )


def solution(mesh):
    spec = P(None, "lat", "lon", None)
    return jax.shard_map(
        local,
        mesh=mesh,
        in_specs=(spec, P("lat", "lon")) + (P(),) * 14,
        out_specs=spec,
        check_vma=False,
    )
```

```python
import jax
import jax.numpy as jnp
from jax import lax
from jax.experimental import pallas as pl
from jax.experimental.pallas import tpu as pltpu
from jax.sharding import PartitionSpec as P

HEAD = 64
WLAT = 6
WLON = 12
WIN = 2 * WLAT * WLON
REACH = 5
MAIN = 128
REST = WIN - MAIN

D1 = 512
D2 = 1024
FF1 = 2048
held = MAIN + REST * (D1 // HEAD)
ROWS, COLS = 12, 24
ROWS2, COLS2 = 6, 12
TOK = 2 * ROWS * COLS
TOK2 = 2 * ROWS2 * COLS2
HALF, HALF2 = TOK // 2, TOK2 // 2
LINE = 2 * COLS
SPAN = (WLAT + REACH) * LINE

EPSILON = 1e-05
NEGATIVE = -1e30
SCALE = HEAD ** (-0.5) * 1.4426950408889634
BF = jnp.bfloat16
F32 = jnp.float32
I32 = jnp.int32
MESH = pl.DeviceIdType.MESH


def div(x, d):
    return (x * ((1 << 20) // d + 1)) >> 20


def col(n):
    return lax.broadcasted_iota(I32, (n, 1), 0)


def row(n):
    return lax.broadcasted_iota(I32, (1, n), 1)


def onehot(target, lanes):
    return jnp.where(lanes == target, 1.0, 0.0).astype(BF)


def mm(a, b):
    return lax.dot_general(a, b, (((1,), (0,)), ((), ())), preferred_element_type=F32)


def mm_nt(a, b):
    return lax.dot_general(a, b, (((1,), (1,)), ((), ())), preferred_element_type=F32)


def mm_tn(a, b):
    return lax.dot_general(a, b, (((0,), (0,)), ((), ())), preferred_element_type=F32)


def norm(x, gain):
    mean = jnp.mean(x, axis=-1, keepdims=True)
    center = x - mean
    var = jnp.mean(center * center, axis=-1, keepdims=True)
    return (center * lax.rsqrt(var + EPSILON) * gain).astype(BF)


def slot_parts(s):
    r = div(s, 24)
    rest = s - r * 24
    lev = div(rest, 12)
    return r, lev, rest - lev * 12


def own_parts(t):
    half = div(t, HALF2)
    rest = t - half * HALF2
    rl = div(rest, COLS2 // 2)
    return rl >> 1, rl & 1, half * (COLS2 // 2) + rest - rl * (COLS2 // 2)


def soften(s, bias):
    s = s + bias
    top = jnp.max(s, axis=0, keepdims=True)
    p = jnp.exp2(s * SCALE - top * SCALE)
    total = jnp.sum(p, axis=0, keepdims=True)
    return p.astype(BF), 1.0 / total


def window_attend(q_of, k_of, v_of, width, bias, put):
    heads = width // HEAD
    pairs = heads // 2
    lane = row(2 * HEAD)
    every = pl.ds(0, width)
    parts = [pl.ds(i * 2 * HEAD, 2 * HEAD) for i in range(pairs)]
    spread = REST * heads
    tiled = jnp.concatenate([q_of(pl.ds(MAIN, REST), every)] * heads, axis=0)
    own = (col(spread) >> 4) == (row(width) >> 6)
    tiled = jnp.where(own, tiled, jnp.zeros_like(tiled))
    scores = [mm_nt(k_of(every), tiled)]
    for part in parts:
        q = q_of(pl.ds(0, MAIN), part)
        zero = jnp.zeros_like(q)
        both = jnp.concatenate(
            [jnp.where(lane < HEAD, q, zero), jnp.where(lane < HEAD, zero, q)], axis=0
        )
        scores.append(mm_nt(k_of(part), both))
    weights = [soften(x, bias) for x in scores]
    results = [mm_tn(v_of(part), p) for part, (p, _) in zip([every] + parts, weights)]
    o = results[0] * weights[0][1]
    o = jnp.where((col(width) >> 6) == (row(spread) >> 4), o, 0.0)
    put(0, width, MAIN, spread, o)
    for i in range(pairs):
        o = results[i + 1] * weights[i + 1][1]
        put(i * 2 * HEAD, HEAD, 0, MAIN, o[:HEAD, :MAIN])
        put(i * 2 * HEAD + HEAD, HEAD, 0, MAIN, o[HEAD:, MAIN:])


def kernel(
    tokens_h, mask_h, embed_h, shifts, gain_attn_h, gain_mlp_h, gain_merge_h, gain_coarse_h,
    w_qkv_h, w_out_h, w_up_h, w_down_h, w_merge_h, w_qkv2_h, w_out2_h, w_expand_h,
    out,
    tokens, mask, embed, gain_attn, gain_mlp, gain_merge, gain_coarse,
    w_qkv, w_out, w_up, w_down, w_merge, w_qkv2, w_out2, w_expand,
    inputs, ext, side_out, side, sel_own, sel_side, sel_back, qkv, mixed, back_out, back_in,
    resid, acc,
    norm2, send2, ext2, sel2, sel2_own, x2, qkv2, mixed2, back2_out, last_out, back2_in, sel_out,
    w_sem, send_sem, recv_sem,
):
    lat = lax.axis_index("lat")
    lon = lax.axis_index("lon")
    lat_n = lax.axis_size("lat")
    lon_n = lax.axis_size("lon")
    right = lax.rem(lon + 1, lon_n)
    left = lax.rem(lon + lon_n - 1, lon_n)
    has_up = lat > 0
    has_down = lat < lat_n - 1
    odd = lax.rem(lat, 2) == 1
    even = jnp.logical_not(odd)

    barrier = pltpu.get_barrier_semaphore()

    def greet(a, b):
        pl.semaphore_signal(barrier, inc=1, device_id=(a, b), device_id_type=MESH)

    greet(lat, left)
    greet(lat, right)

    @pl.when(has_up)
    def _():
        for b in (left, lon, right):
            greet(lat - 1, b)

    @pl.when(has_down)
    def _():
        for b in (left, lon, right):
            greet(lat + 1, b)

    loads = []
    for i, (src, dst) in enumerate(
        [
            (tokens_h, tokens), (mask_h, mask), (embed_h, embed), (gain_attn_h, gain_attn),
            (w_qkv_h, w_qkv), (gain_mlp_h, gain_mlp), (gain_merge_h, gain_merge),
            (gain_coarse_h, gain_coarse), (w_out_h, w_out), (w_up_h, w_up), (w_down_h, w_down),
            (w_merge_h, w_merge), (w_qkv2_h, w_qkv2), (w_out2_h, w_out2), (w_expand_h, w_expand),
        ]
    ):
        load = pltpu.make_async_copy(src, dst, w_sem.at[i])
        load.start()
        loads.append(load)

    def remote(i, src, dst, a, b):
        return pltpu.make_async_remote_copy(
            src_ref=src, dst_ref=dst, send_sem=send_sem.at[i], recv_sem=recv_sem.at[i],
            device_id=(a, b), device_id_type=MESH,
        )

    for load in loads[:4]:
        load.wait()
    eye = col(COLS) == row(COLS)
    add = embed[...]
    gain = gain_attn[...]
    lands = [
        jnp.sum(jnp.where(eye, mask[r : r + 1, :].astype(F32), 0.0), axis=1, keepdims=True)
        for r in range(ROWS)
    ]
    for group in range(0, ROWS, 4):
        lines = []
        for r in range(group, group + 4):
            shift = lands[r] * add
            lines += [tokens[0, r].astype(F32) + shift, tokens[1, r].astype(F32) + shift]
        x = jnp.concatenate(lines, axis=0).astype(BF)
        inputs[group : group + 4] = x.reshape(4, LINE, D1)
        x = norm(x.astype(F32), gain)
        ext[REACH + group : REACH + group + 4] = x.reshape(4, LINE, D1)

    s = col(256)
    part = jnp.where(s < 128, 0, jnp.where(s < 192, 1, 2))
    within = s - jnp.where(part == 0, 0, jnp.where(part == 1, 128, 192))
    r = div(within, 10)
    rest = within - r * 10
    lev = div(rest, 5)
    c = rest - lev * 5
    r = r + jnp.where(part == 1, ROWS - REACH, 0)
    target = jnp.where(r < ROWS, r * LINE + lev * COLS + c + (COLS - REACH), -1)
    own = ext[REACH : REACH + ROWS].reshape(TOK, D1)
    side_out[...] = mm(onehot(target, row(TOK)), own).astype(BF)

    @pl.when(jnp.logical_not(has_up))
    def _():
        for at in (0, 128, 320):
            ext2[at : at + 64] = jnp.zeros((64, D2), BF)

    @pl.when(even | jnp.logical_not(has_down))
    def _():
        for at in (64, 192, 384):
            ext2[at : at + 64] = jnp.zeros((64, D2), BF)

    ext[2 * REACH + ROWS] = jnp.zeros((LINE, D1), BF)

    @pl.when(jnp.logical_not(has_up))
    def _():
        ext[0:REACH] = jnp.zeros((REACH, LINE, D1), BF)
        side[128:192] = jnp.zeros((64, D1), BF)

    @pl.when(jnp.logical_not(has_down))
    def _():
        ext[REACH + ROWS : 2 * REACH + ROWS] = jnp.zeros((REACH, LINE, D1), BF)
        side[192:256] = jnp.zeros((64, D1), BF)

    pl.semaphore_wait(
        barrier, 2 + jnp.where(has_up, 3, 0) + jnp.where(has_down, 3, 0)
    )

    go_right = remote(0, side_out.at[0:128], side.at[0:128], lat, right)
    go_down = remote(1, ext.at[ROWS : ROWS + REACH], ext.at[0:REACH], lat + 1, lon)
    go_up = remote(2, ext.at[REACH : 2 * REACH], ext.at[REACH + ROWS : 2 * REACH + ROWS], lat - 1, lon)
    go_down_right = remote(3, side_out.at[128:192], side.at[128:192], lat + 1, right)
    go_up_right = remote(4, side_out.at[192:256], side.at[192:256], lat - 1, right)

    closing = lon == 0

    def exchange(r_, d_, u_, dr_, ur_):
        @pl.when(closing)
        def _():
            r_.start()

        @pl.when(has_up)
        def _():
            u_.start()

        @pl.when(has_down)
        def _():
            d_.start()

        @pl.when(jnp.logical_not(closing))
        def _():
            r_.start()

        @pl.when(has_up)
        def _():
            ur_.start()

        @pl.when(has_down)
        def _():
            dr_.start()

    def arrived(d_, u_, dr_, ur_):
        @pl.when(has_up)
        def _():
            d_.wait_recv()
            dr_.wait_recv()

        @pl.when(has_down)
        def _():
            u_.wait_recv()
            ur_.wait_recv()

    def sent(r_, d_, u_, dr_, ur_):
        r_.wait_send()

        @pl.when(has_down)
        def _():
            d_.wait_send()
            dr_.wait_send()

        @pl.when(has_up)
        def _():
            u_.wait_send()
            ur_.wait_send()

    moves = (go_right, go_down, go_up, go_down_right, go_up_right)
    exchange(*moves)

    a = shifts[0, 0]
    b = shifts[0, 1]

    sr, sl, sc = slot_parts(col(WIN))
    for jc in range(2):
        c = sc + (WLON * jc) - b
        target = jnp.where(c >= 0, (sr + REACH - a) * LINE + sl * COLS + c, -1)
        sel_own[jc] = onehot(target, row(SPAN))
    c = sc - b
    for jr in range(3):
        r = sr + (WLAT * jr) - a
        place = jnp.where(
            r < 0, 128 + (r + REACH) * 10, jnp.where(r < ROWS, r * 10, 192 + (r - ROWS) * 10)
        )
        target = jnp.where(c < 0, place + sl * 5 + c + REACH, -1)
        sel_side[jr] = onehot(target, row(256))

    q = col(TOK)
    half = div(q, HALF)
    k = div(q - half * HALF, HALF2)
    cr, clev, cc = own_parts(q - half * HALF - k * HALF2)
    fr = cr * 2 + (k & 1)
    fc = (cc + half * (COLS2 // 2)) * 2 + (k >> 1)
    resid[...] = mm(
        onehot(fr * LINE + clev * COLS + fc, row(TOK)), inputs[...].reshape(TOK, D1)
    )
    up = fr + a
    jr = div(up, WLAT)
    over = fc + b
    jc = div(over, WLON)
    slot = ((up - jr * WLAT) * 2 + clev) * WLON + (over - jc * WLON)
    lanes = row(256)
    lanes = jnp.where(lanes < MAIN, lanes, MAIN + (lanes & 15))
    for w in range(6):
        target = jnp.where((jr == w % 3) & (jc == w // 3), slot, -1)
        sel_back[:, w * 256 : (w + 1) * 256] = onehot(target, lanes)
    target = jnp.where(
        jc == 2, jr * 64 + ((up - jr * WLAT) * 2 + clev) * REACH + over - COLS, -1
    )
    sel_back[:, 6 * 256 :] = onehot(target, row(192))

    loads[4].wait()

    def key_bias(jr, rows, a, lat_rows):
        r = sr + jr * WLAT - a + lat * rows
        return jnp.where((r >= 0) & (r < lat_rows), 0.0, NEGATIVE).astype(F32)

    def project(at, *xs):
        x = jnp.concatenate(xs, axis=0)
        qkv[at * WIN : (at + len(xs)) * WIN] = mm(x, w_qkv[...]).astype(BF)

    def gather(jr, jc):
        x = mm(sel_own[jc], ext[WLAT * jr : WLAT * jr + WLAT + REACH].reshape(SPAN, D1))
        if jc == 0:
            n = 128 if jr == 1 else 256
            x = x + mm(sel_side[jr, :, 0:n], side[0:n])
        return x.astype(BF)

    def attend(at, jr, jc):
        base = at * WIN
        lane0 = (jc * 3 + jr) * 256

        def put(r0, rn, l0, ln, value):
            mixed[r0 : r0 + rn, lane0 + l0 : lane0 + l0 + ln] = value.astype(BF)

        window_attend(
            lambda rows, part: qkv[pl.ds(base + rows.start, rows.size), part],
            lambda part: qkv[pl.ds(base, WIN), pl.ds(D1 + part.start, part.size)],
            lambda part: qkv[pl.ds(base, WIN), pl.ds(2 * D1 + part.start, part.size)],
            D1,
            key_bias(jr, ROWS, a, ROWS * lat_n),
            put,
        )

    s = col(64)
    r = div(s, 10)
    rest = s - r * 10
    lev = div(rest, 5)
    first = jnp.where(r < WLAT, (r * 2 + lev) * WLON + rest - lev * 5, -1)
    pick_first = onehot(first, lanes)
    returns = []

    def give_back(jr):
        part = pl.ds(jr * 64, 64)
        back_out[part, :] = mm_nt(pick_first, mixed[:, jr * 256 : (jr + 1) * 256]).astype(BF)
        copy = remote(11 + jr, back_out.at[part], back_in.at[part], lat, left)
        copy.start()
        returns.append(copy)

    project(0, gather(1, 1))
    attend(0, 1, 1)
    moves[0].wait_recv()
    project(1, gather(1, 0))
    attend(1, 1, 0)
    give_back(1)

    arrived(*moves[1:])
    project(2, gather(0, 0), gather(2, 0))
    for at, jr in ((2, 0), (3, 2)):
        attend(at, jr, 0)
        give_back(jr)

    project(4, gather(0, 1), gather(2, 1))
    attend(4, 0, 1)
    attend(5, 2, 1)

    for load in loads[5:12]:
        load.wait()
    a2 = shifts[1, 0]
    b2 = shifts[1, 1]

    def message(i, there, d_lat, d_lon):
        part = pl.ds(i * 64, 64)
        return remote(i + 14, send2.at[part], ext2.at[part], there + d_lat, d_lon)

    downs = [message(i, lat, 1, lon) for i in (0, 2)] + [message(5, lat, 1, right)]
    ups = [message(i, lat, -1, lon) for i in (1, 3)] + [message(6, lat, -1, right)]
    right2 = message(4, lat, 0, right)
    goes_up = even & has_up
    from_below = odd & has_down

    s = col(64)
    rl6 = div(s, 6)
    lines = rl6 * 6 + (s - rl6 * 6)
    rl5 = div(s, 5)
    columns = rl5 * 6 + (s - rl5 * 5) + 1
    top = jnp.where(s < 60, lines, -1)
    bottom = jnp.where(s < 60, lines + 12, -1)
    aside = jnp.where(s < 60, columns, -1)
    aside_bottom = jnp.where(s < 50, columns + 12, -1)
    aside_top = jnp.where(s < 50, columns, -1)

    coarse = []
    for h in range(2):
        if h == 1:
            for copy in returns:
                copy.wait_recv()
        part = slice(h * HALF, (h + 1) * HALF)
        own = mm_nt(sel_back[part, 0 : 6 * 256], mixed[...])
        if h == 1:
            own = own + mm(sel_back[part, 6 * 256 :], back_in[...])
        attended = (resid[part] + mm(own.astype(BF), w_out[...])).astype(BF)
        total = attended.astype(F32)
        x = norm(total, gain_mlp[...])
        y = jax.nn.gelu(mm(x, w_up[...])).astype(BF)
        total = (total + mm(y, w_down[...])).astype(BF).astype(F32)
        acc[part] = total
        merged = jnp.concatenate(
            [total[k * HALF2 : (k + 1) * HALF2] for k in range(4)], axis=1
        )
        merged = mm(norm(merged, gain_merge[...]), w_merge[...]).astype(BF).astype(F32)
        coarse.append(merged)
        normed = norm(merged, gain_coarse[...])
        norm2[h] = normed.astype(F32)
        if h == 0:
            pick = jnp.concatenate([bottom, top], axis=0)
            send2[0:128] = mm(onehot(pick, row(HALF2)), normed).astype(BF)
        else:
            pick = jnp.concatenate([bottom, top, aside, aside_bottom, aside_top], axis=0)
            send2[128:448] = mm(onehot(pick, row(HALF2)), normed).astype(BF)

        if h == 1:

            @pl.when(closing)
            def _():
                right2.start()

        @pl.when(goes_up)
        def _():
            ups[h].start()

        @pl.when(has_down)
        def _():
            downs[h].start()

        if h == 1:

            @pl.when(jnp.logical_not(closing))
            def _():
                right2.start()

            @pl.when(goes_up)
            def _():
                ups[2].start()

            @pl.when(has_down)
            def _():
                downs[2].start()


    c = sc - b2
    for w in range(2):
        r = sr + WLAT * w - a2
        inside = (r >= 0) & (r < ROWS2)
        right_half = jnp.where(c >= 6, 1, 0)
        place = (r * 2 + sl) * 6 + c - right_half * 6
        for h in range(2):
            target = jnp.where(inside & (c >= 0) & (right_half == h), place, -1)
            sel2_own[w, h] = onehot(target, row(HALF2))
        beyond = jnp.where(r < 0, r + REACH, r - ROWS2)
        beyond = jnp.where(beyond < REACH, beyond, -1000)
        line = jnp.where(r < 0, 0, 64) + right_half * 128 + (beyond * 2 + sl) * 6 + c - right_half * 6
        corner = jnp.where(r < 0, 320, 384) + (beyond * 2 + sl) * 5 + c + REACH
        aside = 256 + (r * 2 + sl) * 5 + c + REACH
        target = jnp.where(
            inside, jnp.where(c < 0, aside, -1), jnp.where(c < 0, corner, line)
        )
        sel2[w * WIN : (w + 1) * WIN, :] = onehot(target, row(448))

    def collect(w):
        x = mm(sel2[w * WIN : (w + 1) * WIN, :], ext2[...])
        for h in range(2):
            x = x + mm(sel2_own[w, h], norm2[h].astype(BF))
        return x.astype(BF)

    lanes = row(held)
    lanes = jnp.where(lanes < MAIN, lanes, MAIN + (lanes & 15))
    pick_here, pick_there = [], []
    for h in range(2):
        rr, ll, cc = own_parts(col(HALF2) + h * HALF2)
        up = rr + a2
        over = cc + b2
        here = (up < WLAT) & (over < COLS2)
        pick_here.append(onehot(jnp.where(here, (up * 2 + ll) * WLON + over, -1), lanes))
        below = up >= WLAT
        up = jnp.where(below, up - WLAT, up)
        target = jnp.where(
            over < COLS2,
            jnp.where(below, (up * 2 + ll) * WLON + over, -1),
            jnp.where(below, 192, 128) + (up * 2 + ll) * REACH + over - COLS2,
        )
        pick_there.append(onehot(target, row(256)))
    s = col(192)
    target = jnp.where(s < 128, s, jnp.concatenate([jnp.zeros((128, 1), I32), first], axis=0))
    pick_out = onehot(target, lanes)

    loads[12].wait()
    right2.wait_recv()

    @pl.when(has_up)
    def _():
        for copy in downs:
            copy.wait_recv()

    @pl.when(from_below)
    def _():
        for copy in ups:
            copy.wait_recv()

    x2[0:WIN] = collect(0)

    @pl.when(even)
    def _():
        for i in range(3):
            part = slice(i * D2, (i + 1) * D2)
            qkv2[0:WIN, part] = mm(x2[0:WIN], w_qkv2[:, part]).astype(BF)

    @pl.when(odd)
    def _():
        x2[WIN:] = collect(1)
        for i in range(3):
            part = slice(i * D2, (i + 1) * D2)
            qkv2[:, part] = mm(x2[...], w_qkv2[:, part]).astype(BF)

    def attend2(w, g):
        base = w * WIN

        def put(r0, rn, l0, ln, value):
            mixed2[g * D1 + r0 : g * D1 + r0 + rn, l0 : l0 + ln] = value.astype(BF)

        def at(block, part):
            return pl.ds(block * D2 + g * D1 + part.start, part.size)

        window_attend(
            lambda rows, part: qkv2[pl.ds(base + rows.start, rows.size), at(0, part)],
            lambda part: qkv2[pl.ds(base, WIN), at(1, part)],
            lambda part: qkv2[pl.ds(base, WIN), at(2, part)],
            D1,
            key_bias(w, ROWS2, a2, ROWS2 * lat_n),
            put,
        )
        return mm_nt(pick_out, mixed2[g * D1 : (g + 1) * D1, :]).astype(BF)

    left2, up2, up_left2, last_left2 = [], [], [], []
    for g in range(2):
        back2_out[g] = attend2(0, g)
        column = back2_out.at[g, 128:192]
        left2.append(remote(5 + g, column, back2_in.at[g, 128:192], lat, left))
        up2.append(remote(7 + g, back2_out.at[g, 0:128], back2_in.at[g, 0:128], lat - 1, lon))
        up_left2.append(remote(9 + g, column, back2_in.at[g, 192:256], lat - 1, left))
        last_left2.append(remote(21 + g, last_out.at[g], back2_in.at[g, 192:256], lat, left))

        @pl.when(odd)
        def _():
            up2[g].start()

        left2[g].start()

        @pl.when(odd)
        def _():
            up_left2[g].start()

    own2 = [mm_nt(pick, mixed2[...]) for pick in pick_here]

    @pl.when(odd)
    def _():
        for g in range(2):
            leaving = attend2(1, g)
            back2_in[g, 0:128] = leaving[0:128]
            last_out[g] = leaving[128:192]
            last_left2[g].start()

    t = col(TOK)
    lev = div(t, ROWS * COLS)
    rest = t - lev * (ROWS * COLS)
    r = div(rest, COLS)
    c = rest - r * COLS
    side_of = jnp.where(c >= COLS // 2, 1, 0)
    quadrant = (c & 1) * 2 + (r & 1)
    target = quadrant * HALF2 + ((r >> 1) * 2 + lev) * 6 + (c >> 1) - side_of * 6
    for h in range(2):
        sel_out[h] = onehot(jnp.where(side_of == h, target, -1), row(HALF))

    loads[13].wait()
    loads[14].wait()

    @pl.when(even)
    def _():
        for copy in up2:
            copy.wait_recv()

    def returned(h, rows):
        pick = pick_there[h][:, 0:rows]
        return jnp.concatenate([mm(pick, back2_in[g, 0:rows]) for g in range(2)], axis=1)

    final = None
    for h in range(2):
        if h == 0:
            other = returned(0, 128)
        else:
            for g in range(2):
                left2[g].wait_recv()

            @pl.when(even)
            def _():
                for copy in up_left2:
                    copy.wait_recv()

            @pl.when(odd)
            def _():
                for copy in last_left2:
                    copy.wait_recv()

            other = returned(1, 256)
        coarse_out = (coarse[h] + mm((own2[h] + other).astype(BF), w_out2[...])).astype(BF)
        spread = mm(coarse_out, w_expand[...])
        blended = jnp.concatenate(
            [
                acc[h * HALF + k * HALF2 : h * HALF + (k + 1) * HALF2]
                + spread[:, k * D1 : (k + 1) * D1]
                for k in range(4)
            ],
            axis=0,
        )
        placed = mm(sel_out[h], blended.astype(BF))
        final = placed if h == 0 else final + placed
    out[...] = final.reshape(2, ROWS, COLS, D1).astype(BF)

    sent(*moves)
    right2.wait_send()
    for copy in left2:
        copy.wait_send()

    @pl.when(has_down)
    def _():
        for copy in downs:
            copy.wait_send()

    @pl.when(goes_up)
    def _():
        for copy in ups:
            copy.wait_send()

    @pl.when(odd)
    def _():
        for copy in up2 + up_left2 + last_left2:
            copy.wait_send()

    for copy in returns:
        copy.wait_send()


def local(
    tokens, land_mask, land_embed, shifts, gain_attn, w_qkv_fine, w_out_fine, gain_mlp, w_up_fine,
    w_down_fine, gain_merge, w_merge, gain_coarse, w_qkv_coarse, w_out_coarse, w_expand,
):
    vmem = pl.BlockSpec(memory_space=pltpu.VMEM)
    hbm = pl.BlockSpec(memory_space=pl.ANY)
    smem = pl.BlockSpec(memory_space=pltpu.SMEM)
    weights = [
        w_qkv_fine, w_out_fine, w_up_fine, w_down_fine, w_merge, w_qkv_coarse, w_out_coarse, w_expand,
    ]
    V = pltpu.VMEM
    return pl.pallas_call(
        kernel,
        out_shape=pltpu.VMEM(tokens.shape, BF),
        in_specs=[hbm, hbm, hbm, smem] + [hbm] * 12,
        out_specs=vmem,
        scratch_shapes=[
            V(tokens.shape, BF), V(land_mask.shape, I32), V((1, D1), F32), V((1, D1), F32),
            V((1, D1), F32), V((1, 4 * D1), F32), V((1, D2), F32),
        ]
        + [V(w.shape, BF) for w in weights]
        + [
            V((ROWS, LINE, D1), BF),
            V((ROWS + 2 * REACH + 1, LINE, D1), BF),
            V((256, D1), BF),
            V((256, D1), BF),
            V((2, WIN, SPAN), BF),
            V((3, WIN, 256), BF),
            V((TOK, 6 * 256 + 192), BF),
            V((6 * WIN, 3 * D1), BF),
            V((D1, 6 * 256), BF),
            V((192, D1), BF),
            V((192, D1), BF),
            V((TOK, D1), F32),
            V((TOK, D1), F32),
            V((2, HALF2, D2), F32),
            V((448, D2), BF),
            V((448, D2), BF),
            V((2 * WIN, 448), BF),
            V((2, 2, WIN, HALF2), BF),
            V((2 * WIN, D2), BF),
            V((2 * WIN, 3 * D2), BF),
            V((D2, held), BF),
            V((2, 192, D1), BF),
            V((2, 64, D1), BF),
            V((2, 256, D1), BF),
            V((2, TOK, HALF), BF),
            pltpu.SemaphoreType.DMA((15,)),
            pltpu.SemaphoreType.DMA((23,)),
            pltpu.SemaphoreType.DMA((23,)),
        ],
        compiler_params=pltpu.CompilerParams(
            collective_id=0, has_side_effects=True, vmem_limit_bytes=56 * 1024 * 1024
        ),
    )(
        tokens, land_mask, land_embed.reshape(1, D1), shifts, gain_attn.reshape(1, D1),
        gain_mlp.reshape(1, D1), gain_merge.reshape(1, 4 * D1), gain_coarse.reshape(1, D2), *weights,
    )


def solution(mesh):
    spec = P(None, "lat", "lon", None)
    return jax.shard_map(
        local,
        mesh=mesh,
        in_specs=(spec, P("lat", "lon")) + (P(),) * 14,
        out_specs=spec,
        check_vma=False,
    )
```

```python
import jax
import jax.numpy as jnp
from jax import lax
from jax.experimental import pallas as pl
from jax.experimental.pallas import tpu as pltpu
from jax.sharding import PartitionSpec as P

HEAD = 64
WLAT = 6
WLON = 12
WIN = 2 * WLAT * WLON
REACH = 5
MAIN = 128
REST = WIN - MAIN

D1 = 512
D2 = 1024
FF1 = 2048
held = MAIN + REST * (D1 // HEAD)
ROWS, COLS = 12, 24
ROWS2, COLS2 = 6, 12
TOK = 2 * ROWS * COLS
TOK2 = 2 * ROWS2 * COLS2
HALF, HALF2 = TOK // 2, TOK2 // 2
LINE = 2 * COLS
SPAN = (WLAT + REACH) * LINE

EPSILON = 1e-05
NEGATIVE = -1e30
SCALE = HEAD ** (-0.5) * 1.4426950408889634
BF = jnp.bfloat16
F32 = jnp.float32
I32 = jnp.int32
MESH = pl.DeviceIdType.MESH


def div(x, d):
    return (x * ((1 << 20) // d + 1)) >> 20


def col(n):
    return lax.broadcasted_iota(I32, (n, 1), 0)


def row(n):
    return lax.broadcasted_iota(I32, (1, n), 1)


def onehot(target, lanes):
    return jnp.where(lanes == target, 1.0, 0.0).astype(BF)


def mm(a, b):
    return lax.dot_general(a, b, (((1,), (0,)), ((), ())), preferred_element_type=F32)


def mm_nt(a, b):
    return lax.dot_general(a, b, (((1,), (1,)), ((), ())), preferred_element_type=F32)


def mm_tn(a, b):
    return lax.dot_general(a, b, (((0,), (0,)), ((), ())), preferred_element_type=F32)


def norm(x, gain):
    mean = jnp.mean(x, axis=-1, keepdims=True)
    center = x - mean
    var = jnp.mean(center * center, axis=-1, keepdims=True)
    return (center * lax.rsqrt(var + EPSILON) * gain).astype(BF)


def slot_parts(s):
    r = div(s, 24)
    rest = s - r * 24
    lev = div(rest, 12)
    return r, lev, rest - lev * 12


def own_parts(t):
    half = div(t, HALF2)
    rest = t - half * HALF2
    rl = div(rest, COLS2 // 2)
    return rl >> 1, rl & 1, half * (COLS2 // 2) + rest - rl * (COLS2 // 2)


def soften(s, bias):
    s = s + bias
    top = jnp.max(s, axis=0, keepdims=True)
    p = jnp.exp2(s * SCALE - top * SCALE)
    total = jnp.sum(p, axis=0, keepdims=True)
    return p.astype(BF), 1.0 / total


def window_attend(q_of, k_of, v_of, width, bias, put):
    heads = width // HEAD
    pairs = heads // 2
    lane = row(2 * HEAD)
    every = pl.ds(0, width)
    parts = [pl.ds(i * 2 * HEAD, 2 * HEAD) for i in range(pairs)]
    spread = REST * heads
    tiled = jnp.concatenate([q_of(pl.ds(MAIN, REST), every)] * heads, axis=0)
    own = (col(spread) >> 4) == (row(width) >> 6)
    tiled = jnp.where(own, tiled, jnp.zeros_like(tiled))
    scores = [mm_nt(k_of(every), tiled)]
    for part in parts:
        q = q_of(pl.ds(0, MAIN), part)
        zero = jnp.zeros_like(q)
        both = jnp.concatenate(
            [jnp.where(lane < HEAD, q, zero), jnp.where(lane < HEAD, zero, q)], axis=0
        )
        scores.append(mm_nt(k_of(part), both))
    weights = [soften(x, bias) for x in scores]
    results = [mm_tn(v_of(part), p) for part, (p, _) in zip([every] + parts, weights)]
    o = results[0] * weights[0][1]
    o = jnp.where((col(width) >> 6) == (row(spread) >> 4), o, 0.0)
    put(0, width, MAIN, spread, o)
    for i in range(pairs):
        o = results[i + 1] * weights[i + 1][1]
        put(i * 2 * HEAD, HEAD, 0, MAIN, o[:HEAD, :MAIN])
        put(i * 2 * HEAD + HEAD, HEAD, 0, MAIN, o[HEAD:, MAIN:])


def kernel(
    tokens_h, mask_h, embed_h, shifts, gain_attn_h, gain_mlp_h, gain_merge_h, gain_coarse_h,
    w_qkv_h, w_out_h, w_up_h, w_down_h, w_merge_h, w_qkv2_h, w_out2_h, w_expand_h,
    out,
    tokens, mask, embed, gain_attn, gain_mlp, gain_merge, gain_coarse,
    w_qkv, w_out, w_up, w_down, w_merge, w_qkv2, w_out2, w_expand,
    inputs, ext, side_out, side, sel_own, sel_side, sel_back, qkv, mixed, back_out, back_in,
    resid, acc,
    norm2, send2, ext2, sel2, sel2_own, x2, qkv2, mixed2, back2_out, last_out, back2_in, sel_out,
    w_sem, send_sem, recv_sem,
):
    lat = lax.axis_index("lat")
    lon = lax.axis_index("lon")
    lat_n = lax.axis_size("lat")
    lon_n = lax.axis_size("lon")
    right = lax.rem(lon + 1, lon_n)
    left = lax.rem(lon + lon_n - 1, lon_n)
    has_up = lat > 0
    has_down = lat < lat_n - 1
    odd = lax.rem(lat, 2) == 1
    even = jnp.logical_not(odd)

    barrier = pltpu.get_barrier_semaphore()

    def greet(a, b):
        pl.semaphore_signal(barrier, inc=1, device_id=(a, b), device_id_type=MESH)

    greet(lat, right)

    @pl.when(has_up)
    def _():
        for b in (right, lon, left):
            greet(lat - 1, b)

    @pl.when(has_down)
    def _():
        for b in (right, lon, left):
            greet(lat + 1, b)

    greet(lat, left)

    loads = []
    for i, (src, dst) in enumerate(
        [
            (tokens_h, tokens), (mask_h, mask), (embed_h, embed), (gain_attn_h, gain_attn),
            (w_qkv_h, w_qkv), (gain_mlp_h, gain_mlp), (gain_merge_h, gain_merge),
            (gain_coarse_h, gain_coarse), (w_out_h, w_out), (w_up_h, w_up), (w_down_h, w_down),
            (w_merge_h, w_merge), (w_qkv2_h, w_qkv2), (w_out2_h, w_out2), (w_expand_h, w_expand),
        ]
    ):
        load = pltpu.make_async_copy(src, dst, w_sem.at[i])
        load.start()
        loads.append(load)

    def remote(i, src, dst, a, b):
        return pltpu.make_async_remote_copy(
            src_ref=src, dst_ref=dst, send_sem=send_sem.at[i], recv_sem=recv_sem.at[i],
            device_id=(a, b), device_id_type=MESH,
        )

    for load in loads[:4]:
        load.wait()
    eye = col(COLS) == row(COLS)
    add = embed[...]
    gain = gain_attn[...]
    lands = [
        jnp.sum(jnp.where(eye, mask[r : r + 1, :].astype(F32), 0.0), axis=1, keepdims=True)
        for r in range(ROWS)
    ]
    for group in range(0, ROWS, 4):
        lines = []
        for r in range(group, group + 4):
            shift = lands[r] * add
            lines += [tokens[0, r].astype(F32) + shift, tokens[1, r].astype(F32) + shift]
        x = jnp.concatenate(lines, axis=0).astype(BF)
        inputs[group : group + 4] = x.reshape(4, LINE, D1)
        x = norm(x.astype(F32), gain)
        ext[REACH + group : REACH + group + 4] = x.reshape(4, LINE, D1)

    s = col(256)
    part = jnp.where(s < 128, 0, jnp.where(s < 192, 1, 2))
    within = s - jnp.where(part == 0, 0, jnp.where(part == 1, 128, 192))
    r = div(within, 10)
    rest = within - r * 10
    lev = div(rest, 5)
    c = rest - lev * 5
    r = r + jnp.where(part == 1, ROWS - REACH, 0)
    target = jnp.where(r < ROWS, r * LINE + lev * COLS + c + (COLS - REACH), -1)
    own = ext[REACH : REACH + ROWS].reshape(TOK, D1)
    side_out[...] = mm(onehot(target, row(TOK)), own).astype(BF)

    @pl.when(jnp.logical_not(has_up))
    def _():
        for at in (0, 128, 320):
            ext2[at : at + 64] = jnp.zeros((64, D2), BF)

    @pl.when(even | jnp.logical_not(has_down))
    def _():
        for at in (64, 192, 384):
            ext2[at : at + 64] = jnp.zeros((64, D2), BF)

    ext[2 * REACH + ROWS] = jnp.zeros((LINE, D1), BF)

    @pl.when(jnp.logical_not(has_up))
    def _():
        ext[0:REACH] = jnp.zeros((REACH, LINE, D1), BF)
        side[128:192] = jnp.zeros((64, D1), BF)

    @pl.when(jnp.logical_not(has_down))
    def _():
        ext[REACH + ROWS : 2 * REACH + ROWS] = jnp.zeros((REACH, LINE, D1), BF)
        side[192:256] = jnp.zeros((64, D1), BF)

    pl.semaphore_wait(
        barrier, 2 + jnp.where(has_up, 3, 0) + jnp.where(has_down, 3, 0)
    )

    go_right = remote(0, side_out.at[0:128], side.at[0:128], lat, right)
    go_down = remote(1, ext.at[ROWS : ROWS + REACH], ext.at[0:REACH], lat + 1, lon)
    go_up = remote(2, ext.at[REACH : 2 * REACH], ext.at[REACH + ROWS : 2 * REACH + ROWS], lat - 1, lon)
    go_down_right = remote(3, side_out.at[128:192], side.at[128:192], lat + 1, right)
    go_up_right = remote(4, side_out.at[192:256], side.at[192:256], lat - 1, right)

    closing = (lax.rem(lon, 8) == 0) | (lax.rem(lon, 8) == 7)

    def exchange(r_, d_, u_, dr_, ur_):
        @pl.when(closing)
        def _():
            r_.start()

        @pl.when(has_up)
        def _():
            u_.start()

        @pl.when(has_down)
        def _():
            d_.start()

        @pl.when(jnp.logical_not(closing))
        def _():
            r_.start()

        @pl.when(has_up)
        def _():
            ur_.start()

        @pl.when(has_down)
        def _():
            dr_.start()

    def arrived(d_, u_, dr_, ur_):
        @pl.when(has_up)
        def _():
            d_.wait_recv()
            dr_.wait_recv()

        @pl.when(has_down)
        def _():
            u_.wait_recv()
            ur_.wait_recv()

    def sent(r_, d_, u_, dr_, ur_):
        r_.wait_send()

        @pl.when(has_down)
        def _():
            d_.wait_send()
            dr_.wait_send()

        @pl.when(has_up)
        def _():
            u_.wait_send()
            ur_.wait_send()

    moves = (go_right, go_down, go_up, go_down_right, go_up_right)
    exchange(*moves)

    a = shifts[0, 0]
    b = shifts[0, 1]

    sr, sl, sc = slot_parts(col(WIN))
    for jc in range(2):
        c = sc + (WLON * jc) - b
        target = jnp.where(c >= 0, (sr + REACH - a) * LINE + sl * COLS + c, -1)
        sel_own[jc] = onehot(target, row(SPAN))
    c = sc - b
    for jr in range(3):
        r = sr + (WLAT * jr) - a
        place = jnp.where(
            r < 0, 128 + (r + REACH) * 10, jnp.where(r < ROWS, r * 10, 192 + (r - ROWS) * 10)
        )
        target = jnp.where(c < 0, place + sl * 5 + c + REACH, -1)
        sel_side[jr] = onehot(target, row(256))

    q = col(TOK)
    half = div(q, HALF)
    k = div(q - half * HALF, HALF2)
    cr, clev, cc = own_parts(q - half * HALF - k * HALF2)
    fr = cr * 2 + (k & 1)
    fc = (cc + half * (COLS2 // 2)) * 2 + (k >> 1)
    resid[...] = mm(
        onehot(fr * LINE + clev * COLS + fc, row(TOK)), inputs[...].reshape(TOK, D1)
    )
    up = fr + a
    jr = div(up, WLAT)
    over = fc + b
    jc = div(over, WLON)
    slot = ((up - jr * WLAT) * 2 + clev) * WLON + (over - jc * WLON)
    lanes = row(256)
    lanes = jnp.where(lanes < MAIN, lanes, MAIN + (lanes & 15))
    for w in range(6):
        target = jnp.where((jr == w % 3) & (jc == w // 3), slot, -1)
        sel_back[:, w * 256 : (w + 1) * 256] = onehot(target, lanes)
    target = jnp.where(
        jc == 2, jr * 64 + ((up - jr * WLAT) * 2 + clev) * REACH + over - COLS, -1
    )
    sel_back[:, 6 * 256 :] = onehot(target, row(192))

    loads[4].wait()

    def key_bias(jr, rows, a, lat_rows):
        r = sr + jr * WLAT - a + lat * rows
        return jnp.where((r >= 0) & (r < lat_rows), 0.0, NEGATIVE).astype(F32)

    def project(at, *xs):
        x = jnp.concatenate(xs, axis=0)
        qkv[at * WIN : (at + len(xs)) * WIN] = mm(x, w_qkv[...]).astype(BF)

    def gather(jr, jc):
        x = mm(sel_own[jc], ext[WLAT * jr : WLAT * jr + WLAT + REACH].reshape(SPAN, D1))
        if jc == 0:
            n = 128 if jr == 1 else 256
            x = x + mm(sel_side[jr, :, 0:n], side[0:n])
        return x.astype(BF)

    def attend(at, jr, jc):
        base = at * WIN
        lane0 = (jc * 3 + jr) * 256

        def put(r0, rn, l0, ln, value):
            mixed[r0 : r0 + rn, lane0 + l0 : lane0 + l0 + ln] = value.astype(BF)

        window_attend(
            lambda rows, part: qkv[pl.ds(base + rows.start, rows.size), part],
            lambda part: qkv[pl.ds(base, WIN), pl.ds(D1 + part.start, part.size)],
            lambda part: qkv[pl.ds(base, WIN), pl.ds(2 * D1 + part.start, part.size)],
            D1,
            key_bias(jr, ROWS, a, ROWS * lat_n),
            put,
        )

    s = col(64)
    r = div(s, 10)
    rest = s - r * 10
    lev = div(rest, 5)
    first = jnp.where(r < WLAT, (r * 2 + lev) * WLON + rest - lev * 5, -1)
    pick_first = onehot(first, lanes)
    returns = []

    def give_back(jr):
        part = pl.ds(jr * 64, 64)
        back_out[part, :] = mm_nt(pick_first, mixed[:, jr * 256 : (jr + 1) * 256]).astype(BF)
        copy = remote(11 + jr, back_out.at[part], back_in.at[part], lat, left)
        copy.start()
        returns.append(copy)

    project(0, gather(1, 1))
    attend(0, 1, 1)
    moves[0].wait_recv()
    project(1, gather(1, 0))
    attend(1, 1, 0)
    give_back(1)

    arrived(*moves[1:])
    project(2, gather(0, 0), gather(2, 0))
    for at, jr in ((2, 0), (3, 2)):
        attend(at, jr, 0)
        give_back(jr)

    project(4, gather(0, 1), gather(2, 1))
    attend(4, 0, 1)
    attend(5, 2, 1)

    for load in loads[5:12]:
        load.wait()
    a2 = shifts[1, 0]
    b2 = shifts[1, 1]

    def message(i, there, d_lat, d_lon):
        part = pl.ds(i * 64, 64)
        return remote(i + 14, send2.at[part], ext2.at[part], there + d_lat, d_lon)

    downs = [message(i, lat, 1, lon) for i in (0, 2)] + [message(5, lat, 1, right)]
    ups = [message(i, lat, -1, lon) for i in (1, 3)] + [message(6, lat, -1, right)]
    right2 = message(4, lat, 0, right)
    goes_up = even & has_up
    from_below = odd & has_down

    s = col(64)
    rl6 = div(s, 6)
    lines = rl6 * 6 + (s - rl6 * 6)
    rl5 = div(s, 5)
    columns = rl5 * 6 + (s - rl5 * 5) + 1
    top = jnp.where(s < 60, lines, -1)
    bottom = jnp.where(s < 60, lines + 12, -1)
    aside = jnp.where(s < 60, columns, -1)
    aside_bottom = jnp.where(s < 50, columns + 12, -1)
    aside_top = jnp.where(s < 50, columns, -1)

    coarse = []
    for h in range(2):
        if h == 1:
            for copy in returns:
                copy.wait_recv()
        part = slice(h * HALF, (h + 1) * HALF)
        own = mm_nt(sel_back[part, 0 : 6 * 256], mixed[...])
        if h == 1:
            own = own + mm(sel_back[part, 6 * 256 :], back_in[...])
        attended = (resid[part] + mm(own.astype(BF), w_out[...])).astype(BF)
        total = attended.astype(F32)
        x = norm(total, gain_mlp[...])
        y = jax.nn.gelu(mm(x, w_up[...])).astype(BF)
        total = (total + mm(y, w_down[...])).astype(BF).astype(F32)
        acc[part] = total
        merged = jnp.concatenate(
            [total[k * HALF2 : (k + 1) * HALF2] for k in range(4)], axis=1
        )
        merged = mm(norm(merged, gain_merge[...]), w_merge[...]).astype(BF).astype(F32)
        coarse.append(merged)
        normed = norm(merged, gain_coarse[...])
        norm2[h] = normed.astype(F32)
        if h == 0:
            pick = jnp.concatenate([bottom, top], axis=0)
            send2[0:128] = mm(onehot(pick, row(HALF2)), normed).astype(BF)
        else:
            pick = jnp.concatenate([bottom, top, aside, aside_bottom, aside_top], axis=0)
            send2[128:448] = mm(onehot(pick, row(HALF2)), normed).astype(BF)

        if h == 1:

            @pl.when(closing)
            def _():
                right2.start()

        @pl.when(goes_up)
        def _():
            ups[h].start()

        @pl.when(has_down)
        def _():
            downs[h].start()

        if h == 1:

            @pl.when(jnp.logical_not(closing))
            def _():
                right2.start()

            @pl.when(goes_up)
            def _():
                ups[2].start()

            @pl.when(has_down)
            def _():
                downs[2].start()


    c = sc - b2
    for w in range(2):
        r = sr + WLAT * w - a2
        inside = (r >= 0) & (r < ROWS2)
        right_half = jnp.where(c >= 6, 1, 0)
        place = (r * 2 + sl) * 6 + c - right_half * 6
        for h in range(2):
            target = jnp.where(inside & (c >= 0) & (right_half == h), place, -1)
            sel2_own[w, h] = onehot(target, row(HALF2))
        beyond = jnp.where(r < 0, r + REACH, r - ROWS2)
        beyond = jnp.where(beyond < REACH, beyond, -1000)
        line = jnp.where(r < 0, 0, 64) + right_half * 128 + (beyond * 2 + sl) * 6 + c - right_half * 6
        corner = jnp.where(r < 0, 320, 384) + (beyond * 2 + sl) * 5 + c + REACH
        aside = 256 + (r * 2 + sl) * 5 + c + REACH
        target = jnp.where(
            inside, jnp.where(c < 0, aside, -1), jnp.where(c < 0, corner, line)
        )
        sel2[w * WIN : (w + 1) * WIN, :] = onehot(target, row(448))

    def collect(w):
        x = mm(sel2[w * WIN : (w + 1) * WIN, :], ext2[...])
        for h in range(2):
            x = x + mm(sel2_own[w, h], norm2[h].astype(BF))
        return x.astype(BF)

    lanes = row(held)
    lanes = jnp.where(lanes < MAIN, lanes, MAIN + (lanes & 15))
    pick_here, pick_there = [], []
    for h in range(2):
        rr, ll, cc = own_parts(col(HALF2) + h * HALF2)
        up = rr + a2
        over = cc + b2
        here = (up < WLAT) & (over < COLS2)
        pick_here.append(onehot(jnp.where(here, (up * 2 + ll) * WLON + over, -1), lanes))
        below = up >= WLAT
        up = jnp.where(below, up - WLAT, up)
        target = jnp.where(
            over < COLS2,
            jnp.where(below, (up * 2 + ll) * WLON + over, -1),
            jnp.where(below, 192, 128) + (up * 2 + ll) * REACH + over - COLS2,
        )
        pick_there.append(onehot(target, row(256)))
    s = col(192)
    target = jnp.where(s < 128, s, jnp.concatenate([jnp.zeros((128, 1), I32), first], axis=0))
    pick_out = onehot(target, lanes)

    loads[12].wait()
    right2.wait_recv()

    @pl.when(has_up)
    def _():
        for copy in downs:
            copy.wait_recv()

    @pl.when(from_below)
    def _():
        for copy in ups:
            copy.wait_recv()

    x2[0:WIN] = collect(0)

    @pl.when(even)
    def _():
        for i in range(3):
            part = slice(i * D2, (i + 1) * D2)
            qkv2[0:WIN, part] = mm(x2[0:WIN], w_qkv2[:, part]).astype(BF)

    @pl.when(odd)
    def _():
        x2[WIN:] = collect(1)
        for i in range(3):
            part = slice(i * D2, (i + 1) * D2)
            qkv2[:, part] = mm(x2[...], w_qkv2[:, part]).astype(BF)

    def attend2(w, g):
        base = w * WIN

        def put(r0, rn, l0, ln, value):
            mixed2[g * D1 + r0 : g * D1 + r0 + rn, l0 : l0 + ln] = value.astype(BF)

        def at(block, part):
            return pl.ds(block * D2 + g * D1 + part.start, part.size)

        window_attend(
            lambda rows, part: qkv2[pl.ds(base + rows.start, rows.size), at(0, part)],
            lambda part: qkv2[pl.ds(base, WIN), at(1, part)],
            lambda part: qkv2[pl.ds(base, WIN), at(2, part)],
            D1,
            key_bias(w, ROWS2, a2, ROWS2 * lat_n),
            put,
        )
        return mm_nt(pick_out, mixed2[g * D1 : (g + 1) * D1, :]).astype(BF)

    left2, up2, up_left2, last_left2 = [], [], [], []
    for g in range(2):
        back2_out[g] = attend2(0, g)
        column = back2_out.at[g, 128:192]
        left2.append(remote(5 + g, column, back2_in.at[g, 128:192], lat, left))
        up2.append(remote(7 + g, back2_out.at[g, 0:128], back2_in.at[g, 0:128], lat - 1, lon))
        up_left2.append(remote(9 + g, column, back2_in.at[g, 192:256], lat - 1, left))
        last_left2.append(remote(21 + g, last_out.at[g], back2_in.at[g, 192:256], lat, left))

        @pl.when(odd)
        def _():
            up2[g].start()

        left2[g].start()

        @pl.when(odd)
        def _():
            up_left2[g].start()

    own2 = [mm_nt(pick, mixed2[...]) for pick in pick_here]

    @pl.when(odd)
    def _():
        for g in range(2):
            leaving = attend2(1, g)
            back2_in[g, 0:128] = leaving[0:128]
            last_out[g] = leaving[128:192]
            last_left2[g].start()

    t = col(TOK)
    lev = div(t, ROWS * COLS)
    rest = t - lev * (ROWS * COLS)
    r = div(rest, COLS)
    c = rest - r * COLS
    side_of = jnp.where(c >= COLS // 2, 1, 0)
    quadrant = (c & 1) * 2 + (r & 1)
    target = quadrant * HALF2 + ((r >> 1) * 2 + lev) * 6 + (c >> 1) - side_of * 6
    for h in range(2):
        sel_out[h] = onehot(jnp.where(side_of == h, target, -1), row(HALF))

    loads[13].wait()
    loads[14].wait()

    @pl.when(even)
    def _():
        for copy in up2:
            copy.wait_recv()

    def returned(h, rows):
        pick = pick_there[h][:, 0:rows]
        return jnp.concatenate([mm(pick, back2_in[g, 0:rows]) for g in range(2)], axis=1)

    final = None
    for h in range(2):
        if h == 0:
            other = returned(0, 128)
        else:
            for g in range(2):
                left2[g].wait_recv()

            @pl.when(even)
            def _():
                for copy in up_left2:
                    copy.wait_recv()

            @pl.when(odd)
            def _():
                for copy in last_left2:
                    copy.wait_recv()

            other = returned(1, 256)
        coarse_out = (coarse[h] + mm((own2[h] + other).astype(BF), w_out2[...])).astype(BF)
        spread = mm(coarse_out, w_expand[...])
        blended = jnp.concatenate(
            [
                acc[h * HALF + k * HALF2 : h * HALF + (k + 1) * HALF2]
                + spread[:, k * D1 : (k + 1) * D1]
                for k in range(4)
            ],
            axis=0,
        )
        placed = mm(sel_out[h], blended.astype(BF))
        final = placed if h == 0 else final + placed
    out[...] = final.reshape(2, ROWS, COLS, D1).astype(BF)

    sent(*moves)
    right2.wait_send()
    for copy in left2:
        copy.wait_send()

    @pl.when(has_down)
    def _():
        for copy in downs:
            copy.wait_send()

    @pl.when(goes_up)
    def _():
        for copy in ups:
            copy.wait_send()

    @pl.when(odd)
    def _():
        for copy in up2 + up_left2 + last_left2:
            copy.wait_send()

    for copy in returns:
        copy.wait_send()


def local(
    tokens, land_mask, land_embed, shifts, gain_attn, w_qkv_fine, w_out_fine, gain_mlp, w_up_fine,
    w_down_fine, gain_merge, w_merge, gain_coarse, w_qkv_coarse, w_out_coarse, w_expand,
):
    vmem = pl.BlockSpec(memory_space=pltpu.VMEM)
    hbm = pl.BlockSpec(memory_space=pl.ANY)
    smem = pl.BlockSpec(memory_space=pltpu.SMEM)
    weights = [
        w_qkv_fine, w_out_fine, w_up_fine, w_down_fine, w_merge, w_qkv_coarse, w_out_coarse, w_expand,
    ]
    V = pltpu.VMEM
    return pl.pallas_call(
        kernel,
        out_shape=pltpu.VMEM(tokens.shape, BF),
        in_specs=[hbm, hbm, hbm, smem] + [hbm] * 12,
        out_specs=vmem,
        scratch_shapes=[
            V(tokens.shape, BF), V(land_mask.shape, I32), V((1, D1), F32), V((1, D1), F32),
            V((1, D1), F32), V((1, 4 * D1), F32), V((1, D2), F32),
        ]
        + [V(w.shape, BF) for w in weights]
        + [
            V((ROWS, LINE, D1), BF),
            V((ROWS + 2 * REACH + 1, LINE, D1), BF),
            V((256, D1), BF),
            V((256, D1), BF),
            V((2, WIN, SPAN), BF),
            V((3, WIN, 256), BF),
            V((TOK, 6 * 256 + 192), BF),
            V((6 * WIN, 3 * D1), BF),
            V((D1, 6 * 256), BF),
            V((192, D1), BF),
            V((192, D1), BF),
            V((TOK, D1), F32),
            V((TOK, D1), F32),
            V((2, HALF2, D2), F32),
            V((448, D2), BF),
            V((448, D2), BF),
            V((2 * WIN, 448), BF),
            V((2, 2, WIN, HALF2), BF),
            V((2 * WIN, D2), BF),
            V((2 * WIN, 3 * D2), BF),
            V((D2, held), BF),
            V((2, 192, D1), BF),
            V((2, 64, D1), BF),
            V((2, 256, D1), BF),
            V((2, TOK, HALF), BF),
            pltpu.SemaphoreType.DMA((15,)),
            pltpu.SemaphoreType.DMA((23,)),
            pltpu.SemaphoreType.DMA((23,)),
        ],
        compiler_params=pltpu.CompilerParams(
            collective_id=0, has_side_effects=True, vmem_limit_bytes=56 * 1024 * 1024
        ),
    )(
        tokens, land_mask, land_embed.reshape(1, D1), shifts, gain_attn.reshape(1, D1),
        gain_mlp.reshape(1, D1), gain_merge.reshape(1, 4 * D1), gain_coarse.reshape(1, D2), *weights,
    )


def solution(mesh):
    spec = P(None, "lat", "lon", None)
    return jax.shard_map(
        local,
        mesh=mesh,
        in_specs=(spec, P("lat", "lon")) + (P(),) * 14,
        out_specs=spec,
        check_vma=False,
    )
```

```python
import jax
import jax.numpy as jnp
from jax import lax
from jax.experimental import pallas as pl
from jax.experimental.pallas import tpu as pltpu
from jax.sharding import PartitionSpec as P

HEAD = 64
WLAT = 6
WLON = 12
WIN = 2 * WLAT * WLON
REACH = 5
MAIN = 128
REST = WIN - MAIN

D1 = 512
D2 = 1024
FF1 = 2048
held = MAIN + REST * (D1 // HEAD)
ROWS, COLS = 12, 24
ROWS2, COLS2 = 6, 12
TOK = 2 * ROWS * COLS
TOK2 = 2 * ROWS2 * COLS2
HALF, HALF2 = TOK // 2, TOK2 // 2
LINE = 2 * COLS
SPAN = (WLAT + REACH) * LINE

EPSILON = 1e-05
NEGATIVE = -1e30
SCALE = HEAD ** (-0.5) * 1.4426950408889634
BF = jnp.bfloat16
F32 = jnp.float32
I32 = jnp.int32
MESH = pl.DeviceIdType.MESH


def div(x, d):
    return (x * ((1 << 20) // d + 1)) >> 20


def col(n):
    return lax.broadcasted_iota(I32, (n, 1), 0)


def row(n):
    return lax.broadcasted_iota(I32, (1, n), 1)


def onehot(target, lanes):
    return jnp.where(lanes == target, 1.0, 0.0).astype(BF)


def mm(a, b):
    return lax.dot_general(a, b, (((1,), (0,)), ((), ())), preferred_element_type=F32)


def mm_nt(a, b):
    return lax.dot_general(a, b, (((1,), (1,)), ((), ())), preferred_element_type=F32)


def mm_tn(a, b):
    return lax.dot_general(a, b, (((0,), (0,)), ((), ())), preferred_element_type=F32)


def norm(x, gain):
    mean = jnp.mean(x, axis=-1, keepdims=True)
    center = x - mean
    var = jnp.mean(center * center, axis=-1, keepdims=True)
    return (center * lax.rsqrt(var + EPSILON) * gain).astype(BF)


def slot_parts(s):
    r = div(s, 24)
    rest = s - r * 24
    lev = div(rest, 12)
    return r, lev, rest - lev * 12


def own_parts(t):
    half = div(t, HALF2)
    rest = t - half * HALF2
    rl = div(rest, COLS2 // 2)
    return rl >> 1, rl & 1, half * (COLS2 // 2) + rest - rl * (COLS2 // 2)


def soften(s, bias):
    s = s + bias
    top = jnp.max(s, axis=0, keepdims=True)
    p = jnp.exp2(s * SCALE - top * SCALE)
    total = jnp.sum(p, axis=0, keepdims=True)
    return p.astype(BF), 1.0 / total


def window_attend(q_of, k_of, v_of, width, bias, put):
    heads = width // HEAD
    pairs = heads // 2
    lane = row(2 * HEAD)
    every = pl.ds(0, width)
    parts = [pl.ds(i * 2 * HEAD, 2 * HEAD) for i in range(pairs)]
    spread = REST * heads
    tiled = jnp.concatenate([q_of(pl.ds(MAIN, REST), every)] * heads, axis=0)
    own = (col(spread) >> 4) == (row(width) >> 6)
    tiled = jnp.where(own, tiled, jnp.zeros_like(tiled))
    scores = [mm_nt(k_of(every), tiled)]
    for part in parts:
        q = q_of(pl.ds(0, MAIN), part)
        zero = jnp.zeros_like(q)
        both = jnp.concatenate(
            [jnp.where(lane < HEAD, q, zero), jnp.where(lane < HEAD, zero, q)], axis=0
        )
        scores.append(mm_nt(k_of(part), both))
    weights = [soften(x, bias) for x in scores]
    results = [mm_tn(v_of(part), p) for part, (p, _) in zip([every] + parts, weights)]
    o = results[0] * weights[0][1]
    o = jnp.where((col(width) >> 6) == (row(spread) >> 4), o, 0.0)
    put(0, width, MAIN, spread, o)
    for i in range(pairs):
        o = results[i + 1] * weights[i + 1][1]
        put(i * 2 * HEAD, HEAD, 0, MAIN, o[:HEAD, :MAIN])
        put(i * 2 * HEAD + HEAD, HEAD, 0, MAIN, o[HEAD:, MAIN:])


def kernel(
    tokens_h, mask_h, embed_h, shifts, gain_attn_h, gain_mlp_h, gain_merge_h, gain_coarse_h,
    w_qkv_h, w_out_h, w_up_h, w_down_h, w_merge_h, w_qkv2_h, w_out2_h, w_expand_h,
    out,
    tokens, mask, embed, gain_attn, gain_mlp, gain_merge, gain_coarse,
    w_qkv, w_out, w_up, w_down, w_merge, w_qkv2, w_out2, w_expand,
    inputs, ext, side_out, side, sel_own, sel_side, sel_back, qkv, mixed, back_out, back_in,
    resid, acc,
    norm2, send2, ext2, sel2, sel2_own, x2, qkv2, mixed2, back2_out, last_out, back2_in, sel_out,
    w_sem, send_sem, recv_sem,
):
    lat = lax.axis_index("lat")
    lon = lax.axis_index("lon")
    lat_n = lax.axis_size("lat")
    lon_n = lax.axis_size("lon")
    right = lax.rem(lon + 1, lon_n)
    left = lax.rem(lon + lon_n - 1, lon_n)
    has_up = lat > 0
    has_down = lat < lat_n - 1
    odd = lax.rem(lat, 2) == 1
    even = jnp.logical_not(odd)

    barrier = pltpu.get_barrier_semaphore()

    def greet(a, b):
        pl.semaphore_signal(barrier, inc=1, device_id=(a, b), device_id_type=MESH)

    greet(lat, right)

    @pl.when(has_up)
    def _():
        for b in (right, lon, left):
            greet(lat - 1, b)

    @pl.when(has_down)
    def _():
        for b in (right, lon, left):
            greet(lat + 1, b)

    greet(lat, left)

    loads = []
    for i, (src, dst) in enumerate(
        [
            (tokens_h, tokens), (mask_h, mask), (embed_h, embed), (gain_attn_h, gain_attn),
            (w_qkv_h, w_qkv), (gain_mlp_h, gain_mlp), (gain_merge_h, gain_merge),
            (gain_coarse_h, gain_coarse), (w_out_h, w_out), (w_up_h, w_up), (w_down_h, w_down),
            (w_merge_h, w_merge), (w_qkv2_h, w_qkv2), (w_out2_h, w_out2), (w_expand_h, w_expand),
        ]
    ):
        load = pltpu.make_async_copy(src, dst, w_sem.at[i])
        load.start()
        loads.append(load)

    def remote(i, src, dst, a, b):
        return pltpu.make_async_remote_copy(
            src_ref=src, dst_ref=dst, send_sem=send_sem.at[i], recv_sem=recv_sem.at[i],
            device_id=(a, b), device_id_type=MESH,
        )

    for load in loads[:4]:
        load.wait()
    eye = col(COLS) == row(COLS)
    add = embed[...]
    gain = gain_attn[...]
    lands = [
        jnp.sum(jnp.where(eye, mask[r : r + 1, :].astype(F32), 0.0), axis=1, keepdims=True)
        for r in range(ROWS)
    ]
    for group in range(0, ROWS, 4):
        lines = []
        for r in range(group, group + 4):
            shift = lands[r] * add
            lines += [tokens[0, r].astype(F32) + shift, tokens[1, r].astype(F32) + shift]
        x = jnp.concatenate(lines, axis=0).astype(BF)
        inputs[group : group + 4] = x.reshape(4, LINE, D1)
        x = norm(x.astype(F32), gain)
        ext[REACH + group : REACH + group + 4] = x.reshape(4, LINE, D1)

    s = col(256)
    part = jnp.where(s < 128, 0, jnp.where(s < 192, 1, 2))
    within = s - jnp.where(part == 0, 0, jnp.where(part == 1, 128, 192))
    r = div(within, 10)
    rest = within - r * 10
    lev = div(rest, 5)
    c = rest - lev * 5
    r = r + jnp.where(part == 1, ROWS - REACH, 0)
    target = jnp.where(r < ROWS, r * LINE + lev * COLS + c + (COLS - REACH), -1)
    own = ext[REACH : REACH + ROWS].reshape(TOK, D1)
    side_out[...] = mm(onehot(target, row(TOK)), own).astype(BF)

    @pl.when(jnp.logical_not(has_up))
    def _():
        for at in (0, 128, 320):
            ext2[at : at + 64] = jnp.zeros((64, D2), BF)

    @pl.when(even | jnp.logical_not(has_down))
    def _():
        for at in (64, 192, 384):
            ext2[at : at + 64] = jnp.zeros((64, D2), BF)

    ext[2 * REACH + ROWS] = jnp.zeros((LINE, D1), BF)

    @pl.when(jnp.logical_not(has_up))
    def _():
        ext[0:REACH] = jnp.zeros((REACH, LINE, D1), BF)
        side[128:192] = jnp.zeros((64, D1), BF)

    @pl.when(jnp.logical_not(has_down))
    def _():
        ext[REACH + ROWS : 2 * REACH + ROWS] = jnp.zeros((REACH, LINE, D1), BF)
        side[192:256] = jnp.zeros((64, D1), BF)

    pl.semaphore_wait(
        barrier, 2 + jnp.where(has_up, 3, 0) + jnp.where(has_down, 3, 0)
    )

    go_right = remote(0, side_out.at[0:128], side.at[0:128], lat, right)
    go_down = remote(1, ext.at[ROWS : ROWS + REACH], ext.at[0:REACH], lat + 1, lon)
    go_up = remote(2, ext.at[REACH : 2 * REACH], ext.at[REACH + ROWS : 2 * REACH + ROWS], lat - 1, lon)
    go_down_right = remote(3, side_out.at[128:192], side.at[128:192], lat + 1, right)
    go_up_right = remote(4, side_out.at[192:256], side.at[192:256], lat - 1, right)

    closing = (lax.rem(lon, 8) == 0) | (lax.rem(lon, 8) == 7)
    far = lax.rem(lon, 8) == 7

    def exchange(r_, d_, u_, dr_, ur_):
        @pl.when(closing)
        def _():
            r_.start()

        @pl.when(far & has_up)
        def _():
            ur_.start()

        @pl.when(far & has_down)
        def _():
            dr_.start()

        @pl.when(has_up)
        def _():
            u_.start()

        @pl.when(has_down)
        def _():
            d_.start()

        @pl.when(jnp.logical_not(closing))
        def _():
            r_.start()

        @pl.when(jnp.logical_not(far) & has_up)
        def _():
            ur_.start()

        @pl.when(jnp.logical_not(far) & has_down)
        def _():
            dr_.start()

    def arrived(d_, u_, dr_, ur_):
        @pl.when(has_up)
        def _():
            d_.wait_recv()
            dr_.wait_recv()

        @pl.when(has_down)
        def _():
            u_.wait_recv()
            ur_.wait_recv()

    def sent(r_, d_, u_, dr_, ur_):
        r_.wait_send()

        @pl.when(has_down)
        def _():
            d_.wait_send()
            dr_.wait_send()

        @pl.when(has_up)
        def _():
            u_.wait_send()
            ur_.wait_send()

    moves = (go_right, go_down, go_up, go_down_right, go_up_right)
    exchange(*moves)

    a = shifts[0, 0]
    b = shifts[0, 1]

    sr, sl, sc = slot_parts(col(WIN))
    for jc in range(2):
        c = sc + (WLON * jc) - b
        target = jnp.where(c >= 0, (sr + REACH - a) * LINE + sl * COLS + c, -1)
        sel_own[jc] = onehot(target, row(SPAN))
    c = sc - b
    for jr in range(3):
        r = sr + (WLAT * jr) - a
        place = jnp.where(
            r < 0, 128 + (r + REACH) * 10, jnp.where(r < ROWS, r * 10, 192 + (r - ROWS) * 10)
        )
        target = jnp.where(c < 0, place + sl * 5 + c + REACH, -1)
        sel_side[jr] = onehot(target, row(256))

    q = col(TOK)
    half = div(q, HALF)
    k = div(q - half * HALF, HALF2)
    cr, clev, cc = own_parts(q - half * HALF - k * HALF2)
    fr = cr * 2 + (k & 1)
    fc = (cc + half * (COLS2 // 2)) * 2 + (k >> 1)
    resid[...] = mm(
        onehot(fr * LINE + clev * COLS + fc, row(TOK)), inputs[...].reshape(TOK, D1)
    )
    up = fr + a
    jr = div(up, WLAT)
    over = fc + b
    jc = div(over, WLON)
    slot = ((up - jr * WLAT) * 2 + clev) * WLON + (over - jc * WLON)
    lanes = row(256)
    lanes = jnp.where(lanes < MAIN, lanes, MAIN + (lanes & 15))
    for w in range(6):
        target = jnp.where((jr == w % 3) & (jc == w // 3), slot, -1)
        sel_back[:, w * 256 : (w + 1) * 256] = onehot(target, lanes)
    target = jnp.where(
        jc == 2, jr * 64 + ((up - jr * WLAT) * 2 + clev) * REACH + over - COLS, -1
    )
    sel_back[:, 6 * 256 :] = onehot(target, row(192))

    loads[4].wait()

    def key_bias(jr, rows, a, lat_rows):
        r = sr + jr * WLAT - a + lat * rows
        return jnp.where((r >= 0) & (r < lat_rows), 0.0, NEGATIVE).astype(F32)

    def project(at, *xs):
        x = jnp.concatenate(xs, axis=0)
        qkv[at * WIN : (at + len(xs)) * WIN] = mm(x, w_qkv[...]).astype(BF)

    def gather(jr, jc):
        x = mm(sel_own[jc], ext[WLAT * jr : WLAT * jr + WLAT + REACH].reshape(SPAN, D1))
        if jc == 0:
            n = 128 if jr == 1 else 256
            x = x + mm(sel_side[jr, :, 0:n], side[0:n])
        return x.astype(BF)

    def attend(at, jr, jc):
        base = at * WIN
        lane0 = (jc * 3 + jr) * 256

        def put(r0, rn, l0, ln, value):
            mixed[r0 : r0 + rn, lane0 + l0 : lane0 + l0 + ln] = value.astype(BF)

        window_attend(
            lambda rows, part: qkv[pl.ds(base + rows.start, rows.size), part],
            lambda part: qkv[pl.ds(base, WIN), pl.ds(D1 + part.start, part.size)],
            lambda part: qkv[pl.ds(base, WIN), pl.ds(2 * D1 + part.start, part.size)],
            D1,
            key_bias(jr, ROWS, a, ROWS * lat_n),
            put,
        )

    s = col(64)
    r = div(s, 10)
    rest = s - r * 10
    lev = div(rest, 5)
    first = jnp.where(r < WLAT, (r * 2 + lev) * WLON + rest - lev * 5, -1)
    pick_first = onehot(first, lanes)
    returns = []

    def give_back(jr):
        part = pl.ds(jr * 64, 64)
        back_out[part, :] = mm_nt(pick_first, mixed[:, jr * 256 : (jr + 1) * 256]).astype(BF)
        copy = remote(11 + jr, back_out.at[part], back_in.at[part], lat, left)
        copy.start()
        returns.append(copy)

    project(0, gather(1, 1))
    attend(0, 1, 1)
    moves[0].wait_recv()
    project(1, gather(1, 0))
    attend(1, 1, 0)
    give_back(1)

    arrived(*moves[1:])
    project(2, gather(0, 0), gather(2, 0))
    for at, jr in ((2, 0), (3, 2)):
        attend(at, jr, 0)
        give_back(jr)

    project(4, gather(0, 1), gather(2, 1))
    attend(4, 0, 1)
    attend(5, 2, 1)

    for load in loads[5:12]:
        load.wait()
    a2 = shifts[1, 0]
    b2 = shifts[1, 1]

    def message(i, there, d_lat, d_lon):
        part = pl.ds(i * 64, 64)
        return remote(i + 14, send2.at[part], ext2.at[part], there + d_lat, d_lon)

    downs = [message(i, lat, 1, lon) for i in (0, 2)] + [message(5, lat, 1, right)]
    ups = [message(i, lat, -1, lon) for i in (1, 3)] + [message(6, lat, -1, right)]
    right2 = message(4, lat, 0, right)
    goes_up = even & has_up
    from_below = odd & has_down

    s = col(64)
    rl6 = div(s, 6)
    lines = rl6 * 6 + (s - rl6 * 6)
    rl5 = div(s, 5)
    columns = rl5 * 6 + (s - rl5 * 5) + 1
    top = jnp.where(s < 60, lines, -1)
    bottom = jnp.where(s < 60, lines + 12, -1)
    aside = jnp.where(s < 60, columns, -1)
    aside_bottom = jnp.where(s < 50, columns + 12, -1)
    aside_top = jnp.where(s < 50, columns, -1)

    coarse = []
    for h in range(2):
        if h == 1:
            for copy in returns:
                copy.wait_recv()
        part = slice(h * HALF, (h + 1) * HALF)
        own = mm_nt(sel_back[part, 0 : 6 * 256], mixed[...])
        if h == 1:
            own = own + mm(sel_back[part, 6 * 256 :], back_in[...])
        attended = (resid[part] + mm(own.astype(BF), w_out[...])).astype(BF)
        total = attended.astype(F32)
        x = norm(total, gain_mlp[...])
        y = jax.nn.gelu(mm(x, w_up[...])).astype(BF)
        total = (total + mm(y, w_down[...])).astype(BF).astype(F32)
        acc[part] = total
        merged = jnp.concatenate(
            [total[k * HALF2 : (k + 1) * HALF2] for k in range(4)], axis=1
        )
        merged = mm(norm(merged, gain_merge[...]), w_merge[...]).astype(BF).astype(F32)
        coarse.append(merged)
        normed = norm(merged, gain_coarse[...])
        norm2[h] = normed.astype(F32)
        if h == 0:
            pick = jnp.concatenate([bottom, top], axis=0)
            send2[0:128] = mm(onehot(pick, row(HALF2)), normed).astype(BF)
        else:
            pick = jnp.concatenate([bottom, top, aside, aside_bottom, aside_top], axis=0)
            send2[128:448] = mm(onehot(pick, row(HALF2)), normed).astype(BF)

        if h == 1:

            @pl.when(closing)
            def _():
                right2.start()

        @pl.when(goes_up)
        def _():
            ups[h].start()

        @pl.when(has_down)
        def _():
            downs[h].start()

        if h == 1:

            @pl.when(jnp.logical_not(closing))
            def _():
                right2.start()

            @pl.when(goes_up)
            def _():
                ups[2].start()

            @pl.when(has_down)
            def _():
                downs[2].start()


    c = sc - b2
    for w in range(2):
        r = sr + WLAT * w - a2
        inside = (r >= 0) & (r < ROWS2)
        right_half = jnp.where(c >= 6, 1, 0)
        place = (r * 2 + sl) * 6 + c - right_half * 6
        for h in range(2):
            target = jnp.where(inside & (c >= 0) & (right_half == h), place, -1)
            sel2_own[w, h] = onehot(target, row(HALF2))
        beyond = jnp.where(r < 0, r + REACH, r - ROWS2)
        beyond = jnp.where(beyond < REACH, beyond, -1000)
        line = jnp.where(r < 0, 0, 64) + right_half * 128 + (beyond * 2 + sl) * 6 + c - right_half * 6
        corner = jnp.where(r < 0, 320, 384) + (beyond * 2 + sl) * 5 + c + REACH
        aside = 256 + (r * 2 + sl) * 5 + c + REACH
        target = jnp.where(
            inside, jnp.where(c < 0, aside, -1), jnp.where(c < 0, corner, line)
        )
        sel2[w * WIN : (w + 1) * WIN, :] = onehot(target, row(448))

    def collect(w):
        x = mm(sel2[w * WIN : (w + 1) * WIN, :], ext2[...])
        for h in range(2):
            x = x + mm(sel2_own[w, h], norm2[h].astype(BF))
        return x.astype(BF)

    lanes = row(held)
    lanes = jnp.where(lanes < MAIN, lanes, MAIN + (lanes & 15))
    pick_here, pick_there = [], []
    for h in range(2):
        rr, ll, cc = own_parts(col(HALF2) + h * HALF2)
        up = rr + a2
        over = cc + b2
        here = (up < WLAT) & (over < COLS2)
        pick_here.append(onehot(jnp.where(here, (up * 2 + ll) * WLON + over, -1), lanes))
        below = up >= WLAT
        up = jnp.where(below, up - WLAT, up)
        target = jnp.where(
            over < COLS2,
            jnp.where(below, (up * 2 + ll) * WLON + over, -1),
            jnp.where(below, 192, 128) + (up * 2 + ll) * REACH + over - COLS2,
        )
        pick_there.append(onehot(target, row(256)))
    s = col(192)
    target = jnp.where(s < 128, s, jnp.concatenate([jnp.zeros((128, 1), I32), first], axis=0))
    pick_out = onehot(target, lanes)

    loads[12].wait()
    right2.wait_recv()

    @pl.when(has_up)
    def _():
        for copy in downs:
            copy.wait_recv()

    @pl.when(from_below)
    def _():
        for copy in ups:
            copy.wait_recv()

    x2[0:WIN] = collect(0)

    @pl.when(even)
    def _():
        for i in range(3):
            part = slice(i * D2, (i + 1) * D2)
            qkv2[0:WIN, part] = mm(x2[0:WIN], w_qkv2[:, part]).astype(BF)

    @pl.when(odd)
    def _():
        x2[WIN:] = collect(1)
        for i in range(3):
            part = slice(i * D2, (i + 1) * D2)
            qkv2[:, part] = mm(x2[...], w_qkv2[:, part]).astype(BF)

    def attend2(w, g):
        base = w * WIN

        def put(r0, rn, l0, ln, value):
            mixed2[g * D1 + r0 : g * D1 + r0 + rn, l0 : l0 + ln] = value.astype(BF)

        def at(block, part):
            return pl.ds(block * D2 + g * D1 + part.start, part.size)

        window_attend(
            lambda rows, part: qkv2[pl.ds(base + rows.start, rows.size), at(0, part)],
            lambda part: qkv2[pl.ds(base, WIN), at(1, part)],
            lambda part: qkv2[pl.ds(base, WIN), at(2, part)],
            D1,
            key_bias(w, ROWS2, a2, ROWS2 * lat_n),
            put,
        )
        return mm_nt(pick_out, mixed2[g * D1 : (g + 1) * D1, :]).astype(BF)

    left2, up2, up_left2, last_left2 = [], [], [], []
    for g in range(2):
        back2_out[g] = attend2(0, g)
        column = back2_out.at[g, 128:192]
        left2.append(remote(5 + g, column, back2_in.at[g, 128:192], lat, left))
        up2.append(remote(7 + g, back2_out.at[g, 0:128], back2_in.at[g, 0:128], lat - 1, lon))
        up_left2.append(remote(9 + g, column, back2_in.at[g, 192:256], lat - 1, left))
        last_left2.append(remote(21 + g, last_out.at[g], back2_in.at[g, 192:256], lat, left))

        @pl.when(odd)
        def _():
            up2[g].start()

        left2[g].start()

        @pl.when(odd)
        def _():
            up_left2[g].start()

    own2 = [mm_nt(pick, mixed2[...]) for pick in pick_here]

    @pl.when(odd)
    def _():
        for g in range(2):
            leaving = attend2(1, g)
            back2_in[g, 0:128] = leaving[0:128]
            last_out[g] = leaving[128:192]
            last_left2[g].start()

    t = col(TOK)
    lev = div(t, ROWS * COLS)
    rest = t - lev * (ROWS * COLS)
    r = div(rest, COLS)
    c = rest - r * COLS
    side_of = jnp.where(c >= COLS // 2, 1, 0)
    quadrant = (c & 1) * 2 + (r & 1)
    target = quadrant * HALF2 + ((r >> 1) * 2 + lev) * 6 + (c >> 1) - side_of * 6
    for h in range(2):
        sel_out[h] = onehot(jnp.where(side_of == h, target, -1), row(HALF))

    loads[13].wait()
    loads[14].wait()

    @pl.when(even)
    def _():
        for copy in up2:
            copy.wait_recv()

    def returned(h, rows):
        pick = pick_there[h][:, 0:rows]
        return jnp.concatenate([mm(pick, back2_in[g, 0:rows]) for g in range(2)], axis=1)

    final = None
    for h in range(2):
        if h == 0:
            other = returned(0, 128)
        else:
            for g in range(2):
                left2[g].wait_recv()

            @pl.when(even)
            def _():
                for copy in up_left2:
                    copy.wait_recv()

            @pl.when(odd)
            def _():
                for copy in last_left2:
                    copy.wait_recv()

            other = returned(1, 256)
        coarse_out = (coarse[h] + mm((own2[h] + other).astype(BF), w_out2[...])).astype(BF)
        spread = mm(coarse_out, w_expand[...])
        blended = jnp.concatenate(
            [
                acc[h * HALF + k * HALF2 : h * HALF + (k + 1) * HALF2]
                + spread[:, k * D1 : (k + 1) * D1]
                for k in range(4)
            ],
            axis=0,
        )
        placed = mm(sel_out[h], blended.astype(BF))
        final = placed if h == 0 else final + placed
    out[...] = final.reshape(2, ROWS, COLS, D1).astype(BF)

    sent(*moves)
    right2.wait_send()
    for copy in left2:
        copy.wait_send()

    @pl.when(has_down)
    def _():
        for copy in downs:
            copy.wait_send()

    @pl.when(goes_up)
    def _():
        for copy in ups:
            copy.wait_send()

    @pl.when(odd)
    def _():
        for copy in up2 + up_left2 + last_left2:
            copy.wait_send()

    for copy in returns:
        copy.wait_send()


def local(
    tokens, land_mask, land_embed, shifts, gain_attn, w_qkv_fine, w_out_fine, gain_mlp, w_up_fine,
    w_down_fine, gain_merge, w_merge, gain_coarse, w_qkv_coarse, w_out_coarse, w_expand,
):
    vmem = pl.BlockSpec(memory_space=pltpu.VMEM)
    hbm = pl.BlockSpec(memory_space=pl.ANY)
    smem = pl.BlockSpec(memory_space=pltpu.SMEM)
    weights = [
        w_qkv_fine, w_out_fine, w_up_fine, w_down_fine, w_merge, w_qkv_coarse, w_out_coarse, w_expand,
    ]
    V = pltpu.VMEM
    return pl.pallas_call(
        kernel,
        out_shape=pltpu.VMEM(tokens.shape, BF),
        in_specs=[hbm, hbm, hbm, smem] + [hbm] * 12,
        out_specs=vmem,
        scratch_shapes=[
            V(tokens.shape, BF), V(land_mask.shape, I32), V((1, D1), F32), V((1, D1), F32),
            V((1, D1), F32), V((1, 4 * D1), F32), V((1, D2), F32),
        ]
        + [V(w.shape, BF) for w in weights]
        + [
            V((ROWS, LINE, D1), BF),
            V((ROWS + 2 * REACH + 1, LINE, D1), BF),
            V((256, D1), BF),
            V((256, D1), BF),
            V((2, WIN, SPAN), BF),
            V((3, WIN, 256), BF),
            V((TOK, 6 * 256 + 192), BF),
            V((6 * WIN, 3 * D1), BF),
            V((D1, 6 * 256), BF),
            V((192, D1), BF),
            V((192, D1), BF),
            V((TOK, D1), F32),
            V((TOK, D1), F32),
            V((2, HALF2, D2), F32),
            V((448, D2), BF),
            V((448, D2), BF),
            V((2 * WIN, 448), BF),
            V((2, 2, WIN, HALF2), BF),
            V((2 * WIN, D2), BF),
            V((2 * WIN, 3 * D2), BF),
            V((D2, held), BF),
            V((2, 192, D1), BF),
            V((2, 64, D1), BF),
            V((2, 256, D1), BF),
            V((2, TOK, HALF), BF),
            pltpu.SemaphoreType.DMA((15,)),
            pltpu.SemaphoreType.DMA((23,)),
            pltpu.SemaphoreType.DMA((23,)),
        ],
        compiler_params=pltpu.CompilerParams(
            collective_id=0, has_side_effects=True, vmem_limit_bytes=56 * 1024 * 1024
        ),
    )(
        tokens, land_mask, land_embed.reshape(1, D1), shifts, gain_attn.reshape(1, D1),
        gain_mlp.reshape(1, D1), gain_merge.reshape(1, 4 * D1), gain_coarse.reshape(1, D2), *weights,
    )


def solution(mesh):
    spec = P(None, "lat", "lon", None)
    return jax.shard_map(
        local,
        mesh=mesh,
        in_specs=(spec, P("lat", "lon")) + (P(),) * 14,
        out_specs=spec,
        check_vma=False,
    )
```
